32 devices in a mesh: segment: 4 (over x, core), tx: 2 (over y), ty: 4 (over z).
Axes of the slice: x: 2, y: 2, z: 4, core: 2. Of those that a mesh axis runs over, the one named last changes fastest.
Arguments:
- act_in: bfloat16 [4, 32, 256, 128], P('segment', 'tx', 'ty'), may hold values from -6 to 6
- partner_in: bfloat16 [4, 32, 256, 128], P('segment', 'tx', 'ty'), may hold values from -6 to 6
- stashed: bfloat16 [4, 32, 256, 128], P('segment', 'tx', 'ty'), may hold values from -6 to 6
- grad_in: bfloat16 [4, 32, 256, 128], P('segment', 'tx', 'ty'), may hold values from -6 to 6
- down_weights: bfloat16 [4, 3, 3, 128, 192], P('segment'), may hold values from -0.1875 to 0.1875
- up_weights: bfloat16 [4, 3, 3, 192, 128], P('segment'), may hold values from -0.15625 to 0.15625
- coarse: bfloat16 [512, 128], P(('tx', 'ty')), may hold values from -6 to 6
- nest_owner: int32 [512, 1], P(('tx', 'ty')), may hold values from 0 to 3; in each aligned block of 64 rows (0 to 63, 64 to 127, ...) at most 32 rows name the same one
- nest_cell: int32 [512], P(('tx', 'ty')), may hold values from 0 to 63
- land_weight: int32 [8, 64], P('tx', 'ty'), may hold values from 1 to 4
Outputs:
- act_out: bfloat16 [4, 32, 256, 128], P('segment', 'tx', 'ty')
- grad_out: bfloat16 [4, 32, 256, 128], P('segment', 'tx', 'ty')
- partner_out: bfloat16 [4, 32, 256, 128], P('segment', 'tx', 'ty')
- down_grads: float32 [4, 221184], P('segment', ('tx', 'ty'))
- up_grads: float32 [4, 221184], P('segment', ('tx', 'ty'))
The draws below stay inside these ranges and needn't reach their ends.
Inputs may be any that keep to these rules, and one draw needn't show every extreme that they name: `nest_owner`: within the rows of one device (aligned blocks of 64 rows) no owner is named more than 32 times, a bound that some block reaches; every owner is named by some row.
All inputs are finite; a program needn't handle non-finite values.
Results may differ from the reference program's by a relative error of at most 0.0085.
Values may be sent and summed in bfloat16 or wider, within the bound.
No kernel may reach another device: no remote copies, remote signals or barrier semaphores. Data moves between devices by JAX's collectives and lax.ppermute only.
A program may use at most 64 MiB of HBM per device.

```python
import math
import jax
import jax.numpy as jnp
import numpy as np
from jax import lax

C = 128
C2 = 192
HT = 16
WT = 64
CELLS_C = 64
CAP = 32
NH = 32
NW = 256
N_SEGMENT = 4
N_TX = 2
N_TY = 4


def plant(entries, stream_key, low, high):
    spot = [jax.random.randint(jax.random.fold_in(stream_key, axis), (), 0, length) for axis, length in enumerate(entries.shape)]
    longest = entries.shape.index(max(entries.shape))
    neighbour = spot[:longest] + [(spot[longest] + 1) % entries.shape[longest]] + spot[longest + 1:]
    return entries.at[tuple(spot)].set(low).at[tuple(neighbour)].set(high)


def levels(key, dims, cuts, low, high):
    def one(position, shards_of):
        heights = jax.random.uniform(jax.random.fold_in(jax.random.fold_in(key, 6), position), (shards_of,), jnp.float32, low / len(cuts), high / len(cuts))
        return jnp.repeat(jnp.exp(heights), dims[position] // shards_of).reshape((-1,) + (1,) * (len(dims) - position - 1))

    factor_of = one(*cuts[0])
    for cut in cuts[1:]:
        factor_of = factor_of * one(*cut)
    return factor_of


def assign_block(rng, own, number, rows, amount, top, bound, skew):
    ranking = jax.random.permutation(rng, amount)
    crowded, usual = load_shares(amount, rows * top, bound, skew, True), load_shares(amount, rows * top, bound, skew, False)
    places = jnp.arange(amount)

    def named(sizes, offset_by):
        used = int((sizes > 0).sum())
        fixed = max(1, used // 4)
        shifted = fixed + (places - fixed + offset_by * (used - fixed)) % max(1, amount - fixed)
        return jnp.zeros((amount,), jnp.int32).at[ranking[jnp.where(places < fixed, places, shifted)]].set(jnp.asarray(sizes, jnp.int32))

    sizes = jnp.where(number % 4 == 0, named(crowded, number // 4), named(usual, number - number // 4 - 1))
    mixed = jax.random.permutation(jax.random.fold_in(own, 3), amount)
    source_of, sink = mixed[0:amount // 2 * 2:2], mixed[1:amount // 2 * 2:2]
    room = jnp.minimum(sizes[source_of] - 1, bound - sizes[sink]) // 2
    room = jnp.where((source_of == ranking[0]) | (sink == ranking[0]) | (sizes[sink] == 0), 0, jnp.maximum(room, 0))
    shifted = jax.random.randint(jax.random.fold_in(own, 4), (amount // 2,), 0, 1 << 20) % (room + 1)
    sizes = sizes.at[source_of].add(-shifted).at[sink].add(shifted)
    members = jnp.searchsorted(jnp.cumsum(sizes), jnp.arange(rows * top), side="right").astype(jnp.int32)
    grid = members.reshape(top, rows).T
    grid = grid[jax.random.permutation(jax.random.fold_in(own, 1), rows)]
    offset_by = jax.random.randint(jax.random.fold_in(own, 2), (rows, 1), 0, top)
    return jnp.take_along_axis(grid, (jnp.arange(top)[None, :] + offset_by) % top, axis=1)


def load_shares(number_of, total, bound, slope, full):
    weights = [(1 << 20) // math.isqrt(rank ** slope) + 1 for rank in range(1, number_of + 1)]
    largest = bound if full else min(bound, max(-(-total // number_of), total * weights[0] // sum(weights)))
    least = 1 if total - largest >= number_of - 1 else 0
    holding, spare = [largest] + [least] * (number_of - 1), total - largest - least * (number_of - 1)
    while spare > 0:
        movable = [i for i in range(1, number_of) if holding[i] < largest] or [i for i in range(1, number_of) if holding[i] < bound]
        pool, left = sum([weights[i] for i in movable]), spare
        for i in movable:
            addition = min(bound - holding[i], max(1, left * weights[i] // pool), spare)
            holding[i] = holding[i] + addition
            spare = spare - addition
    return np.array(holding)


def gaussian(own_key, shape, width, most, cuts=(), kind=jnp.bfloat16):
    values = jax.random.normal(own_key, shape, jnp.float32) * width
    if len(cuts) > 0:
        values = levels(own_key, shape, cuts, -0.22, 0.18) * values
    return jnp.clip(values, min=-most, max=most).astype(kind)


def setup_inputs(seed: int = 0) -> dict:
    key_list = jax.random.split(jax.random.key(seed), 11)
    act_in = gaussian(key_list[0], (N_SEGMENT, NH, NW, C), 1.0, 6.0, ((0, 4), (1, 2), (2, 4)))
    partner_in = gaussian(key_list[1], (N_SEGMENT, NH, NW, C), 1.0, 6.0, ((0, 4), (1, 2), (2, 4)))
    stashed = gaussian(key_list[2], (N_SEGMENT, NH, NW, C), 1.0, 6.0, ((0, 4), (1, 2), (2, 4)))
    grad_in = gaussian(key_list[3], (N_SEGMENT, NH, NW, C), 1.0, 6.0, ((0, 4), (1, 2), (2, 4)))
    down_weights = gaussian(key_list[4], (N_SEGMENT, 3, 3, C, C2), (9 * C) ** -0.5, 0.1875, ((0, 4),))
    up_weights = gaussian(key_list[5], (N_SEGMENT, 3, 3, C2, C), (9 * C2) ** -0.5, 0.15625, ((0, 4),))
    coarse = gaussian(key_list[6], (N_TX * N_TY * CELLS_C, C), 1.0, 6.0, ((0, 8),))
    nest_owner_keys = jax.random.split(jax.random.fold_in(key_list[7], 1), (N_TX * N_TY * CELLS_C) // CELLS_C)
    nest_owner_turns = jax.random.permutation(jax.random.fold_in(key_list[7], 3), (N_TX * N_TY * CELLS_C) // CELLS_C)
    nest_owner = jax.vmap(lambda own, number: assign_block(jax.random.fold_in(key_list[7], 2), own, number, CELLS_C, N_TY, 1, CAP, 2))(nest_owner_keys, nest_owner_turns).reshape((N_TX * N_TY * CELLS_C, 1))
    nest_cell = plant(jax.random.randint(key_list[8], (N_TX * N_TY * CELLS_C,), 0, CELLS_C), jax.random.fold_in(key_list[8], 1), 0, CELLS_C - 1).astype(jnp.int32)
    land_weight = plant(jax.random.randint(key_list[9], (NH // 4, NW // 4), 1, 5), jax.random.fold_in(key_list[9], 1), 1, 4).astype(jnp.int32)
    return dict(act_in=act_in, partner_in=partner_in, stashed=stashed, grad_in=grad_in, down_weights=down_weights, up_weights=up_weights, coarse=coarse, nest_owner=nest_owner, nest_cell=nest_cell, land_weight=land_weight)


def convolve(inputs, kernel, stride, padding, dilation):
    result = lax.conv_general_dilated(inputs[None], kernel, (stride, stride), padding, lhs_dilation=(dilation, dilation), dimension_numbers=('NHWC', 'HWIO', 'NHWC'), preferred_element_type=jnp.float32)
    return result[0]

def flipped(kernel):
    return jnp.transpose(kernel[::-1, ::-1], (0, 1, 3, 2))

def enlarge(values, factor):
    return jnp.repeat(jnp.repeat(values, factor, axis=0), factor, axis=1)

def pooled(values):
    height, breadth, channels = values.shape
    return values.reshape(height // 2, 2, breadth // 2, 2, channels).sum(axis=(1, 3))

def silu_slope(preact):
    logistic = jax.nn.sigmoid(preact)
    return logistic * (1.0 + preact * (1.0 - logistic))

def kernel_grad(padded, cotangent, stride):
    height, breadth, channels = cotangent.shape
    flat_grad = cotangent.reshape(height * breadth, channels)
    pieces = []
    for row_tap in range(3):
        for col_tap in range(3):
            window = padded[row_tap:row_tap + stride * (height - 1) + 1:stride, col_tap:col_tap + stride * (breadth - 1) + 1:stride]
            window = window.reshape(height * breadth, window.shape[-1])
            pieces.append(lax.dot_general(window, flat_grad, (((0,), (0,)), ((), ())), preferred_element_type=jnp.float32))
    return jnp.stack(pieces).reshape(-1)

def lower_parts(block_cells, down_kernel):
    pre_down = convolve(block_cells, down_kernel, 2, ((1, 1), (1, 1)), 1)
    reduced = jax.nn.silu(pre_down).astype(jnp.bfloat16)
    return (pre_down, enlarge(reduced, 2))

def reference(act_in, partner_in, stashed, grad_in, down_weights, up_weights, coarse, nest_owner, nest_cell, land_weight):
    row_ids = jnp.arange(N_TX * N_TY * CELLS_C, dtype=jnp.int32)
    tile_row = row_ids // (N_TY * CELLS_C)
    coarse_rows = (tile_row * N_TY + nest_owner[:, 0]) * CELLS_C + nest_cell
    fetched = coarse[coarse_rows].reshape(N_TX, N_TY, HT // 4, WT // 4, C)
    fetched = jnp.transpose(fetched, (0, 2, 1, 3, 4)).reshape(N_TX * (HT // 4), N_TY * (WT // 4), C)
    condition = enlarge(fetched, 4).astype(jnp.float32)
    land_up = enlarge(land_weight.astype(jnp.float32), 4)[:, :, None]
    scaling = 1.0 / float(NH * NW) ** 0.5
    pad_one = ((1, 1), (1, 1), (0, 0))
    outputs, in_grads, down_list, up_list = ([], [], [], [])
    for segment_id in range(N_SEGMENT):
        decoder = 1.0 if segment_id >= N_SEGMENT // 2 else 0.0
        encoder = 1.0 - decoder
        down_kernel = down_weights[segment_id]
        up_kernel = up_weights[segment_id]
        block_in = (act_in[segment_id].astype(jnp.float32) + decoder * partner_in[segment_id].astype(jnp.float32) + condition).astype(jnp.bfloat16)
        pre_down, raised = lower_parts(block_in, down_kernel)
        output = (block_in.astype(jnp.float32) + convolve(raised, up_kernel, 1, ((1, 1), (1, 1)), 1)).astype(jnp.bfloat16)
        weighting = land_up if segment_id == N_SEGMENT - 1 else 1.0
        out_grad = ((grad_in[segment_id].astype(jnp.float32) + encoder * partner_in[segment_id].astype(jnp.float32)) * weighting).astype(jnp.bfloat16)
        pre_back, raised_back = lower_parts(stashed[segment_id], down_kernel)
        raised_grad = convolve(out_grad, flipped(up_kernel), 1, ((1, 1), (1, 1)), 1)
        pre_grad = (pooled(raised_grad) * silu_slope(pre_back)).astype(jnp.bfloat16)
        in_grad = (out_grad.astype(jnp.float32) + convolve(pre_grad, flipped(down_kernel), 1, ((1, 2), (1, 2)), 2)).astype(jnp.bfloat16)
        up_list.append(kernel_grad(jnp.pad(raised_back, pad_one), out_grad, 1) * scaling)
        down_list.append(kernel_grad(jnp.pad(stashed[segment_id], pad_one), pre_grad, 2) * scaling)
        outputs.append(output)
        in_grads.append(in_grad)
    blank = jnp.zeros_like(outputs[0])
    act_out = jnp.stack([blank] + outputs[:N_SEGMENT - 1])
    grad_out = jnp.stack(in_grads[1:] + [blank])
    partner_list = []
    for segment_id in range(N_SEGMENT):
        mirror = N_SEGMENT - 1 - segment_id
        partner_list.append(outputs[mirror] if segment_id >= N_SEGMENT // 2 else in_grads[mirror])
    partner_out = jnp.stack(partner_list)
    return (act_out, grad_out, partner_out, jnp.stack(down_list), jnp.stack(up_list))
```

```python
import functools
import math

import jax
import jax.numpy as jnp
from jax import lax
from jax.experimental import pallas as pl
from jax.experimental.pallas import tpu as pltpu
from jax.sharding import PartitionSpec as P

F32 = jnp.float32
BF16 = jnp.bfloat16
VMEM = pl.BlockSpec(memory_space=pltpu.VMEM)
SMEM = pl.BlockSpec(memory_space=pltpu.SMEM)
LEFT = 8
PAD = 48
STRIP_ROWS = 7


def whole_block(leaf):
    return pl.BlockSpec(leaf.shape, lambda i: (0,) * len(leaf.shape))


def call(body, out_shape, in_specs, scratch=(), flops=0, moved=0, limit=48, grid=()):
    out_specs = jax.tree.map(whole_block if grid else lambda _: VMEM, out_shape)
    return pl.pallas_call(
        body,
        out_shape=out_shape,
        grid=grid,
        in_specs=in_specs,
        out_specs=out_specs,
        scratch_shapes=list(scratch),
        compiler_params=pltpu.CompilerParams(vmem_limit_bytes=limit * 1024 * 1024),
        cost_estimate=pl.CostEstimate(flops=flops, bytes_accessed=moved, transcendentals=0),
    )


def sublane(shape):
    return lax.broadcasted_iota(jnp.int32, shape, len(shape) - 2)


def flag(condition):
    return jnp.where(condition, 1.0, 0.0).astype(F32)


def traits():
    segments = lax.axis_size("segment")
    position = lax.axis_index("segment")
    decoder = flag(position >= segments // 2)
    return decoder, 1.0 - decoder, position == segments - 1


def edge_kernel(owner, cell, land, act_l, act_r, par_l, par_r, st_l, st_r, gr_l, gr_r, coarse, pay0, pay1):
    decoder, encoder, last = traits()
    rows = act_l.shape[1]
    groups = rows // 4
    per_row = cell.shape[0] // groups
    low = sublane((8, 128)) < 4

    def weights(first):
        parts = []
        for row in range(groups):
            pair = [jnp.where(last, land[row, first + k], 1).astype(F32) for k in range(2)]
            parts.append(jnp.where(low, pair[0], pair[1])[None])
        plane = jnp.concatenate(parts, axis=0)
        return jnp.broadcast_to(plane[:, None], (groups, 4, 8, 128)).reshape(rows, 8, 128)

    def ids(column):
        tile = jnp.zeros((8, 128), F32)
        where = sublane((8, 128))
        for row in range(groups):
            spot = row * per_row + column
            tile = jnp.where(where == row, owner[spot, 0].astype(F32), tile)
            tile = jnp.where(where == 4 + row, cell[spot].astype(F32), tile)
        return tile

    def parts(side, act, par, st, gr, first):
        pick = slice(0, 8) if side == 0 else slice(8, 16)
        f = lambda ref: ref[0].astype(F32)[:, pick]
        grad = ((f(gr) + encoder * f(par)) * weights(first)).astype(BF16).astype(F32)
        block = f(act) + decoder * f(par)
        return grad, f(st), block

    where = sublane((rows, 8, 128))
    grad, st, block = parts(0, act_l, par_l, st_l, gr_l, 0)
    after = jnp.where(
        where < 3, grad, jnp.where(where < 5, pltpu.roll(st, 3, 1), pltpu.roll(block, 5, 1))
    )
    grad, st, block = parts(1, act_r, par_r, st_r, gr_r, per_row - 2)
    before = jnp.where(
        where == 7, grad, jnp.where(where == 6, pltpu.roll(st, 7, 1), pltpu.roll(block, 6, 1))
    )
    even = lax.axis_index("ty") % 2 == 0
    pay0[0:rows] = jnp.where(even, before, after).astype(BF16)
    pay1[0:rows] = jnp.where(even, after, before).astype(BF16)
    left_ids, right_ids = ids(0), ids(per_row - 1)
    pay0[rows] = jnp.where(even, right_ids, left_ids).astype(BF16)
    pay1[rows] = jnp.where(even, left_ids, right_ids).astype(BF16)
    held = coarse[...].reshape(coarse.shape[0] // 8, 8, 128)
    pay0[rows + 1 :] = held
    pay1[rows + 1 :] = held


def extend_kernel(
    merged, owner, cell, land, act, par, st, gr, z0, z1, coarse, *rest
):
    if merged:
        z2, ypay0, ypay1, ext, table, plane = rest
    else:
        ypay0, ypay1, ext, table, plane = rest
    decoder, encoder, last = traits()
    rows, breadth = act.shape[1], act.shape[2]
    groups = rows // 4
    per_row = cell.shape[0] // groups
    cells = coarse.shape[0] if merged else cell.shape[0]
    ty, owners = lax.axis_index("ty"), lax.axis_size("ty")
    even = ty % 2 == 0
    has_before, has_after = ty > 0, ty < owners - 1
    low = sublane((8, 128)) < 4
    if merged:
        table[pl.ds(pl.multiple_of(ty * cells, 8), cells)] = coarse[...].astype(F32)
        others = (
            (ty ^ 1, z0[rows + 1 :].astype(F32).reshape(cells, 128)),
            (ty ^ 3, z1[rows + 1 :].astype(F32).reshape(cells, 128)),
            (ty ^ 2, z2[...].astype(F32)),
        )
        for other, value in others:
            table[pl.ds(pl.multiple_of(other * cells, 8), cells)] = value
    else:
        table[...] = coarse[...].astype(F32)

    first, second = z0[0 : rows + 1].astype(F32), z1[0 : rows + 1].astype(F32)
    before = jnp.where(has_before, jnp.where(even, second, first), 0.0)
    after = jnp.where(has_after, jnp.where(even, first, second), 0.0)

    def rim_condition(tile, valid):
        wanted = tile[rows]
        spot = wanted * cells + pltpu.roll(wanted, 4, 0)
        lanes = lax.broadcasted_iota(jnp.int32, (8, table.shape[0]), 1).astype(F32)
        spread = jnp.broadcast_to(spot[:, 0:1], lanes.shape)
        hot = jnp.where(spread == lanes, 1.0, 0.0).astype(BF16)
        named = lax.dot(hot, table[...].astype(BF16), preferred_element_type=F32)
        picked = [jnp.broadcast_to(named[row : row + 1], (8, 128))[None] for row in range(groups)]
        spread_rows = jnp.concatenate([p for p in picked for _ in range(4)], axis=0)
        return jnp.where(valid, spread_rows, 0.0)

    wide = LEFT + breadth
    ext[0, :, 0:8] = before[0:rows].astype(BF16)
    ext[1, :, 0:8] = pltpu.roll(before[0:rows], 1, 1).astype(BF16)
    rim = pltpu.roll(before[0:rows], 2, 1) + rim_condition(before, has_before)
    ext[2, :, 0:8] = rim.astype(BF16)
    ext[0, :, wide : wide + 8] = after[0:rows].astype(BF16)
    ext[1, :, wide : wide + 8] = pltpu.roll(after[0:rows], 5, 1).astype(BF16)
    rim = pltpu.roll(after[0:rows], 3, 1) + rim_condition(after, has_after)
    ext[2, :, wide : wide + 8] = rim.astype(BF16)
    ext[1, :, LEFT:wide] = st[0]

    for group in range(groups):
        for part in range(breadth // 8):
            spots = [group * per_row + 2 * part + k for k in range(2)]
            named = [
                jnp.broadcast_to(table[pl.ds(owner[s, 0] * cells + cell[s], 1)], (8, 128)) for s in spots
            ]
            plane[0, group, 8 * part : 8 * part + 8] = jnp.where(low, named[0], named[1])
            weigh = [jnp.where(last, land[group, 2 * part + k], 1).astype(F32) for k in range(2)]
            plane[1, group, 8 * part : 8 * part + 8] = jnp.where(low, weigh[0], weigh[1])
    for row in range(rows):
        partner = par[0, row].astype(F32)
        block = act[0, row].astype(F32) + decoder * partner + plane[0, row // 4]
        ext[2, row, LEFT:wide] = block.astype(BF16)
        grad = (gr[0, row].astype(F32) + encoder * partner) * plane[1, row // 4]
        ext[0, row, LEFT:wide] = grad.astype(BF16)

    upper = lax.axis_index("tx") % 2 == 0
    leading = [(0, 0), (0, 1), (0, 2), (1, 0), (1, 1), (2, 0), (2, 1)]
    closing = [(0, rows - 1), (1, rows - 1), (2, rows - 3), (2, rows - 2), (2, rows - 1)]
    closing = closing + closing[-1:] * 2
    for k in range(STRIP_ROWS):
        top, bottom = ext[leading[k]], ext[closing[k]]
        ypay0[k] = jnp.where(upper, bottom, top)
        ypay1[k] = jnp.where(upper, top, bottom)


def rims(y0, y1):
    tx = lax.axis_index("tx")
    upper = tx % 2 == 0
    before_ok, after_ok = tx > 0, tx < lax.axis_size("tx") - 1

    def row(valid, from_first, k):
        value = jnp.where(from_first, y0[k].astype(F32), y1[k].astype(F32))
        return jnp.where(valid, value, 0.0)

    before = lambda k: row(before_ok, jnp.logical_not(upper), k)
    after = lambda k: row(after_ok, upper, k)
    return before, after


def spread_taps(field, taps, odd_taps, count, first):
    for row in range(count):
        target = taps if row % 2 == 0 else odd_taps
        for tap in range(3):
            value = field[row, pl.ds(first + tap, PAD, stride=2), :]
            target[row // 2, :, tap * 128 : tap * 128 + 128] = value.astype(BF16)


def three_rows(even_taps, odd_taps, count):
    wide = 3 * 128
    whole = lambda ref, a: ref[a : a + count].reshape(count * PAD, wide)
    return whole(even_taps, 0), whole(odd_taps, 0), whole(even_taps, 1)


def lower(even_taps, odd_taps, count, down):
    views = three_rows(even_taps, odd_taps, count)
    wide = 3 * 128
    total = None
    for a in range(3):
        term = lax.dot(views[a], down[a * wide : a * wide + wide], preferred_element_type=F32)
        total = term if total is None else total + term
    return total


def lane_taps(up, flat_up):
    for tap in range(9):
        flat_up[:, tap * 128 : tap * 128 + 128] = up[tap]


def grads_kernel(
    ext, y0, y1, down, up, coupled, up_flat, down_flat, field, even_taps, odd_taps, sums, flat_up, d0, d1
):
    rows = ext.shape[1]
    breadth = ext.shape[2] - 16
    half_rows, half_cols = rows // 2, breadth // 2
    count = half_rows + 1
    before, after = rims(y0, y1)
    wide = ext.shape[2]
    tx, ty = lax.axis_index("tx"), lax.axis_index("ty")
    has_below, has_right = tx < lax.axis_size("tx") - 1, ty < lax.axis_size("ty") - 1
    lane_taps(up, flat_up)
    field[:, wide:] = jnp.zeros((field.shape[0], field.shape[1] - wide, 128), F32)
    field[0, 0:wide] = before(1)
    for row in range(rows):
        field[row + 1, 0:wide] = ext[1, row].astype(F32)
    for k in range(2):
        field[rows + 1 + k, 0:wide] = after(3 + k)
    spread_taps(field, even_taps, odd_taps, 2 * count + 1, LEFT - 1)
    pre_back = lower(even_taps, odd_taps, count, down)
    logistic = 1.0 / (1.0 + jnp.exp(-pre_back))
    reduced = pre_back * logistic
    slope = logistic * (1.0 + pre_back * (1.0 - logistic))
    depth = pre_back.shape[1]
    shape = (count, PAD, depth)
    row = lax.broadcasted_iota(jnp.int32, shape, 0).reshape(count * PAD, depth)
    col = lax.broadcasted_iota(jnp.int32, shape, 1).reshape(count * PAD, depth)
    own = (row < half_rows) & (col < half_cols)
    inside = ((row < half_rows) | has_below) & ((col < half_cols) | (has_right & (col == half_cols)))
    reduced = jnp.where(own, reduced, 0.0).astype(BF16)

    field[0, 0:wide] = before(0)
    for row_id in range(rows):
        field[row_id + 1, 0:wide] = ext[0, row_id].astype(F32)
    for k in range(3):
        field[rows + 1 + k, 0:wide] = after(k)
    previous = None
    for row_id in range(2 * count + 2):
        plane = [field[row_id, pl.ds(LEFT - 1 + k, PAD, stride=2), :] for k in range(4)]
        current = [plane[2] + plane[3], plane[1] + plane[2], plane[0] + plane[1]]
        if row_id > 0:
            start = row_id - 2
            for a in range(3):
                if (start - 1 + a) % 2 == 0 and 0 <= (start - 1 + a) // 2 < count:
                    p = (start - 1 + a) // 2
                    for b in range(3):
                        tap = 3 * a + b
                        sums[p, :, tap * 128 : tap * 128 + 128] = (previous[b] + current[b]).astype(BF16)
        previous = current
    windows = sums[...].reshape(count * PAD, 9 * 128)
    raised = lax.dot_general(windows, flat_up[...], (((1,), (1,)), ((), ())), preferred_element_type=F32)
    pre_grad = jnp.where(inside, raised * slope, 0.0).astype(BF16)
    coupled[...] = pre_grad.reshape(count, PAD, depth)

    terms = lax.dot_general(reduced, windows, (((0,), (0,)), ((), ())), preferred_element_type=F32)
    for tap in range(9):
        up_flat[tap * depth : tap * depth + depth] = terms[:, tap * 128 : tap * 128 + 128]

    own_grad = jnp.where(own, pre_grad, jnp.zeros_like(pre_grad))
    views = three_rows(even_taps, odd_taps, count)
    span = 3 * 128
    for a in range(3):
        term = lax.dot_general(views[a], own_grad, (((0,), (0,)), ((), ())), preferred_element_type=F32)
        d0[a * span : a * span + span] = term[:, 0:128]
        d1[a * span : a * span + span, 0:64] = term[:, 128:192]
    pairs = d0.shape[0] // 2
    left_even, left_odd = d0[pl.ds(0, pairs, stride=2)], d0[pl.ds(1, pairs, stride=2)]
    right_even, right_odd = d1[pl.ds(0, pairs, stride=2)], d1[pl.ds(1, pairs, stride=2)]
    near = lax.broadcasted_iota(jnp.int32, left_even.shape, 1) < 64
    turned = pltpu.roll(left_odd, 64, 1)
    down_flat[pl.ds(0, pairs, stride=3)] = left_even
    down_flat[pl.ds(1, pairs, stride=3)] = jnp.where(near, right_even, turned)
    down_flat[pl.ds(2, pairs, stride=3)] = jnp.where(near, turned, pltpu.roll(right_odd, 64, 1))


def relay_kernel(
    ext, y0, y1, coupled, down, up, ahead, behind, field, even_taps, odd_taps, products, flat_up, mixed, fine
):
    rows = ext.shape[1]
    breadth = ext.shape[2] - 16
    half_rows, half_cols = rows // 2, breadth // 2
    wide = ext.shape[2]
    depth = coupled.shape[2]
    tx, ty = lax.axis_index("tx"), lax.axis_index("ty")
    has_below, has_right = tx < lax.axis_size("tx") - 1, ty < lax.axis_size("ty") - 1
    position, segments = lax.axis_index("segment"), lax.axis_size("segment")

    count = half_rows + 1
    grads = coupled[...].reshape(count * PAD, depth)
    moved = lax.dot_general(grads, down[...], (((1,), (1,)), ((), ())), preferred_element_type=F32)
    products[0:count] = moved.reshape(count, PAD, 9 * 128)

    def part(p, a, b, offset):
        tap = 3 * a + b
        return products[p, offset : offset + half_cols, tap * 128 : tap * 128 + 128]

    for p in range(half_rows):
        fine[2 * p, pl.ds(0, half_cols, stride=2), :] = part(p, 1, 1, 0)
        fine[2 * p, pl.ds(1, half_cols, stride=2), :] = part(p, 1, 2, 0) + part(p, 1, 0, 1)
        fine[2 * p + 1, pl.ds(0, half_cols, stride=2), :] = part(p, 2, 1, 0) + part(p + 1, 0, 1, 0)
        fine[2 * p + 1, pl.ds(1, half_cols, stride=2), :] = (
            part(p, 2, 2, 0) + part(p, 2, 0, 1) + part(p + 1, 0, 2, 0) + part(p + 1, 0, 0, 1)
        )
    for row in range(rows):
        value = ext[0, row, LEFT : LEFT + breadth].astype(F32) + fine[row]
        behind[row] = value.astype(BF16)

    lane_taps(up, flat_up)
    before, after = rims(y0, y1)
    count = half_rows + 2
    field[:, wide:] = jnp.zeros((field.shape[0], field.shape[1] - wide, 128), F32)
    for k in range(3):
        field[k, 0:wide] = before(2 + k)
    for row in range(rows):
        field[row + 3, 0:wide] = ext[2, row].astype(F32)
    for k in range(2):
        field[rows + 3 + k, 0:wide] = after(5 + k)
    spread_taps(field, even_taps, odd_taps, 2 * count + 1, LEFT - 3)
    pre_down = lower(even_taps, odd_taps, count, down)
    reduced = pre_down / (1.0 + jnp.exp(-pre_down))
    shape = (count, PAD, depth)
    row_id = lax.broadcasted_iota(jnp.int32, shape, 0).reshape(count * PAD, depth)
    col_id = lax.broadcasted_iota(jnp.int32, shape, 1).reshape(count * PAD, depth)
    inside = ((row_id <= half_rows) | has_below) & ((col_id <= half_cols) | has_right)
    reduced = jnp.where(inside, reduced, 0.0).astype(BF16)
    raised = lax.dot(reduced, flat_up[...], preferred_element_type=F32)
    products[0:count] = raised.reshape(count, PAD, 9 * 128)

    def tap_rows(p, dy, b):
        at = lambda q, a: products[q, :, (3 * a + b) * 128 : (3 * a + b) * 128 + 128]
        if dy == 0:
            return at(p, 0) + at(p + 1, 1) + at(p + 1, 2)
        return at(p + 1, 0) + at(p + 1, 1) + at(p + 2, 2)

    for p in range(half_rows):
        for dy in range(2):
            col = [tap_rows(p, dy, b) for b in range(3)]
            mixed[0, 0:PAD], mixed[1, 0:PAD] = col[0], col[1] + col[2]
            mixed[2, 0:PAD], mixed[3, 0:PAD] = col[0] + col[1], col[2]
            line = 2 * p + dy
            fine[line, pl.ds(0, half_cols, stride=2), :] = mixed[0, 0:half_cols] + mixed[1, 1 : half_cols + 1]
            fine[line, pl.ds(1, half_cols, stride=2), :] = (
                mixed[2, 1 : half_cols + 1] + mixed[3, 2 : half_cols + 2]
            )
    for row in range(rows):
        value = (ext[2, row, LEFT : LEFT + breadth].astype(F32) + fine[row]).astype(BF16)
        in_grad = behind[row]
        ahead[row] = jnp.where(position == segments - 1, in_grad, value)
        behind[row] = jnp.where(position == 0, value, in_grad)


def swaps(axis):
    size = lax.axis_size(axis)
    pairs = [(i, i + 1) for i in range(0, size - 1, 2)]
    other = [(i, i + 1) for i in range(1, size - 1, 2)]
    both = lambda pairs: pairs + [(j, i) for i, j in pairs]
    return both(pairs), both(other)


def crossed(axis, distance):
    return [(i, i ^ distance) for i in range(lax.axis_size(axis))]


def split_kernel(up_flat, down_flat, up_send, up_keep, down_send, down_keep):
    half = up_keep.shape[0]
    tx = lax.axis_index("tx")
    mine, theirs = pl.multiple_of(tx * half, 8), pl.multiple_of((1 - tx) * half, 8)
    for flat, send, keep in ((up_flat, up_send, up_keep), (down_flat, down_send, down_keep)):
        send[...] = flat[pl.ds(theirs, half)].astype(BF16)
        keep[...] = flat[pl.ds(mine, half)]


def pieces_kernel(got, kept, own, *sends):
    count = own.shape[0]
    ty = lax.axis_index("ty")
    for distance, target in enumerate(sends):
        start = pl.multiple_of((ty ^ (distance + 1)) * count, 8)
        total = kept[pl.ds(start, count)] + got[pl.ds(start, count)].astype(F32)
        target[...] = total.astype(BF16)
    start = pl.multiple_of(ty * count, 8)
    own[...] = kept[pl.ds(start, count)] + got[pl.ds(start, count)].astype(F32)


def total_kernel(scaling, own, first, second, third, out):
    total = own[...] + first[...].astype(F32) + second[...].astype(F32) + third[...].astype(F32)
    out[...] = total * scaling


def shape(dims, kind):
    return jax.ShapeDtypeStruct(tuple(dims), kind)


def local(
    act_in,
    partner_in,
    stashed,
    grad_in,
    down_weights,
    up_weights,
    coarse,
    nest_owner,
    nest_cell,
    land_weight,
):
    height, breadth, channels = act_in.shape[1:]
    depth = down_weights.shape[-1]
    half_rows = height // 2
    n_tx, n_ty = lax.axis_size("tx"), lax.axis_size("ty")
    position, segments = lax.axis_index("segment"), lax.axis_size("segment")
    scaling = 1.0 / math.sqrt(height * breadth * n_tx * n_ty)
    down_flat_w = down_weights.reshape(9 * channels, depth)
    up_taps = up_weights.reshape(9, depth, channels)

    left = pl.BlockSpec((1, height, 16, channels), lambda i: (0, 0, 0, 0))
    right = pl.BlockSpec((1, height, 16, channels), lambda i: (0, 0, breadth // 16 - 1, 0))
    pay = shape((height + 1 + coarse.shape[0] // 8, 8, channels), BF16)
    z_pay0, z_pay1 = call(edge_kernel, (pay, pay), [SMEM] * 3 + [left, right] * 4 + [whole_block(coarse)], grid=(1,))(
        nest_owner,
        nest_cell,
        land_weight,
        act_in,
        act_in,
        partner_in,
        partner_in,
        stashed,
        stashed,
        grad_in,
        grad_in,
        coarse,
    )
    merged = n_ty == 4
    pairs, others = swaps("ty")
    if merged:
        others = crossed("ty", 3)
    z0 = lax.ppermute(z_pay0, "ty", pairs)
    z1 = lax.ppermute(z_pay1, "ty", others)
    if merged:
        table_parts = (coarse, lax.ppermute(coarse, "ty", crossed("ty", 2)))
    else:
        table_parts = (lax.all_gather(coarse, "ty", tiled=True),)
    strips = shape((STRIP_ROWS, breadth + 16, channels), BF16)
    operands = (act_in, partner_in, stashed, grad_in, z0, z1, table_parts[0], *table_parts[1:])
    y_pay0, y_pay1, ext = call(
        functools.partial(extend_kernel, merged),
        (strips, strips, shape((3, height, breadth + 16, channels), BF16)),
        [SMEM] * 3 + [VMEM] * len(operands),
        [
            pltpu.VMEM((n_ty * coarse.shape[0], channels), F32),
            pltpu.VMEM((2, height // 4, breadth, channels), F32),
        ],
    )(nest_owner, nest_cell, land_weight, *operands)
    pairs, others = swaps("tx")
    y0 = lax.ppermute(y_pay0, "tx", pairs)
    y1 = lax.ppermute(y_pay1, "tx", others) if others else y_pay1

    wide = 2 * PAD + 16
    count = half_rows + 2
    rows_flat = 9 * depth
    taps = [
        pltpu.VMEM((2 * count + 2, wide, channels), F32),
        pltpu.VMEM((count + 1, PAD, 3 * channels), BF16),
        pltpu.VMEM((count + 1, PAD, 3 * channels), BF16),
    ]
    flat_up = pltpu.VMEM((depth, 9 * channels), BF16)
    coupled, up_flat, down_flat = call(
        grads_kernel,
        (
            shape((half_rows + 1, PAD, depth), BF16),
            shape((rows_flat, channels), F32),
            shape((rows_flat, channels), F32),
        ),
        [VMEM] * 5,
        taps
        + [
            pltpu.VMEM((half_rows + 1, PAD, 9 * channels), BF16),
            flat_up,
            pltpu.VMEM((9 * channels, 128), F32),
            pltpu.VMEM((9 * channels, 128), F32),
        ],
        flops=500_000_000,
        moved=4_000_000,
    )(ext, y0, y1, down_flat_w, up_taps)

    if n_tx == 2 and n_ty == 4:
        half, piece = rows_flat // 2, rows_flat // 8
        up_send, up_keep, down_send, down_keep = call(
            split_kernel,
            (shape((half, channels), BF16), shape((half, channels), F32)) * 2,
            [VMEM] * 2,
        )(up_flat, down_flat)
        sums = []
        for send, keep in ((down_send, down_keep), (up_send, up_keep)):
            got = lax.ppermute(send, "tx", crossed("tx", 1))
            own, *sends = call(
                pieces_kernel,
                (shape((piece, channels), F32),) + (shape((piece, channels), BF16),) * 3,
                [VMEM] * 2,
            )(got, keep)
            arrived = [lax.ppermute(s, "ty", crossed("ty", d + 1)) for d, s in enumerate(sends)]
            total = call(
                functools.partial(total_kernel, scaling), shape((piece, channels), F32), [VMEM] * 4
            )(own, *arrived)
            sums.append(total.reshape(1, -1))
        down_sum, up_sum = sums
    else:
        pooled = lambda flat: lax.psum_scatter(
            flat.reshape(-1) * scaling, ("tx", "ty"), scatter_dimension=0, tiled=True
        )[None]
        down_sum, up_sum = pooled(down_flat), pooled(up_flat)

    tile = shape((height, breadth, channels), BF16)
    ahead, behind = call(
        relay_kernel,
        (tile, tile),
        [VMEM] * 6,
        taps
        + [
            pltpu.VMEM((count, PAD, 9 * channels), F32),
            flat_up,
            pltpu.VMEM((4, PAD, channels), F32),
            pltpu.VMEM((height, breadth, channels), F32),
        ],
        flops=600_000_000,
        moved=4_000_000,
    )(ext, y0, y1, coupled, down_flat_w, up_taps)
    from_before = lax.ppermute(ahead, "segment", [(i, (i + 1) % segments) for i in range(segments)])
    from_after = lax.ppermute(behind, "segment", [((i + 1) % segments, i) for i in range(segments)])
    blank = jnp.zeros_like(from_before)
    act_out = jnp.where(position == 0, blank, from_before)
    grad_out = jnp.where(position == segments - 1, blank, from_after)
    partner_out = jnp.where(position % 2 == 0, from_before, from_after)
    return (act_out[None], grad_out[None], partner_out[None], down_sum, up_sum)


def solution(mesh):
    tile = P("segment", "tx", "ty", None)
    weights = P("segment", None, None, None, None)
    grads = P("segment", ("tx", "ty"))
    rows = P(("tx", "ty"))
    return jax.shard_map(
        local,
        mesh=mesh,
        in_specs=(tile,) * 4 + (weights,) * 2 + (P(("tx", "ty"), None),) * 2 + (rows, P("tx", "ty")),
        out_specs=(tile,) * 3 + (grads,) * 2,
        check_vma=False,
    )
```

```python
import functools
import math

import jax
import jax.numpy as jnp
from jax import lax
from jax.experimental import pallas as pl
from jax.experimental.pallas import tpu as pltpu
from jax.sharding import PartitionSpec as P

F32 = jnp.float32
BF16 = jnp.bfloat16
VMEM = pl.BlockSpec(memory_space=pltpu.VMEM)
SMEM = pl.BlockSpec(memory_space=pltpu.SMEM)
HBM = pl.BlockSpec(memory_space=pltpu.HBM)
LEFT = 8
PAD = 48
STRIP_ROWS = 7


def call(body, out_shape, in_specs, scratch=(), flops=0, moved=0, limit=48):
    out_specs = jax.tree.map(lambda _: VMEM, out_shape)
    return pl.pallas_call(
        body,
        out_shape=out_shape,
        in_specs=in_specs,
        out_specs=out_specs,
        scratch_shapes=list(scratch),
        compiler_params=pltpu.CompilerParams(vmem_limit_bytes=limit * 1024 * 1024),
        cost_estimate=pl.CostEstimate(flops=flops, bytes_accessed=moved, transcendentals=0),
    )


def in_hbm(*operands):
    return [pltpu.with_memory_space_constraint(x, pltpu.HBM) for x in operands]


def sublane(shape):
    return lax.broadcasted_iota(jnp.int32, shape, len(shape) - 2)


def flag(condition):
    return jnp.where(condition, 1.0, 0.0).astype(F32)


def traits():
    segments = lax.axis_size("segment")
    position = lax.axis_index("segment")
    decoder = flag(position >= segments // 2)
    return decoder, 1.0 - decoder, position == segments - 1


def edge_kernel(owner_in, cell_in, land_in, act, par, st, gr, coarse, grad_out, pay0, pay1, *scratch):
    act_l, act_r, st_l, st_r, par_v, gr_v, plane, held_v, owner, cell, land, arrived = scratch
    rows, breadth = gr.shape[1], gr.shape[2]
    first, final = pl.ds(0, 16), pl.ds(breadth - 16, 16)
    copies = [
        pltpu.make_async_copy(source, target, arrived.at[k])
        for k, (source, target) in enumerate(
            (
                (gr.at[0], gr_v),
                (par.at[0], par_v),
                (act.at[0, :, first], act_l),
                (act.at[0, :, final], act_r),
                (st.at[0, :, first], st_l),
                (st.at[0, :, final], st_r),
                (coarse, held_v),
                (owner_in, owner),
                (cell_in, cell),
                (land_in, land),
            )
        )
    ]
    for copy in copies:
        copy.start()
    for copy in copies[7:]:
        copy.wait()
    decoder, encoder, last = traits()
    groups = rows // 4
    per_row = breadth // 4
    low = sublane((8, 128)) < 4
    for group in range(groups):
        for part in range(breadth // 8):
            weigh = [jnp.where(last, land[group, 2 * part + k], 1).astype(F32) for k in range(2)]
            plane[group, 8 * part : 8 * part + 8] = jnp.where(low, weigh[0], weigh[1])

    def ids(column):
        tile = jnp.zeros((8, 128), F32)
        where = sublane((8, 128))
        for row in range(groups):
            spot = row * per_row + column
            tile = jnp.where(where == row, owner[spot].astype(F32), tile)
            tile = jnp.where(where == 4 + row, cell[spot].astype(F32), tile)
        return tile

    left_ids, right_ids = ids(0), ids(per_row - 1)
    for copy in copies[:7]:
        copy.wait()
    for row in range(rows):
        grad = gr_v[row].astype(F32) + encoder * par_v[row].astype(F32)
        grad_out[row] = (grad * plane[row // 4]).astype(BF16)

    where = sublane((rows, 8, 128))
    begin, end = slice(0, 16), slice(breadth - 16, breadth)
    grad = grad_out[:, begin].astype(F32)[:, 0:8]
    stash = st_l[...].astype(F32)[:, 0:8]
    block = act_l[...].astype(F32)[:, 0:8] + decoder * par_v[:, begin].astype(F32)[:, 0:8]
    after = jnp.where(
        where < 3, grad, jnp.where(where < 5, pltpu.roll(stash, 3, 1), pltpu.roll(block, 5, 1))
    )
    grad = grad_out[:, end].astype(F32)[:, 8:16]
    stash = st_r[...].astype(F32)[:, 8:16]
    block = act_r[...].astype(F32)[:, 8:16] + decoder * par_v[:, end].astype(F32)[:, 8:16]
    before = jnp.where(
        where == 7, grad, jnp.where(where == 6, pltpu.roll(stash, 7, 1), pltpu.roll(block, 6, 1))
    )
    even = lax.axis_index("ty") % 2 == 0
    strips = jnp.where(even, before, after).astype(BF16), jnp.where(even, after, before).astype(BF16)
    named = jnp.where(even, right_ids, left_ids), jnp.where(even, left_ids, right_ids)
    held = held_v[...].reshape(coarse.shape[0] // 8, 8, 128)
    for k, pay in enumerate((pay0, pay1)):
        pay[0:rows] = strips[k]
        pay[rows] = named[k].astype(BF16)
        pay[rows + 1 :] = held


def prepare_kernel(act, par, st, up, down, base, stash, flat_up, flat_down, *scratch):
    act_v, par_v, up_v, down_v, arrived = scratch
    pairs = (act.at[0], act_v), (par.at[0], par_v), (up, up_v), (down, down_v), (st.at[0], stash)
    copies = [pltpu.make_async_copy(*pair, arrived.at[k]) for k, pair in enumerate(pairs)]
    for copy in copies:
        copy.start()
    decoder, _, _ = traits()
    for copy in copies:
        copy.wait()
    for row in range(act_v.shape[0]):
        base[row] = act_v[row].astype(F32) + decoder * par_v[row].astype(F32)
    lane_taps(up_v, flat_up)
    lane_taps(down_v, flat_down)


def side_rims(z0, z1, rows):
    ty = lax.axis_index("ty")
    even = ty % 2 == 0
    first, second = z0[0:rows].astype(F32), z1[0:rows].astype(F32)
    before = jnp.where(ty > 0, jnp.where(even, second, first), 0.0)
    after = jnp.where(ty < lax.axis_size("ty") - 1, jnp.where(even, first, second), 0.0)
    return before, after


def rim_kernel(z0, z1, _weights, _stash, rim):
    before, after = side_rims(z0, z1, rim.shape[0])
    rim[...] = jnp.where(sublane(rim.shape) < 5, after, before).astype(BF16)


def condition_kernel(merged, owner, cell, base, z0, z1, coarse, *rest):
    rows, breadth = base.shape[0], base.shape[1]
    groups = rows // 4
    per_row = breadth // 4
    cells = groups * per_row
    wide = LEFT + breadth
    ty = lax.axis_index("ty")
    low = sublane((8, 128)) < 4
    if merged:
        z2, pay, ext, table, plane = rest
        table[pl.ds(pl.multiple_of(ty * cells, 8), cells)] = coarse[...].astype(F32)
        others = (
            (ty ^ 1, z0[rows + 1 :].astype(F32).reshape(cells, 128)),
            (ty ^ 3, z1[rows + 1 :].astype(F32).reshape(cells, 128)),
            (ty ^ 2, z2[...].astype(F32)),
        )
        for other, value in others:
            table[pl.ds(pl.multiple_of(other * cells, 8), cells)] = value
    else:
        st, grad_own, pay, pay1, full, table, plane = rest
        ext = full.at[2]
        table[...] = coarse[...].astype(F32)
    before, after = side_rims(z0, z1, rows + 1)

    def rim_condition(tile, valid):
        wanted = tile[rows]
        spot = wanted * cells + pltpu.roll(wanted, 4, 0)
        lanes = lax.broadcasted_iota(jnp.int32, (8, table.shape[0]), 1).astype(F32)
        spread = jnp.broadcast_to(spot[:, 0:1], lanes.shape)
        hot = jnp.where(spread == lanes, 1.0, 0.0).astype(BF16)
        named = lax.dot(hot, table[...].astype(BF16), preferred_element_type=F32)
        picked = [jnp.broadcast_to(named[row : row + 1], (8, 128))[None] for row in range(groups)]
        spread_rows = jnp.concatenate([p for p in picked for _ in range(4)], axis=0)
        return jnp.where(valid, spread_rows, 0.0)

    rim = pltpu.roll(before[0:rows], 2, 1) + rim_condition(before, ty > 0)
    ext[:, 0:8] = rim.astype(BF16)
    rim = pltpu.roll(after[0:rows], 3, 1) + rim_condition(after, ty < lax.axis_size("ty") - 1)
    ext[:, wide : wide + 8] = rim.astype(BF16)
    for group in range(groups):
        for part in range(breadth // 8):
            spots = [group * per_row + 2 * part + k for k in range(2)]
            named = [
                jnp.broadcast_to(table[pl.ds(owner[s] * cells + cell[s], 1)], (8, 128)) for s in spots
            ]
            plane[group, 8 * part : 8 * part + 8] = jnp.where(low, named[0], named[1])
    for row in range(rows):
        ext[row, LEFT:wide] = (base[row] + plane[row // 4]).astype(BF16)

    upper = lax.axis_index("tx") % 2 == 0
    if merged:
        near = sublane((8, 128)) < 5
        for k in range(3):
            top, bottom = min(k, 1), rows - 3 + k
            for part in range(breadth // 8):
                cols = pl.ds(LEFT + 8 * part, 8)
                pay[9 * k + part] = jnp.where(upper, ext[bottom, cols], ext[top, cols])
            tiles = [
                jnp.where(near, ext[row, pl.ds(wide, 8)], ext[row, pl.ds(0, 8)]) for row in (top, bottom)
            ]
            pay[9 * k + breadth // 8] = jnp.where(upper, tiles[1], tiles[0])
        return
    full[0, :, 0:8] = before[0:rows].astype(BF16)
    full[1, :, 0:8] = pltpu.roll(before[0:rows], 1, 1).astype(BF16)
    full[0, :, wide : wide + 8] = after[0:rows].astype(BF16)
    full[1, :, wide : wide + 8] = pltpu.roll(after[0:rows], 5, 1).astype(BF16)
    full[0, :, LEFT:wide] = grad_own[...]
    full[1, :, LEFT:wide] = st[...]
    leading = [(0, 0), (0, 1), (0, 2), (1, 0), (1, 1), (2, 0), (2, 1)]
    closing = [(0, rows - 1), (1, rows - 1), (2, rows - 3), (2, rows - 2), (2, rows - 1)]
    closing = closing + closing[-1:] * 2
    for k in range(STRIP_ROWS):
        top, bottom = full[leading[k]], full[closing[k]]
        pay[k] = jnp.where(upper, bottom, top)
        pay1[k] = jnp.where(upper, top, bottom)


def rims(y0, y1):
    tx = lax.axis_index("tx")
    upper = tx % 2 == 0
    before_ok, after_ok = tx > 0, tx < lax.axis_size("tx") - 1

    def row(valid, from_first, k):
        value = jnp.where(from_first, y0[k].astype(F32), y1[k].astype(F32))
        return jnp.where(valid, value, 0.0)

    before = lambda k: row(before_ok, jnp.logical_not(upper), k)
    after = lambda k: row(after_ok, upper, k)
    return before, after


def spread_taps(field, taps, odd_taps, count, first):
    for row in range(count):
        target = taps if row % 2 == 0 else odd_taps
        for tap in range(3):
            value = field[row, pl.ds(first + tap, PAD, stride=2), :]
            target[row // 2, :, tap * 128 : tap * 128 + 128] = value.astype(BF16)


def three_rows(even_taps, odd_taps, count):
    wide = 3 * 128
    whole = lambda ref, a: ref[a : a + count].reshape(count * PAD, wide)
    return whole(even_taps, 0), whole(odd_taps, 0), whole(even_taps, 1)


def lower(even_taps, odd_taps, count, down):
    views = three_rows(even_taps, odd_taps, count)
    wide = 3 * 128
    total = None
    for a in range(3):
        term = lax.dot_general(
            views[a],
            down[:, a * wide : a * wide + wide],
            (((1,), (1,)), ((), ())),
            preferred_element_type=F32,
        )
        total = term if total is None else total + term
    return total


def lane_taps(taps, flat):
    for tap in range(9):
        flat[:, tap * 128 : tap * 128 + 128] = taps[tap]


def sweep(wide, field, even_taps, odd_taps, sums, flat_up, down, count, fill_stash, fill_grad):
    field[:, wide:] = jnp.zeros((field.shape[0], field.shape[1] - wide, 128), F32)
    fill_stash()
    spread_taps(field, even_taps, odd_taps, 2 * count + 1, LEFT - 1)
    pre_back = lower(even_taps, odd_taps, count, down)
    logistic = 1.0 / (1.0 + jnp.exp(-pre_back))
    reduced = pre_back * logistic
    slope = logistic * (1.0 + pre_back * (1.0 - logistic))
    fill_grad()
    previous = None
    for row in range(2 * count + 2):
        plane = [field[row, pl.ds(LEFT - 1 + k, PAD, stride=2), :] for k in range(4)]
        current = [plane[2] + plane[3], plane[1] + plane[2], plane[0] + plane[1]]
        if row > 0:
            for a in range(3):
                double = row - 3 + a
                if double % 2 == 0 and 0 <= double // 2 < count:
                    for b in range(3):
                        lanes = slice((3 * a + b) * 128, (3 * a + b) * 128 + 128)
                        sums[double // 2, :, lanes] = (previous[b] + current[b]).astype(BF16)
        previous = current
    windows = sums[...].reshape(count * PAD, 9 * 128)
    raised = lax.dot_general(windows, flat_up[...], (((1,), (1,)), ((), ())), preferred_element_type=F32)
    return reduced.astype(BF16), raised * slope


def places(count, depth):
    shape = (count, PAD, depth)
    row = lax.broadcasted_iota(jnp.int32, shape, 0).reshape(count * PAD, depth)
    col = lax.broadcasted_iota(jnp.int32, shape, 1).reshape(count * PAD, depth)
    return row, col


def flatten_rows(d0, d1, flat, start):
    pairs = d0.shape[0] // 2
    left_even, left_odd = d0[pl.ds(0, pairs, stride=2)], d0[pl.ds(1, pairs, stride=2)]
    right_even, right_odd = d1[pl.ds(0, pairs, stride=2)], d1[pl.ds(1, pairs, stride=2)]
    near = lax.broadcasted_iota(jnp.int32, left_even.shape, 1) < 64
    turned = pltpu.roll(left_odd, 64, 1)
    flat[pl.ds(start, pairs, stride=3)] = left_even
    flat[pl.ds(start + 1, pairs, stride=3)] = jnp.where(near, right_even, turned)
    flat[pl.ds(start + 2, pairs, stride=3)] = jnp.where(near, turned, pltpu.roll(right_odd, 64, 1))


def across(left, right):
    return lax.dot_general(left, right, (((0,), (0,)), ((), ())), preferred_element_type=F32)


def grads_kernel(
    ext, y0, y1, flat_up, flat_down, in_grad, up_flat, down_flat, field, even_taps, odd_taps, sums, d0, d1, products, fine
):
    rows = ext.shape[1]
    wide = ext.shape[2]
    half_rows, half_cols = rows // 2, (wide - 16) // 2
    count = half_rows + 1
    before, after = rims(y0, y1)
    tx, ty = lax.axis_index("tx"), lax.axis_index("ty")
    has_below, has_right = tx < lax.axis_size("tx") - 1, ty < lax.axis_size("ty") - 1

    def fill(kind, top, bottom):
        field[0, 0:wide] = before(top)
        for row in range(rows):
            field[row + 1, 0:wide] = ext[kind, row].astype(F32)
        for k, spot in enumerate(bottom):
            field[rows + 1 + k, 0:wide] = after(spot)

    reduced, pre_grad = sweep(
        wide,
        field,
        even_taps,
        odd_taps,
        sums,
        flat_up,
        flat_down,
        count,
        lambda: fill(1, 1, (3, 4)),
        lambda: fill(0, 0, (0, 1, 2)),
    )
    depth = reduced.shape[1]
    row, col = places(count, depth)
    inside = ((row < half_rows) | has_below) & ((col < half_cols) | (has_right & (col == half_cols)))
    pre_grad = jnp.where(inside, pre_grad, 0.0).astype(BF16).reshape(count, PAD, depth)
    base = lambda row_id: ext[0, row_id, LEFT : wide - 8]
    input_grad(pre_grad, flat_down, base, products, fine, in_grad)
    cells = half_rows * half_cols
    own = lambda value: value[:half_rows, :half_cols].reshape(cells, value.shape[-1])
    reduced, own_grad = own(reduced.reshape(count, PAD, depth)), own(pre_grad)
    terms = across(reduced, own(sums))
    for tap in range(9):
        up_flat[tap * depth : tap * depth + depth] = terms[:, tap * 128 : tap * 128 + 128]
    span = 3 * 128
    for a, view in enumerate((even_taps, odd_taps, even_taps)):
        taps = view[a // 2 : a // 2 + half_rows, 0:half_cols].reshape(cells, span)
        term = across(taps, own_grad)
        d0[a * span : a * span + span] = term[:, 0:128]
        d1[a * span : a * span + span, 0:64] = term[:, 128:192]
    flatten_rows(d0, d1, down_flat, 0)


def paired_kernel(
    st, grad, st_far, grad_far, rim, rim_far, flat_up, flat_down, in_grad, own_sum, send1, send2, send3, *scratch
):
    field, even_taps, odd_taps, sums, d0, d1, up_flat, down_flat, grads, products, fine = scratch
    rows, breadth = grad.shape[0], grad.shape[1]
    wide = breadth + 16
    count, half_cols = rows, breadth // 2
    tx, ty = lax.axis_index("tx"), lax.axis_index("ty")
    has_right = ty < lax.axis_size("ty") - 1

    def fill(here_rows, there_rows, turn_before, turn_after):
        blank = jnp.zeros((wide, 128), F32)
        field[0, 0:wide] = blank
        field[2 * rows + 1, 0:wide] = blank
        here, there = 1 + rows * tx, 1 + rows * (1 - tx)
        for start, source, sides in ((here, here_rows, rim), (there, there_rows, rim_far)):
            for row in range(rows):
                field[start + row, LEFT : LEFT + breadth] = source(row).astype(F32)
            sides = sides[...].astype(F32)
            turned = lambda turn: pltpu.roll(sides, turn, 1) if turn else sides
            field[pl.ds(start, rows), 0:8] = turned(turn_before)
            field[pl.ds(start, rows), LEFT + breadth : wide] = turned(turn_after)

    reduced, pre_grad = sweep(
        wide,
        field,
        even_taps,
        odd_taps,
        sums,
        flat_up,
        flat_down,
        count,
        lambda: fill(lambda row: st[row], lambda row: st_far[0, row], 1, 5),
        lambda: fill(lambda row: grad[row], lambda row: grad_far[row], 0, 0),
    )
    depth = reduced.shape[1]
    _, col = places(count, depth)
    inside = (col < half_cols) | (has_right & (col == half_cols))
    pre_grad = jnp.where(inside, pre_grad, 0.0).astype(BF16).reshape(count, PAD, depth)
    grads[0:count] = pre_grad
    grads[count] = jnp.zeros((PAD, depth), BF16)
    base = lambda row: grad[row]
    input_grad(grads[pl.ds(rows // 2 * tx, rows // 2 + 1)], flat_down, base, products, fine, in_grad)
    cells = count * half_cols
    own = lambda value: value[:, :half_cols].reshape(cells, value.shape[-1])
    reduced, own_grad = own(reduced.reshape(count, PAD, depth)), own(pre_grad)
    half = up_flat.shape[0] - depth // 2
    lanes = pl.ds(pl.multiple_of(tx * 512, 128), 640)
    terms = across(reduced, sums[:, 0:half_cols, lanes].reshape(cells, 640))
    for tap in range(5):
        up_flat[tap * depth : tap * depth + depth] = terms[:, tap * 128 : tap * 128 + 128]
    span = 3 * 128
    outer = across(even_taps[pl.ds(tx, count), 0:half_cols].reshape(cells, span), own_grad)
    middle = across(odd_taps[0:count, 0:half_cols].reshape(cells, span), own_grad)
    outer_at = pl.multiple_of(tx * (span // 2), 8)
    middle_at = pl.multiple_of((1 - tx) * span, 8)
    middle_half = jnp.where(tx == 0, middle[0 : span // 2], middle[span // 2 : span])
    d0[pl.ds(outer_at, span)] = outer[:, 0:128]
    d1[pl.ds(outer_at, span), 0:64] = outer[:, 128:192]
    d0[pl.ds(middle_at, span // 2)] = middle_half[:, 0:128]
    d1[pl.ds(middle_at, span // 2), 0:64] = middle_half[:, 128:192]
    flatten_rows(d0, d1, down_flat, 0)
    piece = half // 4
    up_start = tx * (depth // 2)
    for distance, target in enumerate((own_sum, send1, send2, send3)):
        place = (ty ^ distance) * piece
        both = [
            up_flat[pl.ds(pl.multiple_of(up_start + place, 8), piece)],
            down_flat[pl.ds(pl.multiple_of(place, 8), piece)],
        ]
        target[...] = jnp.concatenate(both, axis=0).astype(target.dtype)


def input_grad(grads, down, base, products, fine, target):
    half_rows, half_cols = fine.shape[0] // 2, fine.shape[1] // 2
    count = half_rows + 1
    flat = grads.reshape(count * PAD, grads.shape[2])
    moved = lax.dot(flat, down[...], preferred_element_type=F32)
    products[...] = moved.reshape(count, PAD, 9 * 128)

    def part(p, a, b, offset):
        tap = 3 * a + b
        return products[p, offset : offset + half_cols, tap * 128 : tap * 128 + 128]

    for p in range(half_rows):
        fine[2 * p, pl.ds(0, half_cols, stride=2), :] = part(p, 1, 1, 0)
        fine[2 * p, pl.ds(1, half_cols, stride=2), :] = part(p, 1, 2, 0) + part(p, 1, 0, 1)
        fine[2 * p + 1, pl.ds(0, half_cols, stride=2), :] = part(p, 2, 1, 0) + part(p + 1, 0, 1, 0)
        fine[2 * p + 1, pl.ds(1, half_cols, stride=2), :] = (
            part(p, 2, 2, 0) + part(p, 2, 0, 1) + part(p + 1, 0, 2, 0) + part(p + 1, 0, 0, 1)
        )
    for row in range(fine.shape[0]):
        target[row] = (base(row).astype(F32) + fine[row]).astype(BF16)


def forward_kernel(merged, blocks, *rest):
    ys, rest = (rest[:1], rest[1:]) if merged else (rest[:2], rest[2:])
    in_grad, flat_up, flat_down, near, far, field, even_taps, odd_taps, products, mixed, fine = rest
    ext = blocks if merged else blocks.at[2]
    rows, wide = ext.shape[0], ext.shape[1]
    breadth = wide - 16
    half_rows, half_cols = rows // 2, breadth // 2
    depth = flat_down.shape[0]
    tx, ty = lax.axis_index("tx"), lax.axis_index("ty")
    has_above, has_below = tx > 0, tx < lax.axis_size("tx") - 1
    has_right = ty < lax.axis_size("ty") - 1
    position = lax.axis_index("segment")
    count = half_rows + 2
    field[:, wide:] = jnp.zeros((field.shape[0], field.shape[1] - wide, 128), F32)
    if merged:
        def row_of(k, valid):
            tiles = [ys[0][9 * k + part].astype(F32) for part in range(breadth // 8 + 1)]
            line = jnp.concatenate([tiles[-1]] + tiles, axis=0)
            return jnp.where(valid, line, 0.0)

        before, after = (lambda k: row_of(k, has_above)), (lambda k: row_of(k, has_below))
        top, bottom = 0, 0
    else:
        before, after = rims(*ys)
        top, bottom = 2, 5
    for k in range(3):
        field[k, 0:wide] = before(top + k)
    for row in range(rows):
        field[row + 3, 0:wide] = ext[row].astype(F32)
    for k in range(2):
        field[rows + 3 + k, 0:wide] = after(bottom + k)
    spread_taps(field, even_taps, odd_taps, 2 * count + 1, LEFT - 3)
    pre_down = lower(even_taps, odd_taps, count, flat_down)
    reduced = pre_down / (1.0 + jnp.exp(-pre_down))
    row_id, col_id = places(count, depth)
    inside = ((row_id <= half_rows) | has_below) & ((col_id <= half_cols) | has_right)
    reduced = jnp.where(inside, reduced, 0.0).astype(BF16)
    raised = lax.dot(reduced, flat_up[...], preferred_element_type=F32)
    products[...] = raised.reshape(count, PAD, 9 * 128)

    def tap_rows(p, dy, b):
        at = lambda q, a: products[q, :, (3 * a + b) * 128 : (3 * a + b) * 128 + 128]
        if dy == 0:
            return at(p, 0) + at(p + 1, 1) + at(p + 1, 2)
        return at(p + 1, 0) + at(p + 1, 1) + at(p + 2, 2)

    for p in range(half_rows):
        for dy in range(2):
            col = [tap_rows(p, dy, b) for b in range(3)]
            mixed[0, 0:PAD], mixed[1, 0:PAD] = col[0], col[1] + col[2]
            mixed[2, 0:PAD], mixed[3, 0:PAD] = col[0] + col[1], col[2]
            line = 2 * p + dy
            fine[line, pl.ds(0, half_cols, stride=2), :] = mixed[0, 0:half_cols] + mixed[1, 1 : half_cols + 1]
            fine[line, pl.ds(1, half_cols, stride=2), :] = (
                mixed[2, 1 : half_cols + 1] + mixed[3, 2 : half_cols + 2]
            )
    for row in range(rows):
        value = (ext[row, LEFT : LEFT + breadth].astype(F32) + fine[row]).astype(BF16)
        near[row] = jnp.where(position % 2 == 0, value, in_grad[row])
        far[row] = jnp.where(position < lax.axis_size("segment") // 2, value, in_grad[row])


def swaps(axis):
    size = lax.axis_size(axis)
    pairs = [(i, i + 1) for i in range(0, size - 1, 2)]
    other = [(i, i + 1) for i in range(1, size - 1, 2)]
    both = lambda pairs: pairs + [(j, i) for i, j in pairs]
    return both(pairs), both(other)


def crossed(axis, distance):
    return [(i, i ^ distance) for i in range(lax.axis_size(axis))]


def total_kernel(scaling, own, first, second, third, up_sum, down_sum):
    total = own[...] + first[...].astype(F32) + second[...].astype(F32) + third[...].astype(F32)
    piece = up_sum.shape[0]
    up_sum[...] = total[0:piece] * scaling
    down_sum[...] = total[piece:] * scaling


def shape(dims, kind):
    return jax.ShapeDtypeStruct(tuple(dims), kind)


def local(
    act_in,
    partner_in,
    stashed,
    grad_in,
    down_weights,
    up_weights,
    coarse,
    nest_owner,
    nest_cell,
    land_weight,
):
    height, breadth, channels = act_in.shape[1:]
    depth = down_weights.shape[-1]
    half_rows = height // 2
    n_tx, n_ty = lax.axis_size("tx"), lax.axis_size("ty")
    position, segments = lax.axis_index("segment"), lax.axis_size("segment")
    scaling = 1.0 / math.sqrt(height * breadth * n_tx * n_ty)
    down_taps = jnp.swapaxes(down_weights, 3, 4).reshape(9, depth, channels)
    up_taps = up_weights.reshape(9, depth, channels)

    owners = nest_owner.reshape(-1)
    tile = shape((height, breadth, channels), BF16)
    pay = shape((height + 1 + coarse.shape[0] // 8, 8, channels), BF16)
    merged = n_ty == 4 and n_tx == 2
    if merged:
        st_far = lax.ppermute(stashed, "tx", crossed("tx", 1))
    side = pltpu.VMEM((height, 16, channels), BF16)
    full = pltpu.VMEM((height, breadth, channels), BF16)
    grad_own, z_pay0, z_pay1 = call(
        edge_kernel,
        (tile, pay, pay),
        [HBM] * 8,
        [side] * 4
        + [full] * 2
        + [pltpu.VMEM((height // 4, breadth, channels), F32), pltpu.VMEM(coarse.shape, BF16)]
        + [pltpu.SMEM(scalars.shape, jnp.int32) for scalars in (owners, nest_cell, land_weight)]
        + [pltpu.SemaphoreType.DMA((10,))],
        flops=1000,
        moved=1000,
    )(*in_hbm(owners, nest_cell, land_weight, act_in, partner_in, stashed, grad_in, coarse))
    pairs, others = swaps("ty")
    if merged:
        others = crossed("ty", 3)
        grad_far = lax.ppermute(grad_own, "tx", crossed("tx", 1))
    z0 = lax.ppermute(z_pay0, "ty", pairs)
    z1 = lax.ppermute(z_pay1, "ty", others)
    if merged:
        table_parts = (coarse, lax.ppermute(coarse, "ty", crossed("ty", 2)))
    else:
        table_parts = (lax.all_gather(coarse, "ty", tiled=True),)
    flat = shape((depth, 9 * channels), BF16)
    taps_room = pltpu.VMEM((9, depth, channels), BF16)
    base, stash, flat_up, flat_down = call(
        prepare_kernel,
        (shape((height, breadth, channels), F32), tile, flat, flat),
        [HBM] * 5,
        [full, full, taps_room, taps_room, pltpu.SemaphoreType.DMA((5,))],
        flops=1000,
        moved=1000,
    )(*in_hbm(act_in, partner_in, stashed, up_taps, down_taps))
    operands = (base, z0, z1, *table_parts)
    rooms = [
        pltpu.VMEM((n_ty * coarse.shape[0], channels), F32),
        pltpu.VMEM((height // 4, breadth, channels), F32),
    ]
    pairs, others = swaps("tx")
    if merged:
        rim = call(
            rim_kernel,
            shape((height, 8, channels), BF16),
            [VMEM] * 2 + [pl.BlockSpec(memory_space=pl.ANY)] * 2,
            flops=1000,
            moved=1000,
        )(z0, z1, flat_up, st_far)
        rim_far = lax.ppermute(rim, "tx", pairs)
        pay, blocks = call(
            functools.partial(condition_kernel, True),
            (shape((3 * (breadth // 8 + 1), 8, channels), BF16), shape((height, breadth + 16, channels), BF16)),
            [SMEM] * 2 + [VMEM] * len(operands),
            rooms,
            flops=6_000_000_000,
            moved=1000,
        )(owners, nest_cell, *operands)
        ys = [lax.ppermute(pay, "tx", pairs)]
    else:
        pay = shape((STRIP_ROWS, breadth + 16, channels), BF16)
        *pays, blocks = call(
            functools.partial(condition_kernel, False),
            (pay, pay, shape((3, height, breadth + 16, channels), BF16)),
            [SMEM] * 2 + [VMEM] * (len(operands) + 2),
            rooms,
        )(owners, nest_cell, *operands, stash, grad_own)
        ys = [lax.ppermute(pays[0], "tx", pairs), lax.ppermute(pays[1], "tx", others) if others else pays[1]]

    wide = 2 * PAD + 16
    rows_flat = 9 * depth

    def tap_rooms(count):
        room = pltpu.VMEM((count + 1, PAD, 3 * channels), BF16)
        return [pltpu.VMEM((2 * count + 2, wide, channels), F32), room, room]

    fine = pltpu.VMEM((height, breadth, channels), F32)
    products = lambda count: pltpu.VMEM((count, PAD, 9 * channels), F32)
    if merged:
        piece = rows_flat // (n_tx * n_ty)
        part = shape((2 * piece, channels), BF16)
        flat_half = rows_flat // 2
        in_grad, own_sum, *sends = call(
            paired_kernel,
            (tile, shape((2 * piece, channels), F32), part, part, part),
            [VMEM] * 8,
            tap_rooms(height)
            + [
                pltpu.VMEM((height, PAD, 9 * channels), BF16),
                pltpu.VMEM((9 * channels // 2, 128), F32),
                pltpu.VMEM((9 * channels // 2, 128), F32),
                pltpu.VMEM((5 * depth, channels), F32),
                pltpu.VMEM((flat_half, channels), F32),
                pltpu.VMEM((height + 1, PAD, depth), BF16),
                products(half_rows + 1),
                fine,
            ],
            flops=900_000_000,
            moved=4_000_000,
        )(stash, grad_own, st_far, grad_far, rim, rim_far, flat_up, flat_down)
        arrived = [lax.ppermute(sends[d - 1], "ty", crossed("ty", d)) for d in (3, 2, 1)]
        summed = shape((piece, channels), F32)
        up_sum, down_sum = call(
            functools.partial(total_kernel, scaling), (summed, summed), [VMEM] * 4, flops=10_000_000_000
        )(own_sum, *arrived)
        up_sum, down_sum = up_sum.reshape(1, -1), down_sum.reshape(1, -1)
    else:
        whole = shape((rows_flat, channels), F32)
        in_grad, up_flat, down_flat = call(
            grads_kernel,
            (tile, whole, whole),
            [VMEM] * 5,
            tap_rooms(half_rows + 1)
            + [
                pltpu.VMEM((half_rows + 1, PAD, 9 * channels), BF16),
                pltpu.VMEM((9 * channels, 128), F32),
                pltpu.VMEM((9 * channels, 128), F32),
                products(half_rows + 1),
                fine,
            ],
            flops=500_000_000,
            moved=4_000_000,
        )(blocks, *ys, flat_up, flat_down)
        pooled = lambda flat: lax.psum_scatter(
            flat.reshape(-1) * scaling, ("tx", "ty"), scatter_dimension=0, tiled=True
        )[None]
        down_sum, up_sum = pooled(down_flat), pooled(up_flat)

    count = half_rows + 2
    near, far = call(
        functools.partial(forward_kernel, merged),
        (tile, tile),
        [VMEM] * (4 + len(ys)),
        tap_rooms(count) + [products(count), pltpu.VMEM((4, PAD, channels), F32), fine],
        flops=600_000_000,
        moved=4_000_000,
    )(blocks, *ys, in_grad, flat_up, flat_down)
    from_far = lax.ppermute(far, "segment", [(i, segments - 1 - i) for i in range(segments)])
    from_near = lax.ppermute(near, "segment", crossed("segment", 1))
    blank = jnp.zeros_like(from_near)
    odd = position % 2 == 1
    act_out = jnp.where(position == 0, blank, jnp.where(odd, from_near, from_far))
    grad_out = jnp.where(position == segments - 1, blank, jnp.where(odd, from_far, from_near))
    partner_out = jnp.where(position < segments, from_far, blank)
    return (act_out[None], grad_out[None], partner_out[None], down_sum, up_sum)


def solution(mesh):
    tile = P("segment", "tx", "ty", None)
    weights = P("segment", None, None, None, None)
    grads = P("segment", ("tx", "ty"))
    rows = P(("tx", "ty"))
    return jax.shard_map(
        local,
        mesh=mesh,
        in_specs=(tile,) * 4 + (weights,) * 2 + (P(("tx", "ty"), None),) * 2 + (rows, P("tx", "ty")),
        out_specs=(tile,) * 3 + (grads,) * 2,
        check_vma=False,
    )
```

```python
import functools
import math

import jax
import jax.numpy as jnp
from jax import lax
from jax.experimental import pallas as pl
from jax.experimental.pallas import tpu as pltpu
from jax.sharding import PartitionSpec as P

F32 = jnp.float32
BF16 = jnp.bfloat16
VMEM = pl.BlockSpec(memory_space=pltpu.VMEM)
SMEM = pl.BlockSpec(memory_space=pltpu.SMEM)
HBM = pl.BlockSpec(memory_space=pltpu.HBM)
LEFT = 8
PAD = 48
STRIP_ROWS = 7


def call(body, out_shape, in_specs, scratch=(), flops=0, moved=0, limit=24, out_specs=None, aliases=()):
    out_specs = out_specs or jax.tree.map(lambda _: VMEM, out_shape)
    return pl.pallas_call(
        body,
        out_shape=out_shape,
        in_specs=in_specs,
        out_specs=out_specs,
        scratch_shapes=list(scratch),
        input_output_aliases=dict(aliases),
        compiler_params=pltpu.CompilerParams(vmem_limit_bytes=limit * 1024 * 1024),
        cost_estimate=pl.CostEstimate(flops=flops, bytes_accessed=moved, transcendentals=0),
    )


def passed_on(arrays, flops, after=()):
    here = [pl.BlockSpec(memory_space=pl.ANY)] * len(arrays)
    return list(call(
        lambda *refs: None,
        tuple(jax.ShapeDtypeStruct(x.shape, x.dtype) for x in arrays),
        here + [pl.BlockSpec(memory_space=pl.ANY)] * len(after),
        flops=flops,
        moved=1000,
        out_specs=tuple(here),
        aliases=[(k, k) for k in range(len(arrays))],
    )(*arrays, *after))


def in_hbm(*operands):
    return [pltpu.with_memory_space_constraint(x, pltpu.HBM) for x in operands]


def sublane(shape):
    return lax.broadcasted_iota(jnp.int32, shape, len(shape) - 2)


def flag(condition):
    return jnp.where(condition, 1.0, 0.0).astype(F32)


def traits():
    segments = lax.axis_size("segment")
    position = lax.axis_index("segment")
    decoder = flag(position >= segments // 2)
    return decoder, 1.0 - decoder, position == segments - 1


def edge_kernel(owner_in, cell_in, land_in, act, par, st, gr, coarse, grad_out, pay0, pay1, *scratch):
    act_l, act_r, st_l, st_r, par_v, gr_v, plane, held_v, owner, cell, land, arrived = scratch
    rows, breadth = gr.shape[1], gr.shape[2]
    first, final = pl.ds(0, 16), pl.ds(breadth - 16, 16)
    copies = [
        pltpu.make_async_copy(source, target, arrived.at[k])
        for k, (source, target) in enumerate(
            (
                (gr.at[0], gr_v),
                (par.at[0], par_v),
                (act.at[0, :, first], act_l),
                (act.at[0, :, final], act_r),
                (st.at[0, :, first], st_l),
                (st.at[0, :, final], st_r),
                (coarse, held_v),
                (owner_in, owner),
                (cell_in, cell),
                (land_in, land),
            )
        )
    ]
    for copy in copies:
        copy.start()
    for copy in copies[7:]:
        copy.wait()
    decoder, encoder, last = traits()
    groups = rows // 4
    per_row = breadth // 4
    low = sublane((8, 128)) < 4
    for group in range(groups):
        for part in range(breadth // 8):
            weigh = [jnp.where(last, land[group, 2 * part + k], 1).astype(F32) for k in range(2)]
            plane[group, 8 * part : 8 * part + 8] = jnp.where(low, weigh[0], weigh[1])

    def ids(column):
        tile = jnp.zeros((8, 128), F32)
        where = sublane((8, 128))
        for row in range(groups):
            spot = row * per_row + column
            tile = jnp.where(where == row, owner[spot].astype(F32), tile)
            tile = jnp.where(where == 4 + row, cell[spot].astype(F32), tile)
        return tile

    left_ids, right_ids = ids(0), ids(per_row - 1)
    for copy in copies[:7]:
        copy.wait()
    for row in range(rows):
        grad = gr_v[row].astype(F32) + encoder * par_v[row].astype(F32)
        grad_out[row] = (grad * plane[row // 4]).astype(BF16)

    where = sublane((rows, 8, 128))
    begin, end = slice(0, 16), slice(breadth - 16, breadth)
    grad = grad_out[:, begin].astype(F32)[:, 0:8]
    stash = st_l[...].astype(F32)[:, 0:8]
    block = act_l[...].astype(F32)[:, 0:8] + decoder * par_v[:, begin].astype(F32)[:, 0:8]
    after = jnp.where(
        where < 3, grad, jnp.where(where < 5, pltpu.roll(stash, 3, 1), pltpu.roll(block, 5, 1))
    )
    grad = grad_out[:, end].astype(F32)[:, 8:16]
    stash = st_r[...].astype(F32)[:, 8:16]
    block = act_r[...].astype(F32)[:, 8:16] + decoder * par_v[:, end].astype(F32)[:, 8:16]
    before = jnp.where(
        where == 7, grad, jnp.where(where == 6, pltpu.roll(stash, 7, 1), pltpu.roll(block, 6, 1))
    )
    even = lax.axis_index("ty") % 2 == 0
    strips = jnp.where(even, before, after).astype(BF16), jnp.where(even, after, before).astype(BF16)
    named = jnp.where(even, right_ids, left_ids), jnp.where(even, left_ids, right_ids)
    held = held_v[...].reshape(coarse.shape[0] // 8, 8, 128)
    for k, pay in enumerate((pay0, pay1)):
        pay[0:rows] = strips[k]
        pay[rows] = named[k].astype(BF16)
        pay[rows + 1 :] = held


def prepare_kernel(act, par, st, up, down, base, stash, flat_up, flat_down, *scratch):
    act_v, par_v, up_v, down_v, arrived = scratch
    pairs = (act.at[0], act_v), (par.at[0], par_v), (up, up_v), (down, down_v), (st.at[0], stash)
    copies = [pltpu.make_async_copy(*pair, arrived.at[k]) for k, pair in enumerate(pairs)]
    for copy in copies:
        copy.start()
    decoder, _, _ = traits()
    for copy in copies:
        copy.wait()
    for row in range(act_v.shape[0]):
        base[row] = act_v[row].astype(F32) + decoder * par_v[row].astype(F32)
    lane_taps(up_v, flat_up)
    lane_taps(down_v, flat_down)


def side_rims(z0, z1, rows):
    ty = lax.axis_index("ty")
    even = ty % 2 == 0
    first, second = z0[0:rows].astype(F32), z1[0:rows].astype(F32)
    before = jnp.where(ty > 0, jnp.where(even, second, first), 0.0)
    after = jnp.where(ty < lax.axis_size("ty") - 1, jnp.where(even, first, second), 0.0)
    return before, after


def rim_kernel(z0, z1, _weights, _stash, rim):
    before, after = side_rims(z0, z1, rim.shape[0])
    rim[...] = jnp.where(sublane(rim.shape) < 5, after, before).astype(BF16)


def condition_kernel(merged, owner, cell, base, z0, z1, coarse, *rest):
    rows, breadth = base.shape[0], base.shape[1]
    groups = rows // 4
    per_row = breadth // 4
    cells = groups * per_row
    wide = LEFT + breadth
    ty = lax.axis_index("ty")
    low = sublane((8, 128)) < 4
    if merged:
        z2, pay, ext, table, plane = rest
        table[pl.ds(pl.multiple_of(ty * cells, 8), cells)] = coarse[...].astype(F32)
        others = (
            (ty ^ 1, z0[rows + 1 :].astype(F32).reshape(cells, 128)),
            (ty ^ 3, z1[rows + 1 :].astype(F32).reshape(cells, 128)),
            (ty ^ 2, z2[...].astype(F32)),
        )
        for other, value in others:
            table[pl.ds(pl.multiple_of(other * cells, 8), cells)] = value
    else:
        st, grad_own, pay, pay1, full, table, plane = rest
        ext = full.at[2]
        table[...] = coarse[...].astype(F32)
    before, after = side_rims(z0, z1, rows + 1)

    def rim_condition(tile, valid):
        wanted = tile[rows]
        spot = wanted * cells + pltpu.roll(wanted, 4, 0)
        lanes = lax.broadcasted_iota(jnp.int32, (8, table.shape[0]), 1).astype(F32)
        spread = jnp.broadcast_to(spot[:, 0:1], lanes.shape)
        hot = jnp.where(spread == lanes, 1.0, 0.0).astype(BF16)
        named = lax.dot(hot, table[...].astype(BF16), preferred_element_type=F32)
        picked = [jnp.broadcast_to(named[row : row + 1], (8, 128))[None] for row in range(groups)]
        spread_rows = jnp.concatenate([p for p in picked for _ in range(4)], axis=0)
        return jnp.where(valid, spread_rows, 0.0)

    rim = pltpu.roll(before[0:rows], 2, 1) + rim_condition(before, ty > 0)
    ext[:, 0:8] = rim.astype(BF16)
    rim = pltpu.roll(after[0:rows], 3, 1) + rim_condition(after, ty < lax.axis_size("ty") - 1)
    ext[:, wide : wide + 8] = rim.astype(BF16)
    for group in range(groups):
        for part in range(breadth // 8):
            spots = [group * per_row + 2 * part + k for k in range(2)]
            named = [
                jnp.broadcast_to(table[pl.ds(owner[s] * cells + cell[s], 1)], (8, 128)) for s in spots
            ]
            plane[group, 8 * part : 8 * part + 8] = jnp.where(low, named[0], named[1])
    for row in range(rows):
        ext[row, LEFT:wide] = (base[row] + plane[row // 4]).astype(BF16)

    upper = lax.axis_index("tx") % 2 == 0
    if merged:
        near = sublane((8, 128)) < 5
        for k in range(3):
            top, bottom = min(k, 1), rows - 3 + k
            for part in range(breadth // 8):
                cols = pl.ds(LEFT + 8 * part, 8)
                pay[9 * k + part] = jnp.where(upper, ext[bottom, cols], ext[top, cols])
            tiles = [
                jnp.where(near, ext[row, pl.ds(wide, 8)], ext[row, pl.ds(0, 8)]) for row in (top, bottom)
            ]
            pay[9 * k + breadth // 8] = jnp.where(upper, tiles[1], tiles[0])
        return
    full[0, :, 0:8] = before[0:rows].astype(BF16)
    full[1, :, 0:8] = pltpu.roll(before[0:rows], 1, 1).astype(BF16)
    full[0, :, wide : wide + 8] = after[0:rows].astype(BF16)
    full[1, :, wide : wide + 8] = pltpu.roll(after[0:rows], 5, 1).astype(BF16)
    full[0, :, LEFT:wide] = grad_own[...]
    full[1, :, LEFT:wide] = st[...]
    leading = [(0, 0), (0, 1), (0, 2), (1, 0), (1, 1), (2, 0), (2, 1)]
    closing = [(0, rows - 1), (1, rows - 1), (2, rows - 3), (2, rows - 2), (2, rows - 1)]
    closing = closing + closing[-1:] * 2
    for k in range(STRIP_ROWS):
        top, bottom = full[leading[k]], full[closing[k]]
        pay[k] = jnp.where(upper, bottom, top)
        pay1[k] = jnp.where(upper, top, bottom)


def rims(y0, y1):
    tx = lax.axis_index("tx")
    upper = tx % 2 == 0
    before_ok, after_ok = tx > 0, tx < lax.axis_size("tx") - 1

    def row(valid, from_first, k):
        value = jnp.where(from_first, y0[k].astype(F32), y1[k].astype(F32))
        return jnp.where(valid, value, 0.0)

    before = lambda k: row(before_ok, jnp.logical_not(upper), k)
    after = lambda k: row(after_ok, upper, k)
    return before, after


def spread_taps(field, taps, odd_taps, count, first):
    width = taps.shape[1]
    for row in range(count):
        target = taps if row % 2 == 0 else odd_taps
        for tap in range(3):
            value = field[row, pl.ds(first + tap, width, stride=2), :]
            target[row // 2, :, tap * 128 : tap * 128 + 128] = value.astype(BF16)


def three_rows(even_taps, odd_taps, count):
    wide = 3 * 128
    whole = lambda ref, a: ref[a : a + count].reshape(count * ref.shape[1], wide)
    return whole(even_taps, 0), whole(odd_taps, 0), whole(even_taps, 1)


def lower(even_taps, odd_taps, count, down):
    views = three_rows(even_taps, odd_taps, count)
    wide = 3 * 128
    total = None
    for a in range(3):
        term = lax.dot_general(
            views[a],
            down[:, a * wide : a * wide + wide],
            (((1,), (1,)), ((), ())),
            preferred_element_type=F32,
        )
        total = term if total is None else total + term
    return total


def lane_taps(taps, flat):
    for tap in range(9):
        flat[:, tap * 128 : tap * 128 + 128] = taps[tap]


def window_sums(plane_of, count, sums):
    previous = None
    for row in range(2 * count + 2):
        plane = [plane_of(row, k) for k in range(4)]
        current = [plane[2] + plane[3], plane[1] + plane[2], plane[0] + plane[1]]
        if row > 0:
            for a in range(3):
                double = row - 3 + a
                if double % 2 == 0 and 0 <= double // 2 < count:
                    for b in range(3):
                        lanes = slice((3 * a + b) * 128, (3 * a + b) * 128 + 128)
                        sums[double // 2, :, lanes] = (previous[b] + current[b]).astype(sums.dtype)
        previous = current


def sweep(wide, field, even_taps, odd_taps, sums, flat_up, down, count, fill_stash, fill_grad):
    field[:, wide:] = jnp.zeros((field.shape[0], field.shape[1] - wide, 128), F32)
    fill_stash()
    spread_taps(field, even_taps, odd_taps, 2 * count + 1, LEFT - 1)
    pre_back = lower(even_taps, odd_taps, count, down)
    logistic = 0.5 + 0.5 * jnp.tanh(0.5 * pre_back)
    reduced = pre_back * logistic
    slope = logistic * (1.0 + pre_back * (1.0 - logistic))
    fill_grad()
    window_sums(lambda row, k: field[row, pl.ds(LEFT - 1 + k, PAD, stride=2), :], count, sums)
    windows = sums[...].reshape(count * PAD, 9 * 128)
    raised = lax.dot_general(windows, flat_up[...], (((1,), (1,)), ((), ())), preferred_element_type=F32)
    return reduced.astype(BF16), raised * slope


def places(count, depth):
    shape = (count, PAD, depth)
    row = lax.broadcasted_iota(jnp.int32, shape, 0).reshape(count * PAD, depth)
    col = lax.broadcasted_iota(jnp.int32, shape, 1).reshape(count * PAD, depth)
    return row, col


def flatten_rows(d0, d1, flat, start):
    pairs = d0.shape[0] // 2
    left_even, left_odd = d0[pl.ds(0, pairs, stride=2)], d0[pl.ds(1, pairs, stride=2)]
    right_even, right_odd = d1[pl.ds(0, pairs, stride=2)], d1[pl.ds(1, pairs, stride=2)]
    near = lax.broadcasted_iota(jnp.int32, left_even.shape, 1) < 64
    turned = pltpu.roll(left_odd, 64, 1)
    flat[pl.ds(start, pairs, stride=3)] = left_even
    flat[pl.ds(start + 1, pairs, stride=3)] = jnp.where(near, right_even, turned)
    flat[pl.ds(start + 2, pairs, stride=3)] = jnp.where(near, turned, pltpu.roll(right_odd, 64, 1))


def across(left, right):
    return lax.dot_general(left, right, (((0,), (0,)), ((), ())), preferred_element_type=F32)


def grads_kernel(
    ext, y0, y1, flat_up, flat_down, in_grad, up_flat, down_flat, field, even_taps, odd_taps, sums, d0, d1, products, fine
):
    rows = ext.shape[1]
    wide = ext.shape[2]
    half_rows, half_cols = rows // 2, (wide - 16) // 2
    count = half_rows + 1
    before, after = rims(y0, y1)
    tx, ty = lax.axis_index("tx"), lax.axis_index("ty")
    has_below, has_right = tx < lax.axis_size("tx") - 1, ty < lax.axis_size("ty") - 1

    def fill(kind, top, bottom):
        field[0, 0:wide] = before(top)
        for row in range(rows):
            field[row + 1, 0:wide] = ext[kind, row].astype(F32)
        for k, spot in enumerate(bottom):
            field[rows + 1 + k, 0:wide] = after(spot)

    reduced, pre_grad = sweep(
        wide,
        field,
        even_taps,
        odd_taps,
        sums,
        flat_up,
        flat_down,
        count,
        lambda: fill(1, 1, (3, 4)),
        lambda: fill(0, 0, (0, 1, 2)),
    )
    depth = reduced.shape[1]
    row, col = places(count, depth)
    inside = ((row < half_rows) | has_below) & ((col < half_cols) | (has_right & (col == half_cols)))
    pre_grad = jnp.where(inside, pre_grad, 0.0).astype(BF16).reshape(count, PAD, depth)
    base = lambda row_id: ext[0, row_id, LEFT : wide - 8]
    moved = lax.dot(pre_grad.reshape(count * PAD, depth), flat_down[...], preferred_element_type=F32)
    products[...] = moved.reshape(count, PAD, 9 * 128)
    combine_fine(products, base, fine, in_grad)
    cells = half_rows * half_cols
    own = lambda value: value[:half_rows, :half_cols].reshape(cells, value.shape[-1])
    reduced, own_grad = own(reduced.reshape(count, PAD, depth)), own(pre_grad)
    terms = across(reduced, own(sums))
    for tap in range(9):
        up_flat[tap * depth : tap * depth + depth] = terms[:, tap * 128 : tap * 128 + 128]
    span = 3 * 128
    for a, view in enumerate((even_taps, odd_taps, even_taps)):
        taps = view[a // 2 : a // 2 + half_rows, 0:half_cols].reshape(cells, span)
        term = across(taps, own_grad)
        d0[a * span : a * span + span] = term[:, 0:128]
        d1[a * span : a * span + span, 0:64] = term[:, 128:192]
    flatten_rows(d0, d1, down_flat, 0)


def paired_kernel(
    st, grad, st_far, grad_far, rim, rim_far, flat_up, flat_down, value, far, in_grad, *rest
):
    own_sum, send1, send2, send3, field, even_taps, odd_taps, sums, d0, d1, up_flat, down_flat = rest[:12]
    grads, products, fine, edge_taps, edge_sums = rest[12:]
    rows, breadth = grad.shape[0], grad.shape[1]
    wide = breadth + 16
    count, half_rows, half_cols = rows, rows // 2, breadth // 2
    cells = count * half_cols
    edge_count = half_rows + 1
    tx, ty = lax.axis_index("tx"), lax.axis_index("ty")
    has_below = tx < lax.axis_size("tx") - 1
    has_right = ty < lax.axis_size("ty") - 1
    first_row = rows * tx

    def fill(here_rows, there_rows, turn_before, turn_after):
        blank = jnp.zeros((wide, 128), F32)
        field[0, 0:wide] = blank
        field[2 * rows + 1, 0:wide] = blank
        here, there = 1 + rows * tx, 1 + rows * (1 - tx)
        for start, source, sides in ((here, here_rows, rim), (there, there_rows, rim_far)):
            for row in range(rows):
                field[start + row, LEFT : LEFT + breadth] = source(row).astype(F32)
            sides = sides[...].astype(F32)
            turned = lambda turn: pltpu.roll(sides, turn, 1) if turn else sides
            field[pl.ds(start, rows), 0:8] = turned(turn_before)
            field[pl.ds(start, rows), LEFT + breadth : wide] = turned(turn_after)

    def slopes(pre_back):
        logistic = 0.5 + 0.5 * jnp.tanh(0.5 * pre_back)
        return logistic, logistic * (1.0 + pre_back * (1.0 - logistic))

    def full_taps(values, weights):
        return lax.dot_general(values, weights[...], (((1,), (1,)), ((), ())), preferred_element_type=F32)

    edge = lambda row, k: field[first_row + row, pl.ds(LEFT - 1 + k + breadth, 8, stride=2), :]
    flat_edge = lambda ref: ref[...].reshape(edge_count * 8, 9 * 128).astype(BF16)

    field[:, wide:] = jnp.zeros((field.shape[0], field.shape[1] - wide, 128), F32)
    fill(lambda row: st[row], lambda row: st_far[0, row], 1, 5)
    spread_taps(field, even_taps, odd_taps, 2 * count + 1, LEFT - 1)
    for p in range(edge_count):
        for tap in range(9):
            edge_taps[p, :, tap * 128 : tap * 128 + 128] = edge(2 * p + tap // 3, tap % 3)
    pre_back = lower(even_taps, odd_taps, count, flat_down)
    logistic, slope = slopes(pre_back)
    reduced = (pre_back * logistic).astype(BF16)
    edge_slope = slopes(full_taps(flat_edge(edge_taps), flat_down))[1]

    fill(lambda row: grad[row], lambda row: grad_far[row], 0, 0)
    window_sums(lambda row, k: field[row, pl.ds(LEFT - 1 + k, half_cols, stride=2), :], count, sums)
    window_sums(edge, edge_count, edge_sums)
    depth = reduced.shape[1]
    coupled = (full_taps(sums[...].reshape(cells, 9 * 128), flat_up) * slope).astype(BF16)
    edge_shape = (edge_count, 8, depth)
    row = lax.broadcasted_iota(jnp.int32, edge_shape, 0).reshape(edge_count * 8, depth)
    inside = has_right & ((row < half_rows) | has_below)
    edge_grad = jnp.where(inside, full_taps(flat_edge(edge_sums), flat_up) * edge_slope, 0.0).astype(BF16)
    grads[0:count] = coupled.reshape(count, half_cols, depth)
    grads[count] = jnp.zeros((half_cols, depth), BF16)
    own_rows = grads[pl.ds(half_rows * tx, edge_count)].reshape(edge_count * half_cols, depth)
    moved = lax.dot(own_rows, flat_down[...], preferred_element_type=F32)
    products[:, 0:half_cols] = moved.reshape(edge_count, half_cols, 9 * 128)
    moved = lax.dot(edge_grad, flat_down[...], preferred_element_type=F32)
    products[:, half_cols:] = moved.reshape(edge_count, 8, 9 * 128)
    combine_fine(products, lambda row: grad[row], fine, in_grad)
    for row in range(rows):
        far[row] = relay_choices(value[row], in_grad[row])[1]
    half = up_flat.shape[0] - depth // 2
    lanes = pl.ds(pl.multiple_of(tx * 512, 128), 640)
    terms = across(reduced, sums[:, :, lanes].reshape(cells, 640))
    for tap in range(5):
        up_flat[tap * depth : tap * depth + depth] = terms[:, tap * 128 : tap * 128 + 128]
    span = 3 * 128
    outer = across(even_taps[pl.ds(tx, count)].reshape(cells, span), coupled)
    middle = across(odd_taps[0:count].reshape(cells, span), coupled)
    outer_at = pl.multiple_of(tx * (span // 2), 8)
    middle_at = pl.multiple_of((1 - tx) * span, 8)
    middle_half = jnp.where(tx == 0, middle[0 : span // 2], middle[span // 2 : span])
    d0[pl.ds(outer_at, span)] = outer[:, 0:128]
    d1[pl.ds(outer_at, span), 0:64] = outer[:, 128:192]
    d0[pl.ds(middle_at, span // 2)] = middle_half[:, 0:128]
    d1[pl.ds(middle_at, span // 2), 0:64] = middle_half[:, 128:192]
    flatten_rows(d0, d1, down_flat, 0)
    piece = half // 4
    up_start = tx * (depth // 2)
    for distance, target in enumerate((own_sum, send1, send2, send3)):
        place = (ty ^ distance) * piece
        both = [
            up_flat[pl.ds(pl.multiple_of(up_start + place, 8), piece)],
            down_flat[pl.ds(pl.multiple_of(place, 8), piece)],
        ]
        target[...] = jnp.concatenate(both, axis=0).astype(target.dtype)


def combine_fine(products, base, fine, target):
    half_rows, half_cols = fine.shape[0] // 2, fine.shape[1] // 2

    def part(p, a, b, offset):
        tap = 3 * a + b
        return products[p, offset : offset + half_cols, tap * 128 : tap * 128 + 128]

    for p in range(half_rows):
        fine[2 * p, pl.ds(0, half_cols, stride=2), :] = part(p, 1, 1, 0)
        fine[2 * p, pl.ds(1, half_cols, stride=2), :] = part(p, 1, 2, 0) + part(p, 1, 0, 1)
        fine[2 * p + 1, pl.ds(0, half_cols, stride=2), :] = part(p, 2, 1, 0) + part(p + 1, 0, 1, 0)
        fine[2 * p + 1, pl.ds(1, half_cols, stride=2), :] = (
            part(p, 2, 2, 0) + part(p, 2, 0, 1) + part(p + 1, 0, 2, 0) + part(p + 1, 0, 0, 1)
        )
    for row in range(fine.shape[0]):
        target[row] = (base(row).astype(F32) + fine[row]).astype(BF16)


def raise_rows(field, even_taps, odd_taps, products, flat_up, flat_down, count, first, valid):
    spread_taps(field, even_taps, odd_taps, 2 * count + 1, first)
    pre_down = lower(even_taps, odd_taps, count, flat_down)
    reduced = pre_down * (0.5 + 0.5 * jnp.tanh(0.5 * pre_down))
    row, col = places(count, reduced.shape[1])
    reduced = jnp.where(valid(row, col), reduced, 0.0).astype(BF16)
    raised = lax.dot(reduced, flat_up[...], preferred_element_type=F32)
    products[...] = raised.reshape(count, PAD, 9 * 128)


def fine_row(products, mixed, target, picks):
    half_cols = target.shape[0] // 2
    col = []
    for b in range(3):
        terms = [
            products[q, :, (3 * a + b) * 128 : (3 * a + b) * 128 + 128]
            for a, q in enumerate(picks)
            if q is not None
        ]
        col.append(sum(terms[1:], terms[0]))
    mixed[0], mixed[1] = col[0], col[1] + col[2]
    mixed[2], mixed[3] = col[0] + col[1], col[2]
    target[pl.ds(0, half_cols, stride=2), :] = mixed[0, 0:half_cols] + mixed[1, 1 : half_cols + 1]
    target[pl.ds(1, half_cols, stride=2), :] = mixed[2, 1 : half_cols + 1] + mixed[3, 2 : half_cols + 2]


def right_edge(half_cols):
    has_right = lax.axis_index("ty") < lax.axis_size("ty") - 1
    return lambda row, col: (col <= half_cols) | has_right


def relay_choices(value, in_grad):
    position, segments = lax.axis_index("segment"), lax.axis_size("segment")
    near = jnp.where(position % 2 == 0, value, in_grad)
    return near, jnp.where(position < segments // 2, value, in_grad)


def forward_kernel(blocks, y0, y1, in_grad, flat_up, flat_down, near, far, *scratch):
    field, even_taps, odd_taps, products, mixed, fine = scratch
    rows, wide = blocks.shape[1], blocks.shape[2]
    breadth = wide - 16
    half_rows, half_cols = rows // 2, breadth // 2
    has_below = lax.axis_index("tx") < lax.axis_size("tx") - 1
    before, after = rims(y0, y1)
    field[:, wide:] = jnp.zeros((field.shape[0], field.shape[1] - wide, 128), F32)
    for k in range(3):
        field[k, 0:wide] = before(2 + k)
    for row in range(rows):
        field[row + 3, 0:wide] = blocks[2, row].astype(F32)
    for k in range(2):
        field[rows + 3 + k, 0:wide] = after(5 + k)
    edge = right_edge(half_cols)
    valid = lambda row, col: ((row <= half_rows) | has_below) & edge(row, col)
    raise_rows(field, even_taps, odd_taps, products, flat_up, flat_down, half_rows + 2, LEFT - 3, valid)
    for p in range(half_rows):
        fine_row(products, mixed, fine.at[2 * p], (p, p + 1, p + 1))
        fine_row(products, mixed, fine.at[2 * p + 1], (p + 1, p + 1, p + 2))
    for row in range(rows):
        value = (blocks[2, row, LEFT : LEFT + breadth].astype(F32) + fine[row]).astype(BF16)
        near[row], far[row] = relay_choices(value, in_grad[row])


def inner_kernel(blocks, flat_up, flat_down, value, *scratch):
    field, even_taps, odd_taps, products, mixed, fine = scratch
    rows, wide = blocks.shape[0], blocks.shape[1]
    breadth = wide - 16
    half_rows, half_cols = rows // 2, breadth // 2
    field[:, wide:] = jnp.zeros((field.shape[0], field.shape[1] - wide, 128), F32)
    field[0, 0:wide] = jnp.zeros((wide, 128), F32)
    for row in range(rows):
        field[row + 1, 0:wide] = blocks[row].astype(F32)
    edge = right_edge(half_cols)
    raise_rows(field, even_taps, odd_taps, products, flat_up, flat_down, half_rows, LEFT - 3, edge)
    for p in range(half_rows):
        fine_row(products, mixed, fine.at[2 * p], (p - 1 if p else None, p, p))
        below = p + 1 if p + 1 < half_rows else None
        fine_row(products, mixed, fine.at[2 * p + 1], (p, p, below))
    for row in range(rows):
        value[row] = (blocks[row, LEFT : LEFT + breadth].astype(F32) + fine[row]).astype(BF16)


def border_kernel(blocks, y0, value, in_grad, flat_up, flat_down, near, strip, *scratch):
    field, even_taps, odd_taps, products, mixed, fine = scratch
    rows, wide = blocks.shape[0], blocks.shape[1]
    breadth = wide - 16
    half_cols = breadth // 2
    upper = lax.axis_index("tx") == 0
    field[:, wide:] = jnp.zeros((field.shape[0], field.shape[1] - wide, 128), F32)

    def far_row(k):
        tiles = [y0[(breadth // 8 + 1) * k + part].astype(F32) for part in range(breadth // 8 + 1)]
        return jnp.concatenate([tiles[-1]] + tiles, axis=0)

    own = lambda row: blocks[row].astype(F32)
    for k in range(7):
        lower_tile = far_row(k) if k < 3 else own(k - 3)
        upper_tile = own(rows - 5 + k) if k < 5 else far_row(k - 5)
        field[k, 0:wide] = jnp.where(upper, upper_tile, lower_tile)
    edge = right_edge(half_cols)
    raise_rows(field, even_taps, odd_taps, products, flat_up, flat_down, 3, LEFT - 3, edge)
    fine_row(products, mixed, fine.at[0], (0, 1, 1))
    fine_row(products, mixed, fine.at[1], (1, 1, 2))
    fine_row(products, mixed, fine.at[2], (1, 2, 2))
    repaired = [None] * 3
    for k in range(3):
        base = jnp.where(upper, own(rows - 3 + k), own(k))[LEFT : LEFT + breadth]
        added = jnp.where(upper, fine[max(k - 1, 0)], fine[k])
        repaired[k] = (base + added).astype(BF16)
        if k == 0:
            repaired[k] = jnp.where(upper, value[rows - 3], repaired[k])
        strip[k] = relay_choices(repaired[k], jnp.where(upper, in_grad[rows - 3 + k], in_grad[k]))[1]
    for row in range(rows):
        result = value[row]
        if row < 3:
            result = jnp.where(upper, result, repaired[row])
        if row >= rows - 3:
            result = jnp.where(upper, repaired[row - (rows - 3)], result)
        near[row] = relay_choices(result, in_grad[row])[0]


def final_kernel(
    scaling, near, far, strip, own, first, second, third, act_out, grad_out, partner_out, up_sum, down_sum
):
    rows = near.shape[0]
    position, segments = lax.axis_index("segment"), lax.axis_size("segment")
    upper = lax.axis_index("tx") == 0
    odd = position % 2 == 1
    for row in range(rows):
        from_far = far[row]
        if row < 3:
            from_far = jnp.where(upper, from_far, strip[row])
        if row >= rows - 3:
            from_far = jnp.where(upper, strip[row - (rows - 3)], from_far)
        blank = jnp.zeros_like(from_far)
        partner_out[0, row] = from_far
        act_out[0, row] = jnp.where(position == 0, blank, jnp.where(odd, near[row], from_far))
        grad_out[0, row] = jnp.where(position == segments - 1, blank, jnp.where(odd, from_far, near[row]))
    total = own[...] + first[...].astype(F32) + second[...].astype(F32) + third[...].astype(F32)
    piece = up_sum.shape[0]
    up_sum[...] = total[0:piece] * scaling
    down_sum[...] = total[piece:] * scaling


def swaps(axis):
    size = lax.axis_size(axis)
    pairs = [(i, i + 1) for i in range(0, size - 1, 2)]
    other = [(i, i + 1) for i in range(1, size - 1, 2)]
    both = lambda pairs: pairs + [(j, i) for i, j in pairs]
    return both(pairs), both(other)


def crossed(axis, distance):
    return [(i, i ^ distance) for i in range(lax.axis_size(axis))]


def shape(dims, kind):
    return jax.ShapeDtypeStruct(tuple(dims), kind)


def local(
    act_in,
    partner_in,
    stashed,
    grad_in,
    down_weights,
    up_weights,
    coarse,
    nest_owner,
    nest_cell,
    land_weight,
):
    height, breadth, channels = act_in.shape[1:]
    depth = down_weights.shape[-1]
    half_rows = height // 2
    n_tx, n_ty = lax.axis_size("tx"), lax.axis_size("ty")
    position, segments = lax.axis_index("segment"), lax.axis_size("segment")
    scaling = 1.0 / math.sqrt(height * breadth * n_tx * n_ty)
    down_taps = jnp.swapaxes(down_weights, 3, 4).reshape(9, depth, channels)
    up_taps = up_weights.reshape(9, depth, channels)

    owners = nest_owner.reshape(-1)
    tile = shape((height, breadth, channels), BF16)
    pay = shape((height + 1 + coarse.shape[0] // 8, 8, channels), BF16)
    merged = n_ty == 4 and n_tx == 2
    if merged:
        st_far = lax.ppermute(stashed, "tx", crossed("tx", 1))
    side = pltpu.VMEM((height, 16, channels), BF16)
    full = pltpu.VMEM((height, breadth, channels), BF16)
    grad_own, z_pay0, z_pay1 = call(
        edge_kernel,
        (tile, pay, pay),
        [HBM] * 8,
        [side] * 4
        + [full] * 2
        + [pltpu.VMEM((height // 4, breadth, channels), F32), pltpu.VMEM(coarse.shape, BF16)]
        + [pltpu.SMEM(scalars.shape, jnp.int32) for scalars in (owners, nest_cell, land_weight)]
        + [pltpu.SemaphoreType.DMA((10,))],
        flops=1000,
        moved=1000,
    )(*in_hbm(owners, nest_cell, land_weight, act_in, partner_in, stashed, grad_in, coarse))
    pairs, others = swaps("ty")
    if merged:
        others = crossed("ty", 3)
        grad_far = lax.ppermute(grad_own, "tx", crossed("tx", 1))
    z0 = lax.ppermute(z_pay0, "ty", pairs)
    z1 = lax.ppermute(z_pay1, "ty", others)
    if merged:
        table_parts = (coarse, lax.ppermute(coarse, "ty", crossed("ty", 2)))
    else:
        table_parts = (lax.all_gather(coarse, "ty", tiled=True),)
    flat = shape((depth, 9 * channels), BF16)
    taps_room = pltpu.VMEM((9, depth, channels), BF16)
    base, stash, flat_up, flat_down = call(
        prepare_kernel,
        (shape((height, breadth, channels), F32), tile, flat, flat),
        [HBM] * 5,
        [full, full, taps_room, taps_room, pltpu.SemaphoreType.DMA((5,))],
        flops=1000,
        moved=1000,
    )(*in_hbm(act_in, partner_in, stashed, up_taps, down_taps))
    operands = (base, z0, z1, *table_parts)
    rooms = [
        pltpu.VMEM((n_ty * coarse.shape[0], channels), F32),
        pltpu.VMEM((height // 4, breadth, channels), F32),
    ]
    pairs, others = swaps("tx")
    if merged:
        rim = call(
            rim_kernel,
            shape((height, 8, channels), BF16),
            [VMEM] * 2 + [pl.BlockSpec(memory_space=pl.ANY)] * 2,
            flops=1000,
            moved=1000,
        )(z0, z1, flat_up, st_far)
        rim_far = lax.ppermute(rim, "tx", pairs)
        pay, blocks = call(
            functools.partial(condition_kernel, True),
            (shape((3 * (breadth // 8 + 1), 8, channels), BF16), shape((height, breadth + 16, channels), BF16)),
            [SMEM] * 2 + [VMEM] * len(operands),
            rooms,
            flops=2_000_000_000,
            moved=1000,
        )(owners, nest_cell, *operands)
        ys = [lax.ppermute(pay, "tx", pairs)]
    else:
        pay = shape((STRIP_ROWS, breadth + 16, channels), BF16)
        *pays, blocks = call(
            functools.partial(condition_kernel, False),
            (pay, pay, shape((3, height, breadth + 16, channels), BF16)),
            [SMEM] * 2 + [VMEM] * (len(operands) + 2),
            rooms,
        )(owners, nest_cell, *operands, stash, grad_own)
        ys = [lax.ppermute(pays[0], "tx", pairs), lax.ppermute(pays[1], "tx", others) if others else pays[1]]

    wide = 2 * PAD + 16
    rows_flat = 9 * depth

    def tap_rooms(count):
        room = pltpu.VMEM((count + 1, PAD, 3 * channels), BF16)
        return [pltpu.VMEM((2 * count + 2, wide, channels), F32), room, room]

    fine = pltpu.VMEM((height, breadth, channels), F32)
    products = lambda count: pltpu.VMEM((count, PAD, 9 * channels), F32)
    forward_rooms = lambda count: tap_rooms(count) + [
        products(count),
        pltpu.VMEM((4, PAD, channels), F32),
        fine,
    ]
    if merged:
        value = call(
            inner_kernel,
            tile,
            [VMEM] * 3,
            forward_rooms(half_rows),
            flops=1_000,
            moved=1000,
        )(blocks, flat_up, flat_down)
        piece = rows_flat // (n_tx * n_ty)
        part = shape((2 * piece, channels), BF16)
        far, in_grad, own_sum, *sends = call(
            paired_kernel,
            (tile, tile, shape((2 * piece, channels), F32), part, part, part),
            [VMEM] * 9,
            [
                pltpu.VMEM((2 * height + 4, wide, channels), F32),
                pltpu.VMEM((height + 1, breadth // 2, 3 * channels), BF16),
                pltpu.VMEM((height, breadth // 2, 3 * channels), BF16),
                pltpu.VMEM((height, breadth // 2, 9 * channels), BF16),
                pltpu.VMEM((9 * channels // 2, 128), F32),
                pltpu.VMEM((9 * channels // 2, 128), F32),
                pltpu.VMEM((5 * depth, channels), F32),
                pltpu.VMEM((rows_flat // 2, channels), F32),
                pltpu.VMEM((height + 1, breadth // 2, depth), BF16),
                pltpu.VMEM((half_rows + 1, breadth // 2 + 8, 9 * channels), F32),
                fine,
                pltpu.VMEM((half_rows + 1, 8, 9 * channels), F32),
                pltpu.VMEM((half_rows + 1, 8, 9 * channels), F32),
            ],
            flops=5_000_000_000,
            moved=4_000_000,
        )(stash, grad_own, st_far, grad_far, rim, rim_far, flat_up, flat_down, value)
    else:
        whole = shape((rows_flat, channels), F32)
        in_grad, up_flat, down_flat = call(
            grads_kernel,
            (tile, whole, whole),
            [VMEM] * 5,
            tap_rooms(half_rows + 1)
            + [
                pltpu.VMEM((half_rows + 1, PAD, 9 * channels), BF16),
                pltpu.VMEM((9 * channels, 128), F32),
                pltpu.VMEM((9 * channels, 128), F32),
                products(half_rows + 1),
                fine,
            ],
            flops=500_000_000,
            moved=4_000_000,
        )(blocks, *ys, flat_up, flat_down)
        pooled = lambda flat: lax.psum_scatter(
            flat.reshape(-1) * scaling, ("tx", "ty"), scatter_dimension=0, tiled=True
        )[None]
        down_sum, up_sum = pooled(down_flat), pooled(up_flat)

    mirror = [(i, segments - 1 - i) for i in range(segments)]
    if merged:
        ys = passed_on(ys, 2_000_000_000)
        near, strip = call(
            border_kernel,
            (tile, shape((3, breadth, channels), BF16)),
            [VMEM] * 6,
            forward_rooms(3),
            flops=600_000_000,
            moved=4_000_000,
        )(blocks, ys[0], value, in_grad, flat_up, flat_down)
        from_far = lax.ppermute(far, "segment", mirror)
        from_strip = lax.ppermute(strip, "segment", mirror)
        from_near = lax.ppermute(near, "segment", crossed("segment", 1))
        arrived = [lax.ppermute(sends[d - 1], "ty", crossed("ty", d)) for d in (2, 3, 1)]
        arrived = passed_on(arrived[:1], 800_000_000) + arrived[1:]
        (from_far,) = passed_on([from_far], 100_000_000, arrived[:1])
        arrived = arrived[:1] + passed_on(arrived[1:], 3_000_000_000, [from_far])
        summed = shape((piece, channels), F32)
        act_out, grad_out, partner_out, up_sum, down_sum = call(
            functools.partial(final_kernel, scaling),
            (shape(act_in.shape, BF16),) * 3 + (summed, summed),
            [VMEM] * 7,
            flops=1_000,
            moved=1000,
        )(from_near, from_far, from_strip, own_sum, *arrived)
        return act_out, grad_out, partner_out, down_sum.reshape(1, -1), up_sum.reshape(1, -1)
    near, far = call(
        forward_kernel,
        (tile, tile),
        [VMEM] * 6,
        forward_rooms(half_rows + 2),
        flops=600_000_000,
        moved=4_000_000,
    )(blocks, *ys, in_grad, flat_up, flat_down)
    from_far = lax.ppermute(far, "segment", mirror)
    from_near = lax.ppermute(near, "segment", crossed("segment", 1))
    blank = jnp.zeros_like(from_near)
    odd = position % 2 == 1
    act_out = jnp.where(position == 0, blank, jnp.where(odd, from_near, from_far))
    grad_out = jnp.where(position == segments - 1, blank, jnp.where(odd, from_far, from_near))
    return (act_out[None], grad_out[None], from_far[None], down_sum, up_sum)


def solution(mesh):
    tile = P("segment", "tx", "ty", None)
    weights = P("segment", None, None, None, None)
    grads = P("segment", ("tx", "ty"))
    rows = P(("tx", "ty"))
    return jax.shard_map(
        local,
        mesh=mesh,
        in_specs=(tile,) * 4 + (weights,) * 2 + (P(("tx", "ty"), None),) * 2 + (rows, P("tx", "ty")),
        out_specs=(tile,) * 3 + (grads,) * 2,
        check_vma=False,
    )
```

```python
import functools
import math

import jax
import jax.numpy as jnp
from jax import lax
from jax.experimental import pallas as pl
from jax.experimental.pallas import tpu as pltpu
from jax.sharding import PartitionSpec as P

F32 = jnp.float32
BF16 = jnp.bfloat16
VMEM = pl.BlockSpec(memory_space=pltpu.VMEM)
SMEM = pl.BlockSpec(memory_space=pltpu.SMEM)
HBM = pl.BlockSpec(memory_space=pltpu.HBM)
LEFT = 8
PAD = 48
BORDER = 3
STRIP_ROWS = 7


def call(body, out_shape, in_specs, scratch=(), flops=0, moved=0, limit=24, out_specs=None, aliases=()):
    out_specs = out_specs or jax.tree.map(lambda _: VMEM, out_shape)
    return pl.pallas_call(
        body,
        out_shape=out_shape,
        in_specs=in_specs,
        out_specs=out_specs,
        scratch_shapes=list(scratch),
        input_output_aliases=dict(aliases),
        compiler_params=pltpu.CompilerParams(vmem_limit_bytes=limit * 1024 * 1024),
        cost_estimate=pl.CostEstimate(flops=flops, bytes_accessed=moved, transcendentals=0),
    )


def passed_on(arrays, flops, after=()):
    here = [pl.BlockSpec(memory_space=pl.ANY)] * len(arrays)
    return list(call(
        lambda *refs: None,
        tuple(jax.ShapeDtypeStruct(x.shape, x.dtype) for x in arrays),
        here + [pl.BlockSpec(memory_space=pl.ANY)] * len(after),
        flops=flops,
        moved=1000,
        out_specs=tuple(here),
        aliases=[(k, k) for k in range(len(arrays))],
    )(*arrays, *after))


def copies_in_parts(pairs, arrived):
    copies = []
    for source, target, parts in pairs:
        length = source.shape[0] // parts
        for part in range(parts):
            rows = pl.ds(part * length, length)
            views = (source.at[rows], target.at[rows]) if parts > 1 else (source, target)
            copies.append(pltpu.make_async_copy(*views, arrived.at[len(copies)]))
    return copies


def in_hbm(*operands):
    return [pltpu.with_memory_space_constraint(x, pltpu.HBM) for x in operands]


def sublane(shape):
    return lax.broadcasted_iota(jnp.int32, shape, len(shape) - 2)


def flag(condition):
    return jnp.where(condition, 1.0, 0.0).astype(F32)


def traits():
    segments = lax.axis_size("segment")
    position = lax.axis_index("segment")
    decoder = flag(position >= segments // 2)
    return decoder, 1.0 - decoder, position == segments - 1


def edge_kernel(owner_in, cell_in, land_in, act, par, st, gr, coarse, grad_out, pay0, pay1, *scratch):
    act_l, act_r, st_l, st_r, par_v, gr_v, plane, held_v, owner, cell, land, arrived = scratch
    rows, breadth = gr.shape[1], gr.shape[2]
    first, final = pl.ds(0, 16), pl.ds(breadth - 16, 16)
    scalars = copies_in_parts(((owner_in, owner, 1), (cell_in, cell, 1), (land_in, land, 1)), arrived)
    copies = copies_in_parts(
        (
            (gr.at[0], gr_v, 1),
            (par.at[0], par_v, 1),
            (act.at[0, :, first], act_l, 1),
            (act.at[0, :, final], act_r, 1),
            (st.at[0, :, first], st_l, 1),
            (st.at[0, :, final], st_r, 1),
            (coarse, held_v, 1),
        ),
        arrived.at[pl.ds(3, 13)],
    )
    for copy in scalars + copies:
        copy.start()
    for copy in scalars:
        copy.wait()
    decoder, encoder, last = traits()
    groups = rows // 4
    per_row = breadth // 4
    low = sublane((8, 128)) < 4
    for group in range(groups):
        for part in range(breadth // 8):
            weigh = [jnp.where(last, land[group, 2 * part + k], 1).astype(F32) for k in range(2)]
            plane[group, 8 * part : 8 * part + 8] = jnp.where(low, weigh[0], weigh[1])

    def ids(column):
        tile = jnp.zeros((8, 128), F32)
        where = sublane((8, 128))
        for row in range(groups):
            spot = row * per_row + column
            tile = jnp.where(where == row, owner[spot].astype(F32), tile)
            tile = jnp.where(where == 4 + row, cell[spot].astype(F32), tile)
        return tile

    left_ids, right_ids = ids(0), ids(per_row - 1)
    for copy in copies:
        copy.wait()
    for row in range(rows):
        grad = gr_v[row].astype(F32) + encoder * par_v[row].astype(F32)
        grad_out[row] = (grad * plane[row // 4]).astype(BF16)

    where = sublane((rows, 8, 128))
    begin, end = slice(0, 16), slice(breadth - 16, breadth)
    grad = grad_out[:, begin].astype(F32)[:, 0:8]
    stash = st_l[...].astype(F32)[:, 0:8]
    block = act_l[...].astype(F32)[:, 0:8] + decoder * par_v[:, begin].astype(F32)[:, 0:8]
    after = jnp.where(
        where < 3, grad, jnp.where(where < 5, pltpu.roll(stash, 3, 1), pltpu.roll(block, 5, 1))
    )
    grad = grad_out[:, end].astype(F32)[:, 8:16]
    stash = st_r[...].astype(F32)[:, 8:16]
    block = act_r[...].astype(F32)[:, 8:16] + decoder * par_v[:, end].astype(F32)[:, 8:16]
    before = jnp.where(
        where == 7, grad, jnp.where(where == 6, pltpu.roll(stash, 7, 1), pltpu.roll(block, 6, 1))
    )
    even = lax.axis_index("ty") % 2 == 0
    strips = jnp.where(even, before, after).astype(BF16), jnp.where(even, after, before).astype(BF16)
    named = jnp.where(even, right_ids, left_ids), jnp.where(even, left_ids, right_ids)
    held = held_v[...].reshape(coarse.shape[0] // 8, 8, 128)
    for k, pay in enumerate((pay0, pay1)):
        pay[0:rows] = strips[k]
        pay[rows] = named[k].astype(BF16)
        pay[rows + 1 :] = held


def prepare_kernel(act, par, st, up, down, base, stash, flat_up, flat_down, *scratch):
    act_v, par_v, up_v, down_v, arrived = scratch
    tiles = (act.at[0], act_v, 1), (par.at[0], par_v, 1), (st.at[0], stash, 1)
    copies = copies_in_parts(tiles + ((up, up_v, 1), (down, down_v, 1)), arrived)
    for copy in copies:
        copy.start()
    decoder, _, _ = traits()
    for copy in copies:
        copy.wait()
    for row in range(act_v.shape[0]):
        base[row] = act_v[row].astype(F32) + decoder * par_v[row].astype(F32)
    lane_taps(up_v, flat_up)
    lane_taps(down_v, flat_down)


def side_rims(z0, z1, rows):
    ty = lax.axis_index("ty")
    even = ty % 2 == 0
    first, second = z0[0:rows].astype(F32), z1[0:rows].astype(F32)
    before = jnp.where(ty > 0, jnp.where(even, second, first), 0.0)
    after = jnp.where(ty < lax.axis_size("ty") - 1, jnp.where(even, first, second), 0.0)
    return before, after


def rim_kernel(z0, z1, _weights, _stash, rim):
    before, after = side_rims(z0, z1, rim.shape[0])
    rim[...] = jnp.where(sublane(rim.shape) < 5, after, before).astype(BF16)


def condition_kernel(merged, owner, cell, base, z0, z1, coarse, *rest):
    rows, breadth = base.shape[0], base.shape[1]
    groups = rows // 4
    per_row = breadth // 4
    cells = groups * per_row
    wide = LEFT + breadth
    ty = lax.axis_index("ty")
    low = sublane((8, 128)) < 4
    if merged:
        z2, pay, ext, table, plane = rest
        table[pl.ds(pl.multiple_of(ty * cells, 8), cells)] = coarse[...].astype(F32)
        others = (
            (ty ^ 1, z0[rows + 1 :].astype(F32).reshape(cells, 128)),
            (ty ^ 3, z1[rows + 1 :].astype(F32).reshape(cells, 128)),
            (ty ^ 2, z2[...].astype(F32)),
        )
        for other, value in others:
            table[pl.ds(pl.multiple_of(other * cells, 8), cells)] = value
    else:
        st, grad_own, pay, pay1, full, table, plane = rest
        ext = full.at[2]
        table[...] = coarse[...].astype(F32)
    before, after = side_rims(z0, z1, rows + 1)

    def rim_condition(tile, valid):
        wanted = tile[rows]
        spot = wanted * cells + pltpu.roll(wanted, 4, 0)
        lanes = lax.broadcasted_iota(jnp.int32, (8, table.shape[0]), 1).astype(F32)
        spread = jnp.broadcast_to(spot[:, 0:1], lanes.shape)
        hot = jnp.where(spread == lanes, 1.0, 0.0).astype(BF16)
        named = lax.dot(hot, table[...].astype(BF16), preferred_element_type=F32)
        picked = [jnp.broadcast_to(named[row : row + 1], (8, 128))[None] for row in range(groups)]
        spread_rows = jnp.concatenate([p for p in picked for _ in range(4)], axis=0)
        return jnp.where(valid, spread_rows, 0.0)

    rim = pltpu.roll(before[0:rows], 2, 1) + rim_condition(before, ty > 0)
    ext[:, 0:8] = rim.astype(BF16)
    rim = pltpu.roll(after[0:rows], 3, 1) + rim_condition(after, ty < lax.axis_size("ty") - 1)
    ext[:, wide : wide + 8] = rim.astype(BF16)
    for group in range(groups):
        for part in range(breadth // 8):
            spots = [group * per_row + 2 * part + k for k in range(2)]
            named = [
                jnp.broadcast_to(table[pl.ds(owner[s] * cells + cell[s], 1)], (8, 128)) for s in spots
            ]
            plane[group, 8 * part : 8 * part + 8] = jnp.where(low, named[0], named[1])
    for row in range(rows):
        ext[row, LEFT:wide] = (base[row] + plane[row // 4]).astype(BF16)

    upper = lax.axis_index("tx") % 2 == 0
    if merged:
        near = sublane((8, 128)) < 5
        for k in range(3):
            top, bottom = min(k, 1), rows - 3 + k
            for part in range(breadth // 8):
                cols = pl.ds(LEFT + 8 * part, 8)
                pay[9 * k + part] = jnp.where(upper, ext[bottom, cols], ext[top, cols])
            tiles = [
                jnp.where(near, ext[row, pl.ds(wide, 8)], ext[row, pl.ds(0, 8)]) for row in (top, bottom)
            ]
            pay[9 * k + breadth // 8] = jnp.where(upper, tiles[1], tiles[0])
        return
    full[0, :, 0:8] = before[0:rows].astype(BF16)
    full[1, :, 0:8] = pltpu.roll(before[0:rows], 1, 1).astype(BF16)
    full[0, :, wide : wide + 8] = after[0:rows].astype(BF16)
    full[1, :, wide : wide + 8] = pltpu.roll(after[0:rows], 5, 1).astype(BF16)
    full[0, :, LEFT:wide] = grad_own[...]
    full[1, :, LEFT:wide] = st[...]
    leading = [(0, 0), (0, 1), (0, 2), (1, 0), (1, 1), (2, 0), (2, 1)]
    closing = [(0, rows - 1), (1, rows - 1), (2, rows - 3), (2, rows - 2), (2, rows - 1)]
    closing = closing + closing[-1:] * 2
    for k in range(STRIP_ROWS):
        top, bottom = full[leading[k]], full[closing[k]]
        pay[k] = jnp.where(upper, bottom, top)
        pay1[k] = jnp.where(upper, top, bottom)


def rims(y0, y1):
    tx = lax.axis_index("tx")
    upper = tx % 2 == 0
    before_ok, after_ok = tx > 0, tx < lax.axis_size("tx") - 1

    def row(valid, from_first, k):
        value = jnp.where(from_first, y0[k].astype(F32), y1[k].astype(F32))
        return jnp.where(valid, value, 0.0)

    before = lambda k: row(before_ok, jnp.logical_not(upper), k)
    after = lambda k: row(after_ok, upper, k)
    return before, after


def spread_taps(field, taps, odd_taps, count, first):
    width = taps.shape[1]
    for row in range(count):
        target = taps if row % 2 == 0 else odd_taps
        for tap in range(3):
            value = field[row, pl.ds(first + tap, width, stride=2), :]
            target[row // 2, :, tap * 128 : tap * 128 + 128] = value.astype(BF16)


def three_rows(even_taps, odd_taps, count):
    wide = 3 * 128
    whole = lambda ref, a: ref[a : a + count].reshape(count * ref.shape[1], wide)
    return whole(even_taps, 0), whole(odd_taps, 0), whole(even_taps, 1)


def lower(even_taps, odd_taps, count, down):
    views = three_rows(even_taps, odd_taps, count)
    wide = 3 * 128
    total = None
    for a in range(3):
        term = lax.dot_general(
            views[a],
            down[:, a * wide : a * wide + wide],
            (((1,), (1,)), ((), ())),
            preferred_element_type=F32,
        )
        total = term if total is None else total + term
    return total


def lane_taps(taps, flat):
    for tap in range(9):
        flat[:, tap * 128 : tap * 128 + 128] = taps[tap]


def window_sums(plane_of, count, sums):
    previous = None
    for row in range(2 * count + 2):
        plane = [plane_of(row, k) for k in range(4)]
        current = [plane[2] + plane[3], plane[1] + plane[2], plane[0] + plane[1]]
        if row > 0:
            for a in range(3):
                double = row - 3 + a
                if double % 2 == 0 and 0 <= double // 2 < count:
                    for b in range(3):
                        lanes = slice((3 * a + b) * 128, (3 * a + b) * 128 + 128)
                        sums[double // 2, :, lanes] = (previous[b] + current[b]).astype(sums.dtype)
        previous = current


def sweep(wide, field, even_taps, odd_taps, sums, flat_up, down, count, fill_stash, fill_grad):
    field[:, wide:] = jnp.zeros((field.shape[0], field.shape[1] - wide, 128), F32)
    fill_stash()
    spread_taps(field, even_taps, odd_taps, 2 * count + 1, LEFT - 1)
    pre_back = lower(even_taps, odd_taps, count, down)
    logistic = 0.5 + 0.5 * jnp.tanh(0.5 * pre_back)
    reduced = pre_back * logistic
    slope = logistic * (1.0 + pre_back * (1.0 - logistic))
    fill_grad()
    window_sums(lambda row, k: field[row, pl.ds(LEFT - 1 + k, PAD, stride=2), :], count, sums)
    windows = sums[...].reshape(count * PAD, 9 * 128)
    raised = lax.dot_general(windows, flat_up[...], (((1,), (1,)), ((), ())), preferred_element_type=F32)
    return reduced.astype(BF16), raised * slope


def places(count, depth):
    shape = (count, PAD, depth)
    row = lax.broadcasted_iota(jnp.int32, shape, 0).reshape(count * PAD, depth)
    col = lax.broadcasted_iota(jnp.int32, shape, 1).reshape(count * PAD, depth)
    return row, col


def flatten_rows(d0, d1, flat, start):
    pairs = d0.shape[0] // 2
    left_even, left_odd = d0[pl.ds(0, pairs, stride=2)], d0[pl.ds(1, pairs, stride=2)]
    right_even, right_odd = d1[pl.ds(0, pairs, stride=2)], d1[pl.ds(1, pairs, stride=2)]
    near = lax.broadcasted_iota(jnp.int32, left_even.shape, 1) < 64
    turned = pltpu.roll(left_odd, 64, 1)
    flat[pl.ds(start, pairs, stride=3)] = left_even
    flat[pl.ds(start + 1, pairs, stride=3)] = jnp.where(near, right_even, turned)
    flat[pl.ds(start + 2, pairs, stride=3)] = jnp.where(near, turned, pltpu.roll(right_odd, 64, 1))


def across(left, right):
    return lax.dot_general(left, right, (((0,), (0,)), ((), ())), preferred_element_type=F32)


def grads_kernel(
    ext, y0, y1, flat_up, flat_down, in_grad, up_flat, down_flat, field, even_taps, odd_taps, sums, d0, d1, products, fine
):
    rows = ext.shape[1]
    wide = ext.shape[2]
    half_rows, half_cols = rows // 2, (wide - 16) // 2
    count = half_rows + 1
    before, after = rims(y0, y1)
    tx, ty = lax.axis_index("tx"), lax.axis_index("ty")
    has_below, has_right = tx < lax.axis_size("tx") - 1, ty < lax.axis_size("ty") - 1

    def fill(kind, top, bottom):
        field[0, 0:wide] = before(top)
        for row in range(rows):
            field[row + 1, 0:wide] = ext[kind, row].astype(F32)
        for k, spot in enumerate(bottom):
            field[rows + 1 + k, 0:wide] = after(spot)

    reduced, pre_grad = sweep(
        wide,
        field,
        even_taps,
        odd_taps,
        sums,
        flat_up,
        flat_down,
        count,
        lambda: fill(1, 1, (3, 4)),
        lambda: fill(0, 0, (0, 1, 2)),
    )
    depth = reduced.shape[1]
    row, col = places(count, depth)
    inside = ((row < half_rows) | has_below) & ((col < half_cols) | (has_right & (col == half_cols)))
    pre_grad = jnp.where(inside, pre_grad, 0.0).astype(BF16).reshape(count, PAD, depth)
    base = lambda row_id: ext[0, row_id, LEFT : wide - 8]
    moved = lax.dot(pre_grad.reshape(count * PAD, depth), flat_down[...], preferred_element_type=F32)
    products[...] = moved.reshape(count, PAD, 9 * 128)
    combine_fine(products, base, fine, in_grad)
    cells = half_rows * half_cols
    own = lambda value: value[:half_rows, :half_cols].reshape(cells, value.shape[-1])
    reduced, own_grad = own(reduced.reshape(count, PAD, depth)), own(pre_grad)
    terms = across(reduced, own(sums))
    for tap in range(9):
        up_flat[tap * depth : tap * depth + depth] = terms[:, tap * 128 : tap * 128 + 128]
    span = 3 * 128
    for a, view in enumerate((even_taps, odd_taps, even_taps)):
        taps = view[a // 2 : a // 2 + half_rows, 0:half_cols].reshape(cells, span)
        term = across(taps, own_grad)
        d0[a * span : a * span + span] = term[:, 0:128]
        d1[a * span : a * span + span, 0:64] = term[:, 128:192]
    flatten_rows(d0, d1, down_flat, 0)


def paired_kernel(
    st, grad, st_far, grad_far, rim, rim_far, flat_up, flat_down, value, far, in_grad, *rest
):
    own_sum, send1, send2, send3, field, even_taps, odd_taps, sums, d0, d1, up_flat, down_flat = rest[:12]
    grads, products, fine, edge_taps, edge_sums, grad_field = rest[12:]
    rows, breadth = grad.shape[0], grad.shape[1]
    wide = breadth + 16
    count, half_rows, half_cols = rows, rows // 2, breadth // 2
    cells = count * half_cols
    edge_count = half_rows + 1
    tx, ty = lax.axis_index("tx"), lax.axis_index("ty")
    has_below = tx < lax.axis_size("tx") - 1
    has_right = ty < lax.axis_size("ty") - 1
    first_row = rows * tx

    def fill(field, here_rows, there_rows, turn_before, turn_after):
        blank = jnp.zeros((wide, 128), F32)
        field[0, 0:wide] = blank
        field[2 * rows + 1, 0:wide] = blank
        here, there = 1 + rows * tx, 1 + rows * (1 - tx)
        for start, source, sides in ((here, here_rows, rim), (there, there_rows, rim_far)):
            for row in range(rows):
                field[start + row, LEFT : LEFT + breadth] = source(row).astype(F32)
            sides = sides[...].astype(F32)
            turned = lambda turn: pltpu.roll(sides, turn, 1) if turn else sides
            field[pl.ds(start, rows), 0:8] = turned(turn_before)
            field[pl.ds(start, rows), LEFT + breadth : wide] = turned(turn_after)

    def slopes(pre_back):
        logistic = 0.5 + 0.5 * jnp.tanh(0.5 * pre_back)
        return logistic, logistic * (1.0 + pre_back * (1.0 - logistic))

    def full_taps(values, weights):
        return lax.dot_general(values, weights[...], (((1,), (1,)), ((), ())), preferred_element_type=F32)

    edge = lambda field, row, k: field[first_row + row, pl.ds(LEFT - 1 + k + breadth, 8, stride=2), :]
    flat_edge = lambda ref: ref[...].reshape(edge_count * 8, 9 * 128).astype(BF16)

    for each in (field, grad_field):
        each[:, wide:] = jnp.zeros((each.shape[0], each.shape[1] - wide, 128), F32)
    fill(field, lambda row: st[row], lambda row: st_far[0, row], 1, 5)
    spread_taps(field, even_taps, odd_taps, 2 * count + 1, LEFT - 1)
    for p in range(edge_count):
        for tap in range(9):
            edge_taps[p, :, tap * 128 : tap * 128 + 128] = edge(field, 2 * p + tap // 3, tap % 3)
    pre_back = lower(even_taps, odd_taps, count, flat_down)
    logistic, slope = slopes(pre_back)
    reduced = (pre_back * logistic).astype(BF16)
    edge_slope = slopes(full_taps(flat_edge(edge_taps), flat_down))[1]

    fill(grad_field, lambda row: grad[row], lambda row: grad_far[row], 0, 0)
    window_sums(lambda row, k: grad_field[row, pl.ds(LEFT - 1 + k, half_cols, stride=2), :], count, sums)
    window_sums(lambda row, k: edge(grad_field, row, k), edge_count, edge_sums)
    depth = reduced.shape[1]
    coupled = (full_taps(sums[...].reshape(cells, 9 * 128), flat_up) * slope).astype(BF16)
    edge_shape = (edge_count, 8, depth)
    row = lax.broadcasted_iota(jnp.int32, edge_shape, 0).reshape(edge_count * 8, depth)
    inside = has_right & ((row < half_rows) | has_below)
    edge_grad = jnp.where(inside, full_taps(flat_edge(edge_sums), flat_up) * edge_slope, 0.0).astype(BF16)
    half = up_flat.shape[0] - depth // 2
    lanes = pl.ds(pl.multiple_of(tx * 512, 128), 640)
    terms = across(reduced, sums[:, :, lanes].reshape(cells, 640))
    for tap in range(5):
        up_flat[tap * depth : tap * depth + depth] = terms[:, tap * 128 : tap * 128 + 128]
    span = 3 * 128
    outer = across(even_taps[pl.ds(tx, count)].reshape(cells, span), coupled)
    middle = across(odd_taps[0:count].reshape(cells, span), coupled)
    outer_at = pl.multiple_of(tx * (span // 2), 8)
    middle_at = pl.multiple_of((1 - tx) * span, 8)
    middle_half = jnp.where(tx == 0, middle[0 : span // 2], middle[span // 2 : span])
    d0[pl.ds(outer_at, span)] = outer[:, 0:128]
    d1[pl.ds(outer_at, span), 0:64] = outer[:, 128:192]
    d0[pl.ds(middle_at, span // 2)] = middle_half[:, 0:128]
    d1[pl.ds(middle_at, span // 2), 0:64] = middle_half[:, 128:192]
    flatten_rows(d0, d1, down_flat, 0)
    piece = half // 4
    up_start = tx * (depth // 2)
    for distance, target in enumerate((own_sum, send1, send2, send3)):
        place = (ty ^ distance) * piece
        both = [
            up_flat[pl.ds(pl.multiple_of(up_start + place, 8), piece)],
            down_flat[pl.ds(pl.multiple_of(place, 8), piece)],
        ]
        target[...] = jnp.concatenate(both, axis=0).astype(target.dtype)
    grads[0:count] = coupled.reshape(count, half_cols, depth)
    grads[count] = jnp.zeros((half_cols, depth), BF16)
    own_rows = grads[pl.ds(half_rows * tx, edge_count)].reshape(edge_count * half_cols, depth)
    moved = lax.dot(own_rows, flat_down[...], preferred_element_type=F32)
    products[:, 0:half_cols] = moved.reshape(edge_count, half_cols, 9 * 128)
    moved = lax.dot(edge_grad, flat_down[...], preferred_element_type=F32)
    products[:, half_cols:] = moved.reshape(edge_count, 8, 9 * 128)
    combine_fine(products, lambda row: grad[row], fine, in_grad)
    for row in range(far.shape[0]):
        here = row + (rows - far.shape[0]) * tx
        far[row] = relay_choices(value[here], in_grad[here])[1]


def combine_fine(products, base, fine, target):
    half_rows, half_cols = fine.shape[0] // 2, fine.shape[1] // 2

    def part(p, a, b, offset):
        tap = 3 * a + b
        return products[p, offset : offset + half_cols, tap * 128 : tap * 128 + 128]

    for p in range(half_rows):
        fine[2 * p, pl.ds(0, half_cols, stride=2), :] = part(p, 1, 1, 0)
        fine[2 * p, pl.ds(1, half_cols, stride=2), :] = part(p, 1, 2, 0) + part(p, 1, 0, 1)
        fine[2 * p + 1, pl.ds(0, half_cols, stride=2), :] = part(p, 2, 1, 0) + part(p + 1, 0, 1, 0)
        fine[2 * p + 1, pl.ds(1, half_cols, stride=2), :] = (
            part(p, 2, 2, 0) + part(p, 2, 0, 1) + part(p + 1, 0, 2, 0) + part(p + 1, 0, 0, 1)
        )
    for row in range(fine.shape[0]):
        target[row] = (base(row).astype(F32) + fine[row]).astype(BF16)


def raise_rows(field, even_taps, odd_taps, products, flat_up, flat_down, count, first, valid):
    spread_taps(field, even_taps, odd_taps, 2 * count + 1, first)
    pre_down = lower(even_taps, odd_taps, count, flat_down)
    reduced = pre_down * (0.5 + 0.5 * jnp.tanh(0.5 * pre_down))
    row, col = places(count, reduced.shape[1])
    reduced = jnp.where(valid(row, col), reduced, 0.0).astype(BF16)
    raised = lax.dot(reduced, flat_up[...], preferred_element_type=F32)
    products[...] = raised.reshape(count, PAD, 9 * 128)


def fine_row(products, mixed, target, picks):
    half_cols = target.shape[0] // 2
    col = []
    for b in range(3):
        terms = [
            products[q, :, (3 * a + b) * 128 : (3 * a + b) * 128 + 128]
            for a, q in enumerate(picks)
            if q is not None
        ]
        col.append(sum(terms[1:], terms[0]))
    mixed[0], mixed[1] = col[0], col[1] + col[2]
    mixed[2], mixed[3] = col[0] + col[1], col[2]
    target[pl.ds(0, half_cols, stride=2), :] = mixed[0, 0:half_cols] + mixed[1, 1 : half_cols + 1]
    target[pl.ds(1, half_cols, stride=2), :] = mixed[2, 1 : half_cols + 1] + mixed[3, 2 : half_cols + 2]


def right_edge(half_cols):
    has_right = lax.axis_index("ty") < lax.axis_size("ty") - 1
    return lambda row, col: (col <= half_cols) | has_right


def relay_choices(value, in_grad):
    position, segments = lax.axis_index("segment"), lax.axis_size("segment")
    near = jnp.where(position % 2 == 0, value, in_grad)
    return near, jnp.where(position < segments // 2, value, in_grad)


def forward_kernel(blocks, y0, y1, in_grad, flat_up, flat_down, near, far, *scratch):
    field, even_taps, odd_taps, products, mixed, fine = scratch
    rows, wide = blocks.shape[1], blocks.shape[2]
    breadth = wide - 16
    half_rows, half_cols = rows // 2, breadth // 2
    has_below = lax.axis_index("tx") < lax.axis_size("tx") - 1
    before, after = rims(y0, y1)
    field[:, wide:] = jnp.zeros((field.shape[0], field.shape[1] - wide, 128), F32)
    for k in range(3):
        field[k, 0:wide] = before(2 + k)
    for row in range(rows):
        field[row + 3, 0:wide] = blocks[2, row].astype(F32)
    for k in range(2):
        field[rows + 3 + k, 0:wide] = after(5 + k)
    edge = right_edge(half_cols)
    valid = lambda row, col: ((row <= half_rows) | has_below) & edge(row, col)
    raise_rows(field, even_taps, odd_taps, products, flat_up, flat_down, half_rows + 2, LEFT - 3, valid)
    for p in range(half_rows):
        fine_row(products, mixed, fine.at[2 * p], (p, p + 1, p + 1))
        fine_row(products, mixed, fine.at[2 * p + 1], (p + 1, p + 1, p + 2))
    for row in range(rows):
        value = (blocks[2, row, LEFT : LEFT + breadth].astype(F32) + fine[row]).astype(BF16)
        near[row], far[row] = relay_choices(value, in_grad[row])


def inner_kernel(blocks, flat_up, flat_down, value, *scratch):
    field, even_taps, odd_taps, products, mixed, fine = scratch
    rows, wide = blocks.shape[0], blocks.shape[1]
    breadth = wide - 16
    half_rows, half_cols = rows // 2, breadth // 2
    field[:, wide:] = jnp.zeros((field.shape[0], field.shape[1] - wide, 128), F32)
    field[0, 0:wide] = jnp.zeros((wide, 128), F32)
    for row in range(rows):
        field[row + 1, 0:wide] = blocks[row].astype(F32)
    edge = right_edge(half_cols)
    raise_rows(field, even_taps, odd_taps, products, flat_up, flat_down, half_rows, LEFT - 3, edge)
    for p in range(half_rows):
        fine_row(products, mixed, fine.at[2 * p], (p - 1 if p else None, p, p))
        below = p + 1 if p + 1 < half_rows else None
        fine_row(products, mixed, fine.at[2 * p + 1], (p, p, below))
    for row in range(rows):
        value[row] = (blocks[row, LEFT : LEFT + breadth].astype(F32) + fine[row]).astype(BF16)


def border_kernel(blocks, y0, value, in_grad, flat_up, flat_down, near, strip, *scratch):
    field, even_taps, odd_taps, products, mixed, fine = scratch
    rows, wide = blocks.shape[0], blocks.shape[1]
    breadth = wide - 16
    half_cols = breadth // 2
    upper = lax.axis_index("tx") == 0
    field[:, wide:] = jnp.zeros((field.shape[0], field.shape[1] - wide, 128), F32)

    def far_row(k):
        tiles = [y0[(breadth // 8 + 1) * k + part].astype(F32) for part in range(breadth // 8 + 1)]
        return jnp.concatenate([tiles[-1]] + tiles, axis=0)

    own = lambda row: blocks[row].astype(F32)
    for k in range(7):
        lower_tile = far_row(k) if k < 3 else own(k - 3)
        upper_tile = own(rows - 5 + k) if k < 5 else far_row(k - 5)
        field[k, 0:wide] = jnp.where(upper, upper_tile, lower_tile)
    edge = right_edge(half_cols)
    raise_rows(field, even_taps, odd_taps, products, flat_up, flat_down, 3, LEFT - 3, edge)
    fine_row(products, mixed, fine.at[0], (0, 1, 1))
    fine_row(products, mixed, fine.at[1], (1, 1, 2))
    fine_row(products, mixed, fine.at[2], (1, 2, 2))
    repaired = [None] * 3
    for k in range(3):
        base = jnp.where(upper, own(rows - 3 + k), own(k))[LEFT : LEFT + breadth]
        added = jnp.where(upper, fine[max(k - 1, 0)], fine[k])
        repaired[k] = (base + added).astype(BF16)
        if k == 0:
            repaired[k] = jnp.where(upper, value[rows - 3], repaired[k])
        strip[k] = relay_choices(repaired[k], jnp.where(upper, in_grad[rows - 3 + k], in_grad[k]))[1]
    for row in range(rows):
        result = value[row]
        if row < 3:
            result = jnp.where(upper, result, repaired[row])
        if row >= rows - 3:
            result = jnp.where(upper, repaired[row - (rows - 3)], result)
        near[row] = relay_choices(result, in_grad[row])[0]


def final_kernel(
    scaling, near, far, strip, own, first, second, third, act_out, grad_out, partner_out, up_sum, down_sum
):
    rows, border = near.shape[0], strip.shape[0]
    position, last = lax.axis_index("segment"), lax.axis_size("segment") - 1
    upper = lax.axis_index("tx") == 0
    odd = position % 2 == 1
    for row in range(rows):
        from_upper = far[row] if row < rows - border else strip[row - (rows - border)]
        from_lower = strip[row] if row < border else far[row - border]
        from_far = jnp.where(upper, from_upper, from_lower)
        blank = jnp.zeros_like(from_far)
        partner_out[0, row] = from_far
        act_out[0, row] = jnp.where(position == 0, blank, jnp.where(odd, near[row], from_far))
        grad_out[0, row] = jnp.where(position == last, blank, jnp.where(odd, from_far, near[row]))
    total = own[...] + first[...].astype(F32) + second[...].astype(F32) + third[...].astype(F32)
    piece = up_sum.shape[0]
    up_sum[...] = total[0:piece] * scaling
    down_sum[...] = total[piece:] * scaling


def swaps(axis):
    size = lax.axis_size(axis)
    pairs = [(i, i + 1) for i in range(0, size - 1, 2)]
    other = [(i, i + 1) for i in range(1, size - 1, 2)]
    both = lambda pairs: pairs + [(j, i) for i, j in pairs]
    return both(pairs), both(other)


def crossed(axis, distance):
    return [(i, i ^ distance) for i in range(lax.axis_size(axis))]


def shape(dims, kind):
    return jax.ShapeDtypeStruct(tuple(dims), kind)


def local(
    act_in,
    partner_in,
    stashed,
    grad_in,
    down_weights,
    up_weights,
    coarse,
    nest_owner,
    nest_cell,
    land_weight,
):
    height, breadth, channels = act_in.shape[1:]
    depth = down_weights.shape[-1]
    half_rows = height // 2
    n_tx, n_ty = lax.axis_size("tx"), lax.axis_size("ty")
    position, segments = lax.axis_index("segment"), lax.axis_size("segment")
    scaling = 1.0 / math.sqrt(height * breadth * n_tx * n_ty)
    down_taps = jnp.swapaxes(down_weights, 3, 4).reshape(9, depth, channels)
    up_taps = up_weights.reshape(9, depth, channels)

    owners = nest_owner.reshape(-1)
    tile = shape((height, breadth, channels), BF16)
    pay = shape((height + 1 + coarse.shape[0] // 8, 8, channels), BF16)
    merged = n_ty == 4 and n_tx == 2
    if merged:
        st_far = lax.ppermute(stashed, "tx", crossed("tx", 1))
    side = pltpu.VMEM((height, 16, channels), BF16)
    full = pltpu.VMEM((height, breadth, channels), BF16)
    grad_own, z_pay0, z_pay1 = call(
        edge_kernel,
        (tile, pay, pay),
        [HBM] * 8,
        [side] * 4
        + [full] * 2
        + [pltpu.VMEM((height // 4, breadth, channels), F32), pltpu.VMEM(coarse.shape, BF16)]
        + [pltpu.SMEM(scalars.shape, jnp.int32) for scalars in (owners, nest_cell, land_weight)]
        + [pltpu.SemaphoreType.DMA((16,))],
        flops=1000,
        moved=1000,
    )(*in_hbm(owners, nest_cell, land_weight, act_in, partner_in, stashed, grad_in, coarse))
    pairs, others = swaps("ty")
    if merged:
        others = crossed("ty", 3)
        grad_far = lax.ppermute(grad_own, "tx", crossed("tx", 1))
    z0 = lax.ppermute(z_pay0, "ty", pairs)
    z1 = lax.ppermute(z_pay1, "ty", others)
    if merged:
        table_parts = (coarse, lax.ppermute(coarse, "ty", crossed("ty", 2)))
    else:
        table_parts = (lax.all_gather(coarse, "ty", tiled=True),)
    flat = shape((depth, 9 * channels), BF16)
    taps_room = pltpu.VMEM((9, depth, channels), BF16)
    base, stash, flat_up, flat_down = call(
        prepare_kernel,
        (shape((height, breadth, channels), F32), tile, flat, flat),
        [HBM] * 5,
        [full, full, taps_room, taps_room, pltpu.SemaphoreType.DMA((30,))],
        flops=1000,
        moved=1000,
    )(*in_hbm(act_in, partner_in, stashed, up_taps, down_taps))
    operands = (base, z0, z1, *table_parts)
    rooms = [
        pltpu.VMEM((n_ty * coarse.shape[0], channels), F32),
        pltpu.VMEM((height // 4, breadth, channels), F32),
    ]
    pairs, others = swaps("tx")
    if merged:
        rim = call(
            rim_kernel,
            shape((height, 8, channels), BF16),
            [VMEM] * 2 + [pl.BlockSpec(memory_space=pl.ANY)] * 2,
            flops=1000,
            moved=1000,
        )(z0, z1, flat_up, st_far)
        rim_far = lax.ppermute(rim, "tx", pairs)
        pay, blocks = call(
            functools.partial(condition_kernel, True),
            (shape((3 * (breadth // 8 + 1), 8, channels), BF16), shape((height, breadth + 16, channels), BF16)),
            [SMEM] * 2 + [VMEM] * len(operands),
            rooms,
            flops=2_000_000_000,
            moved=1000,
        )(owners, nest_cell, *operands)
        ys = [lax.ppermute(pay, "tx", pairs)]
    else:
        pay = shape((STRIP_ROWS, breadth + 16, channels), BF16)
        *pays, blocks = call(
            functools.partial(condition_kernel, False),
            (pay, pay, shape((3, height, breadth + 16, channels), BF16)),
            [SMEM] * 2 + [VMEM] * (len(operands) + 2),
            rooms,
        )(owners, nest_cell, *operands, stash, grad_own)
        ys = [lax.ppermute(pays[0], "tx", pairs), lax.ppermute(pays[1], "tx", others) if others else pays[1]]

    wide = 2 * PAD + 16
    rows_flat = 9 * depth

    def tap_rooms(count):
        room = pltpu.VMEM((count + 1, PAD, 3 * channels), BF16)
        return [pltpu.VMEM((2 * count + 2, wide, channels), F32), room, room]

    fine = pltpu.VMEM((height, breadth, channels), F32)
    products = lambda count: pltpu.VMEM((count, PAD, 9 * channels), F32)
    forward_rooms = lambda count: tap_rooms(count) + [
        products(count),
        pltpu.VMEM((4, PAD, channels), F32),
        fine,
    ]
    if merged:
        value = call(
            inner_kernel,
            tile,
            [VMEM] * 3,
            forward_rooms(half_rows),
            flops=1_000,
            moved=1000,
        )(blocks, flat_up, flat_down)
        piece = rows_flat // (n_tx * n_ty)
        part = shape((2 * piece, channels), BF16)
        far, in_grad, own_sum, *sends = call(
            paired_kernel,
            (shape((height - BORDER, breadth, channels), BF16), tile, shape((2 * piece, channels), F32), part, part, part),
            [VMEM] * 9,
            [
                pltpu.VMEM((2 * height + 4, wide, channels), F32),
                pltpu.VMEM((height + 1, breadth // 2, 3 * channels), BF16),
                pltpu.VMEM((height, breadth // 2, 3 * channels), BF16),
                pltpu.VMEM((height, breadth // 2, 9 * channels), BF16),
                pltpu.VMEM((9 * channels // 2, 128), F32),
                pltpu.VMEM((9 * channels // 2, 128), F32),
                pltpu.VMEM((5 * depth, channels), F32),
                pltpu.VMEM((rows_flat // 2, channels), F32),
                pltpu.VMEM((height + 1, breadth // 2, depth), BF16),
                pltpu.VMEM((half_rows + 1, breadth // 2 + 8, 9 * channels), F32),
                fine,
                pltpu.VMEM((half_rows + 1, 8, 9 * channels), F32),
                pltpu.VMEM((half_rows + 1, 8, 9 * channels), F32),
                pltpu.VMEM((2 * height + 4, wide, channels), F32),
            ],
            flops=5_000_000_000,
            moved=4_000_000,
        )(stash, grad_own, st_far, grad_far, rim, rim_far, flat_up, flat_down, value)
    else:
        whole = shape((rows_flat, channels), F32)
        in_grad, up_flat, down_flat = call(
            grads_kernel,
            (tile, whole, whole),
            [VMEM] * 5,
            tap_rooms(half_rows + 1)
            + [
                pltpu.VMEM((half_rows + 1, PAD, 9 * channels), BF16),
                pltpu.VMEM((9 * channels, 128), F32),
                pltpu.VMEM((9 * channels, 128), F32),
                products(half_rows + 1),
                fine,
            ],
            flops=500_000_000,
            moved=4_000_000,
        )(blocks, *ys, flat_up, flat_down)
        pooled = lambda flat: lax.psum_scatter(
            flat.reshape(-1) * scaling, ("tx", "ty"), scatter_dimension=0, tiled=True
        )[None]
        down_sum, up_sum = pooled(down_flat), pooled(up_flat)

    mirror = [(i, segments - 1 - i) for i in range(segments)]
    if merged:
        ys = passed_on(ys, 2_000_000_000)
        near, strip = call(
            border_kernel,
            (tile, shape((BORDER, breadth, channels), BF16)),
            [VMEM] * 6,
            forward_rooms(3),
            flops=600_000_000,
            moved=4_000_000,
        )(blocks, ys[0], value, in_grad, flat_up, flat_down)
        from_far = lax.ppermute(far, "segment", mirror)
        from_strip = lax.ppermute(strip, "segment", mirror)
        from_near = lax.ppermute(near, "segment", crossed("segment", 1))
        arrived = [lax.ppermute(sends[d - 1], "ty", crossed("ty", d)) for d in (2, 1, 3)]
        arrived = passed_on(arrived[:1], 800_000_000) + arrived[1:]
        (from_far,) = passed_on([from_far], 100_000_000, arrived[:1])
        arrived = arrived[:1] + passed_on(arrived[1:], 3_000_000_000, [from_far])
        summed = shape((piece, channels), F32)
        act_out, grad_out, partner_out, up_sum, down_sum = call(
            functools.partial(final_kernel, scaling),
            (shape(act_in.shape, BF16),) * 3 + (summed, summed),
            [VMEM] * 7,
            flops=1_000,
            moved=1000,
        )(from_near, from_far, from_strip, own_sum, *arrived)
        return act_out, grad_out, partner_out, down_sum.reshape(1, -1), up_sum.reshape(1, -1)
    near, far = call(
        forward_kernel,
        (tile, tile),
        [VMEM] * 6,
        forward_rooms(half_rows + 2),
        flops=600_000_000,
        moved=4_000_000,
    )(blocks, *ys, in_grad, flat_up, flat_down)
    from_far = lax.ppermute(far, "segment", mirror)
    from_near = lax.ppermute(near, "segment", crossed("segment", 1))
    blank = jnp.zeros_like(from_near)
    odd = position % 2 == 1
    act_out = jnp.where(position == 0, blank, jnp.where(odd, from_near, from_far))
    grad_out = jnp.where(position == segments - 1, blank, jnp.where(odd, from_far, from_near))
    return (act_out[None], grad_out[None], from_far[None], down_sum, up_sum)


def solution(mesh):
    tile = P("segment", "tx", "ty", None)
    weights = P("segment", None, None, None, None)
    grads = P("segment", ("tx", "ty"))
    rows = P(("tx", "ty"))
    return jax.shard_map(
        local,
        mesh=mesh,
        in_specs=(tile,) * 4 + (weights,) * 2 + (P(("tx", "ty"), None),) * 2 + (rows, P("tx", "ty")),
        out_specs=(tile,) * 3 + (grads,) * 2,
        check_vma=False,
    )
```

```python
import functools
import math

import jax
import jax.numpy as jnp
from jax import lax
from jax.experimental import pallas as pl
from jax.experimental.pallas import tpu as pltpu
from jax.sharding import PartitionSpec as P

F32 = jnp.float32
BF16 = jnp.bfloat16
VMEM = pl.BlockSpec(memory_space=pltpu.VMEM)
SMEM = pl.BlockSpec(memory_space=pltpu.SMEM)
HBM = pl.BlockSpec(memory_space=pltpu.HBM)
LEFT = 8
PAD = 48
BORDER = 3
STRIP_ROWS = 7


def call(body, out_shape, in_specs, scratch=(), flops=0, moved=0, limit=24, out_specs=None, aliases=()):
    out_specs = out_specs or jax.tree.map(lambda _: VMEM, out_shape)
    return pl.pallas_call(
        body,
        out_shape=out_shape,
        in_specs=in_specs,
        out_specs=out_specs,
        scratch_shapes=list(scratch),
        input_output_aliases=dict(aliases),
        compiler_params=pltpu.CompilerParams(vmem_limit_bytes=limit * 1024 * 1024),
        cost_estimate=pl.CostEstimate(flops=flops, bytes_accessed=moved, transcendentals=0),
    )


def passed_on(arrays, flops, after=()):
    here = [pl.BlockSpec(memory_space=pl.ANY)] * len(arrays)
    return list(call(
        lambda *refs: None,
        tuple(jax.ShapeDtypeStruct(x.shape, x.dtype) for x in arrays),
        here + [pl.BlockSpec(memory_space=pl.ANY)] * len(after),
        flops=flops,
        moved=1000,
        out_specs=tuple(here),
        aliases=[(k, k) for k in range(len(arrays))],
    )(*arrays, *after))


def copies_in_parts(pairs, arrived):
    copies = []
    for source, target, parts in pairs:
        length = source.shape[0] // parts
        for part in range(parts):
            rows = pl.ds(part * length, length)
            views = (source.at[rows], target.at[rows]) if parts > 1 else (source, target)
            copies.append(pltpu.make_async_copy(*views, arrived.at[len(copies)]))
    return copies


def in_hbm(*operands):
    return [pltpu.with_memory_space_constraint(x, pltpu.HBM) for x in operands]


def sublane(shape):
    return lax.broadcasted_iota(jnp.int32, shape, len(shape) - 2)


def flag(condition):
    return jnp.where(condition, 1.0, 0.0).astype(F32)


def traits():
    segments = lax.axis_size("segment")
    position = lax.axis_index("segment")
    decoder = flag(position >= segments // 2)
    return decoder, 1.0 - decoder, position == segments - 1


def edge_kernel(owner_in, cell_in, land_in, act, par, st, gr, coarse, grad_out, pay0, pay1, *scratch):
    act_l, act_r, st_l, st_r, par_v, gr_v, plane, held_v, owner, cell, land, arrived = scratch
    rows, breadth = gr.shape[1], gr.shape[2]
    first, final = pl.ds(0, 16), pl.ds(breadth - 16, 16)
    scalars = copies_in_parts(((owner_in, owner, 1), (cell_in, cell, 1), (land_in, land, 1)), arrived)
    copies = copies_in_parts(
        (
            (gr.at[0], gr_v, 1),
            (par.at[0], par_v, 1),
            (act.at[0, :, first], act_l, 1),
            (act.at[0, :, final], act_r, 1),
            (st.at[0, :, first], st_l, 1),
            (st.at[0, :, final], st_r, 1),
            (coarse, held_v, 1),
        ),
        arrived.at[pl.ds(3, 13)],
    )
    for copy in scalars + copies:
        copy.start()
    for copy in scalars:
        copy.wait()
    decoder, encoder, last = traits()
    groups = rows // 4
    per_row = breadth // 4
    low = sublane((8, 128)) < 4
    for group in range(groups):
        for part in range(breadth // 8):
            weigh = [jnp.where(last, land[group, 2 * part + k], 1).astype(F32) for k in range(2)]
            plane[group, 8 * part : 8 * part + 8] = jnp.where(low, weigh[0], weigh[1])

    def ids(column):
        tile = jnp.zeros((8, 128), F32)
        where = sublane((8, 128))
        for row in range(groups):
            spot = row * per_row + column
            tile = jnp.where(where == row, owner[spot].astype(F32), tile)
            tile = jnp.where(where == 4 + row, cell[spot].astype(F32), tile)
        return tile

    left_ids, right_ids = ids(0), ids(per_row - 1)
    for copy in copies:
        copy.wait()
    for row in range(rows):
        grad = gr_v[row].astype(F32) + encoder * par_v[row].astype(F32)
        grad_out[row] = (grad * plane[row // 4]).astype(BF16)

    where = sublane((rows, 8, 128))
    begin, end = slice(0, 16), slice(breadth - 16, breadth)
    grad = grad_out[:, begin].astype(F32)[:, 0:8]
    stash = st_l[...].astype(F32)[:, 0:8]
    block = act_l[...].astype(F32)[:, 0:8] + decoder * par_v[:, begin].astype(F32)[:, 0:8]
    after = jnp.where(
        where < 3, grad, jnp.where(where < 5, pltpu.roll(stash, 3, 1), pltpu.roll(block, 5, 1))
    )
    grad = grad_out[:, end].astype(F32)[:, 8:16]
    stash = st_r[...].astype(F32)[:, 8:16]
    block = act_r[...].astype(F32)[:, 8:16] + decoder * par_v[:, end].astype(F32)[:, 8:16]
    before = jnp.where(
        where == 7, grad, jnp.where(where == 6, pltpu.roll(stash, 7, 1), pltpu.roll(block, 6, 1))
    )
    even = lax.axis_index("ty") % 2 == 0
    strips = jnp.where(even, before, after).astype(BF16), jnp.where(even, after, before).astype(BF16)
    named = jnp.where(even, right_ids, left_ids), jnp.where(even, left_ids, right_ids)
    held = held_v[...].reshape(coarse.shape[0] // 8, 8, 128)
    for k, pay in enumerate((pay0, pay1)):
        pay[0:rows] = strips[k]
        pay[rows] = named[k].astype(BF16)
        pay[rows + 1 :] = held


def prepare_kernel(act, par, st, up, down, base, stash, flat_up, flat_down, *scratch):
    act_v, par_v, up_v, down_v, arrived = scratch
    tiles = (act.at[0], act_v, 1), (par.at[0], par_v, 1), (st.at[0], stash, 1)
    copies = copies_in_parts(tiles + ((up, up_v, 1), (down, down_v, 1)), arrived)
    for copy in copies:
        copy.start()
    decoder, _, _ = traits()
    for copy in copies:
        copy.wait()
    for row in range(act_v.shape[0]):
        base[row] = act_v[row].astype(F32) + decoder * par_v[row].astype(F32)
    lane_taps(up_v, flat_up)
    lane_taps(down_v, flat_down)


def side_rims(z0, z1, rows):
    ty = lax.axis_index("ty")
    even = ty % 2 == 0
    first, second = z0[0:rows].astype(F32), z1[0:rows].astype(F32)
    before = jnp.where(ty > 0, jnp.where(even, second, first), 0.0)
    after = jnp.where(ty < lax.axis_size("ty") - 1, jnp.where(even, first, second), 0.0)
    return before, after


def rim_kernel(z0, z1, _weights, _stash, rim):
    before, after = side_rims(z0, z1, rim.shape[0])
    rim[...] = jnp.where(sublane(rim.shape) < 5, after, before).astype(BF16)


def condition_kernel(merged, owner, cell, base, z0, z1, coarse, *rest):
    rows, breadth = base.shape[0], base.shape[1]
    groups = rows // 4
    per_row = breadth // 4
    cells = groups * per_row
    wide = LEFT + breadth
    ty = lax.axis_index("ty")
    low = sublane((8, 128)) < 4
    if merged:
        z2, pay, ext, table, plane = rest
        table[pl.ds(pl.multiple_of(ty * cells, 8), cells)] = coarse[...].astype(F32)
        others = (
            (ty ^ 1, z0[rows + 1 :].astype(F32).reshape(cells, 128)),
            (ty ^ 3, z1[rows + 1 :].astype(F32).reshape(cells, 128)),
            (ty ^ 2, z2[...].astype(F32)),
        )
        for other, value in others:
            table[pl.ds(pl.multiple_of(other * cells, 8), cells)] = value
    else:
        st, grad_own, pay, pay1, full, table, plane = rest
        ext = full.at[2]
        table[...] = coarse[...].astype(F32)
    before, after = side_rims(z0, z1, rows + 1)

    def rim_condition(tile, valid):
        wanted = tile[rows]
        spot = wanted * cells + pltpu.roll(wanted, 4, 0)
        lanes = lax.broadcasted_iota(jnp.int32, (8, table.shape[0]), 1).astype(F32)
        spread = jnp.broadcast_to(spot[:, 0:1], lanes.shape)
        hot = jnp.where(spread == lanes, 1.0, 0.0).astype(BF16)
        named = lax.dot(hot, table[...].astype(BF16), preferred_element_type=F32)
        picked = [jnp.broadcast_to(named[row : row + 1], (8, 128))[None] for row in range(groups)]
        spread_rows = jnp.concatenate([p for p in picked for _ in range(4)], axis=0)
        return jnp.where(valid, spread_rows, 0.0)

    rim = pltpu.roll(before[0:rows], 2, 1) + rim_condition(before, ty > 0)
    ext[:, 0:8] = rim.astype(BF16)
    rim = pltpu.roll(after[0:rows], 3, 1) + rim_condition(after, ty < lax.axis_size("ty") - 1)
    ext[:, wide : wide + 8] = rim.astype(BF16)
    for group in range(groups):
        for part in range(breadth // 8):
            spots = [group * per_row + 2 * part + k for k in range(2)]
            named = [
                jnp.broadcast_to(table[pl.ds(owner[s] * cells + cell[s], 1)], (8, 128)) for s in spots
            ]
            plane[group, 8 * part : 8 * part + 8] = jnp.where(low, named[0], named[1])
    for row in range(rows):
        ext[row, LEFT:wide] = (base[row] + plane[row // 4]).astype(BF16)

    upper = lax.axis_index("tx") % 2 == 0
    if merged:
        near = sublane((8, 128)) < 5
        for k in range(3):
            top, bottom = min(k, 1), rows - 3 + k
            for part in range(breadth // 8):
                cols = pl.ds(LEFT + 8 * part, 8)
                pay[9 * k + part] = jnp.where(upper, ext[bottom, cols], ext[top, cols])
            tiles = [
                jnp.where(near, ext[row, pl.ds(wide, 8)], ext[row, pl.ds(0, 8)]) for row in (top, bottom)
            ]
            pay[9 * k + breadth // 8] = jnp.where(upper, tiles[1], tiles[0])
        return
    full[0, :, 0:8] = before[0:rows].astype(BF16)
    full[1, :, 0:8] = pltpu.roll(before[0:rows], 1, 1).astype(BF16)
    full[0, :, wide : wide + 8] = after[0:rows].astype(BF16)
    full[1, :, wide : wide + 8] = pltpu.roll(after[0:rows], 5, 1).astype(BF16)
    full[0, :, LEFT:wide] = grad_own[...]
    full[1, :, LEFT:wide] = st[...]
    leading = [(0, 0), (0, 1), (0, 2), (1, 0), (1, 1), (2, 0), (2, 1)]
    closing = [(0, rows - 1), (1, rows - 1), (2, rows - 3), (2, rows - 2), (2, rows - 1)]
    closing = closing + closing[-1:] * 2
    for k in range(STRIP_ROWS):
        top, bottom = full[leading[k]], full[closing[k]]
        pay[k] = jnp.where(upper, bottom, top)
        pay1[k] = jnp.where(upper, top, bottom)


def rims(y0, y1):
    tx = lax.axis_index("tx")
    upper = tx % 2 == 0
    before_ok, after_ok = tx > 0, tx < lax.axis_size("tx") - 1

    def row(valid, from_first, k):
        value = jnp.where(from_first, y0[k].astype(F32), y1[k].astype(F32))
        return jnp.where(valid, value, 0.0)

    before = lambda k: row(before_ok, jnp.logical_not(upper), k)
    after = lambda k: row(after_ok, upper, k)
    return before, after


def spread_taps(field, taps, odd_taps, count, first):
    width = taps.shape[1]
    for row in range(count):
        target = taps if row % 2 == 0 else odd_taps
        for tap in range(3):
            value = field[row, pl.ds(first + tap, width, stride=2), :]
            target[row // 2, :, tap * 128 : tap * 128 + 128] = value.astype(BF16)


def three_rows(even_taps, odd_taps, count):
    wide = 3 * 128
    whole = lambda ref, a: ref[a : a + count].reshape(count * ref.shape[1], wide)
    return whole(even_taps, 0), whole(odd_taps, 0), whole(even_taps, 1)


def lower(even_taps, odd_taps, count, down):
    views = three_rows(even_taps, odd_taps, count)
    wide = 3 * 128
    total = None
    for a in range(3):
        term = lax.dot_general(
            views[a],
            down[:, a * wide : a * wide + wide],
            (((1,), (1,)), ((), ())),
            preferred_element_type=F32,
        )
        total = term if total is None else total + term
    return total


def lane_taps(taps, flat):
    for tap in range(9):
        flat[:, tap * 128 : tap * 128 + 128] = taps[tap]


def window_sums(plane_of, count, sums):
    previous = None
    for row in range(2 * count + 2):
        plane = [plane_of(row, k) for k in range(4)]
        current = [plane[2] + plane[3], plane[1] + plane[2], plane[0] + plane[1]]
        if row > 0:
            for a in range(3):
                double = row - 3 + a
                if double % 2 == 0 and 0 <= double // 2 < count:
                    for b in range(3):
                        lanes = slice((3 * a + b) * 128, (3 * a + b) * 128 + 128)
                        sums[double // 2, :, lanes] = (previous[b] + current[b]).astype(sums.dtype)
        previous = current


def sweep(wide, field, even_taps, odd_taps, sums, flat_up, down, count, fill_stash, fill_grad):
    field[:, wide:] = jnp.zeros((field.shape[0], field.shape[1] - wide, 128), F32)
    fill_stash()
    spread_taps(field, even_taps, odd_taps, 2 * count + 1, LEFT - 1)
    pre_back = lower(even_taps, odd_taps, count, down)
    logistic = 0.5 + 0.5 * jnp.tanh(0.5 * pre_back)
    reduced = pre_back * logistic
    slope = logistic * (1.0 + pre_back * (1.0 - logistic))
    fill_grad()
    window_sums(lambda row, k: field[row, pl.ds(LEFT - 1 + k, PAD, stride=2), :], count, sums)
    windows = sums[...].reshape(count * PAD, 9 * 128)
    raised = lax.dot_general(windows, flat_up[...], (((1,), (1,)), ((), ())), preferred_element_type=F32)
    return reduced.astype(BF16), raised * slope


def places(count, depth):
    shape = (count, PAD, depth)
    row = lax.broadcasted_iota(jnp.int32, shape, 0).reshape(count * PAD, depth)
    col = lax.broadcasted_iota(jnp.int32, shape, 1).reshape(count * PAD, depth)
    return row, col


def flatten_rows(d0, d1, flat, start):
    pairs = d0.shape[0] // 2
    left_even, left_odd = d0[pl.ds(0, pairs, stride=2)], d0[pl.ds(1, pairs, stride=2)]
    right_even, right_odd = d1[pl.ds(0, pairs, stride=2)], d1[pl.ds(1, pairs, stride=2)]
    near = lax.broadcasted_iota(jnp.int32, left_even.shape, 1) < 64
    turned = pltpu.roll(left_odd, 64, 1)
    flat[pl.ds(start, pairs, stride=3)] = left_even
    flat[pl.ds(start + 1, pairs, stride=3)] = jnp.where(near, right_even, turned)
    flat[pl.ds(start + 2, pairs, stride=3)] = jnp.where(near, turned, pltpu.roll(right_odd, 64, 1))


def across(left, right):
    return lax.dot_general(left, right, (((0,), (0,)), ((), ())), preferred_element_type=F32)


def grads_kernel(
    ext, y0, y1, flat_up, flat_down, in_grad, up_flat, down_flat, field, even_taps, odd_taps, sums, d0, d1, products, fine
):
    rows = ext.shape[1]
    wide = ext.shape[2]
    half_rows, half_cols = rows // 2, (wide - 16) // 2
    count = half_rows + 1
    before, after = rims(y0, y1)
    tx, ty = lax.axis_index("tx"), lax.axis_index("ty")
    has_below, has_right = tx < lax.axis_size("tx") - 1, ty < lax.axis_size("ty") - 1

    def fill(kind, top, bottom):
        field[0, 0:wide] = before(top)
        for row in range(rows):
            field[row + 1, 0:wide] = ext[kind, row].astype(F32)
        for k, spot in enumerate(bottom):
            field[rows + 1 + k, 0:wide] = after(spot)

    reduced, pre_grad = sweep(
        wide,
        field,
        even_taps,
        odd_taps,
        sums,
        flat_up,
        flat_down,
        count,
        lambda: fill(1, 1, (3, 4)),
        lambda: fill(0, 0, (0, 1, 2)),
    )
    depth = reduced.shape[1]
    row, col = places(count, depth)
    inside = ((row < half_rows) | has_below) & ((col < half_cols) | (has_right & (col == half_cols)))
    pre_grad = jnp.where(inside, pre_grad, 0.0).astype(BF16).reshape(count, PAD, depth)
    base = lambda row_id: ext[0, row_id, LEFT : wide - 8]
    moved = lax.dot(pre_grad.reshape(count * PAD, depth), flat_down[...], preferred_element_type=F32)
    products[...] = moved.reshape(count, PAD, 9 * 128)
    combine_fine(products, base, fine, in_grad)
    cells = half_rows * half_cols
    own = lambda value: value[:half_rows, :half_cols].reshape(cells, value.shape[-1])
    reduced, own_grad = own(reduced.reshape(count, PAD, depth)), own(pre_grad)
    terms = across(reduced, own(sums))
    for tap in range(9):
        up_flat[tap * depth : tap * depth + depth] = terms[:, tap * 128 : tap * 128 + 128]
    span = 3 * 128
    for a, view in enumerate((even_taps, odd_taps, even_taps)):
        taps = view[a // 2 : a // 2 + half_rows, 0:half_cols].reshape(cells, span)
        term = across(taps, own_grad)
        d0[a * span : a * span + span] = term[:, 0:128]
        d1[a * span : a * span + span, 0:64] = term[:, 128:192]
    flatten_rows(d0, d1, down_flat, 0)


def paired_kernel(
    st, grad, st_far, grad_far, rim, rim_far, flat_up, flat_down, value, far, in_grad, *rest
):
    own_sum, send1, send2, send3, field, taps, sums, d0, d1, up_flat = rest[:10]
    grads, products, fine, edge_taps, edge_sums, grad_field = rest[10:]
    rows, breadth = grad.shape[0], grad.shape[1]
    wide = breadth + 16
    count, half_rows, half_cols = rows, rows // 2, breadth // 2
    cells = count * half_cols
    edge_count = half_rows + 1
    tx, ty = lax.axis_index("tx"), lax.axis_index("ty")
    has_below = tx < lax.axis_size("tx") - 1
    has_right = ty < lax.axis_size("ty") - 1
    first_row = rows * tx

    def fill(field, here_rows, there_rows, turn_before, turn_after):
        blank = jnp.zeros((wide, 128), F32)
        field[0, 0:wide] = blank
        field[2 * rows + 1, 0:wide] = blank
        here, there = 1 + rows * tx, 1 + rows * (1 - tx)
        for start, source, sides in ((here, here_rows, rim), (there, there_rows, rim_far)):
            for row in range(rows):
                field[start + row, LEFT : LEFT + breadth] = source(row).astype(F32)
            sides = sides[...].astype(F32)
            turned = lambda turn: pltpu.roll(sides, turn, 1) if turn else sides
            field[pl.ds(start, rows), 0:8] = turned(turn_before)
            field[pl.ds(start, rows), LEFT + breadth : wide] = turned(turn_after)

    def slopes(pre_back):
        logistic = 0.5 + 0.5 * jnp.tanh(0.5 * pre_back)
        return logistic, logistic * (1.0 + pre_back * (1.0 - logistic))

    def full_taps(values, weights):
        return lax.dot_general(values, weights[...], (((1,), (1,)), ((), ())), preferred_element_type=F32)

    edge = lambda field, row, k: field[first_row + row, pl.ds(LEFT - 1 + k + breadth, 8, stride=2), :]
    flat_edge = lambda ref: ref[...].reshape(edge_count * 8, 9 * 128).astype(BF16)

    for each in (field, grad_field):
        each[:, wide:] = jnp.zeros((each.shape[0], each.shape[1] - wide, 128), F32)
    fill(field, lambda row: st[row], lambda row: st_far[0, row], 1, 5)
    spread_taps(field, taps.at[:, :, 0:384], taps.at[:, :, 384:768], 2 * count + 1, LEFT - 1)
    for p in range(edge_count):
        for tap in range(9):
            edge_taps[p, :, tap * 128 : tap * 128 + 128] = edge(field, 2 * p + tap // 3, tap % 3)
    pre_back = full_taps(taps[0:count].reshape(cells, 768), flat_down.at[:, 0:768])
    pre_back += full_taps(taps[1 : count + 1, :, 0:384].reshape(cells, 384), flat_down.at[:, 768:1152])
    logistic, slope = slopes(pre_back)
    reduced = (pre_back * logistic).astype(BF16)
    edge_slope = slopes(full_taps(flat_edge(edge_taps), flat_down))[1]

    fill(grad_field, lambda row: grad[row], lambda row: grad_far[row], 0, 0)
    window_sums(lambda row, k: grad_field[row, pl.ds(LEFT - 1 + k, half_cols, stride=2), :], count, sums)
    window_sums(lambda row, k: edge(grad_field, row, k), edge_count, edge_sums)
    depth = reduced.shape[1]
    coupled = (full_taps(sums[...].reshape(cells, 9 * 128), flat_up) * slope).astype(BF16)
    edge_shape = (edge_count, 8, depth)
    row = lax.broadcasted_iota(jnp.int32, edge_shape, 0).reshape(edge_count * 8, depth)
    inside = has_right & ((row < half_rows) | has_below)
    edge_grad = jnp.where(inside, full_taps(flat_edge(edge_sums), flat_up) * edge_slope, 0.0).astype(BF16)
    half = up_flat.shape[0] - depth // 2
    lanes = pl.ds(pl.multiple_of(tx * 512, 128), 640)
    terms = across(reduced, sums[:, :, lanes].reshape(cells, 640))
    for tap in range(5):
        up_flat[tap * depth : tap * depth + depth] = terms[:, tap * 128 : tap * 128 + 128]
    span = 3 * 128
    outer = across(taps[pl.ds(tx, count), :, 0:span].reshape(cells, span), coupled)
    middle = across(taps[0:count, :, span : 2 * span].reshape(cells, span), coupled)
    outer_at = pl.multiple_of(tx * (span // 2), 8)
    middle_at = pl.multiple_of((1 - tx) * span, 8)
    middle_half = jnp.where(tx == 0, middle[0 : span // 2], middle[span // 2 : span])
    d0[pl.ds(outer_at, span)] = outer[:, 0:128]
    d1[pl.ds(outer_at, span), 0:64] = outer[:, 128:192]
    d0[pl.ds(middle_at, span // 2)] = middle_half[:, 0:128]
    d1[pl.ds(middle_at, span // 2), 0:64] = middle_half[:, 128:192]
    piece, tall = half // 4, d0.shape[0] // 4
    up_start = tx * (depth // 2)
    near = lax.broadcasted_iota(jnp.int32, (tall // 2, 128), 1) < 64
    for distance, target in enumerate((own_sum, send1, send2, send3)):
        peer = ty ^ distance
        start = pl.multiple_of(peer * tall, 8)
        later = pl.multiple_of(peer * tall + tall // 2, 8)
        rests = jnp.where(near, d1[pl.ds(start, tall // 2)], pltpu.roll(d1[pl.ds(later, tall // 2)], 64, 1))
        parts = [up_flat[pl.ds(pl.multiple_of(up_start + peer * piece, 8), piece)], d0[pl.ds(start, tall)], rests]
        target[...] = jnp.concatenate(parts, axis=0).astype(target.dtype)
    grads[0:count] = coupled.reshape(count, half_cols, depth)
    grads[count] = jnp.zeros((half_cols, depth), BF16)
    own_rows = grads[pl.ds(half_rows * tx, edge_count)].reshape(edge_count * half_cols, depth)
    moved = lax.dot(own_rows, flat_down[...], preferred_element_type=F32)
    products[:, 0:half_cols] = moved.reshape(edge_count, half_cols, 9 * 128)
    moved = lax.dot(edge_grad, flat_down[...], preferred_element_type=F32)
    products[:, half_cols:] = moved.reshape(edge_count, 8, 9 * 128)
    combine_fine(products, lambda row: grad[row], fine, in_grad)
    for row in range(far.shape[0]):
        here = row + (rows - far.shape[0]) * tx
        far[row] = relay_choices(value[here], in_grad[here])[1]


def combine_fine(products, base, fine, target):
    half_rows, half_cols = fine.shape[0] // 2, fine.shape[1] // 2

    def part(p, a, b, offset):
        tap = 3 * a + b
        return products[p, offset : offset + half_cols, tap * 128 : tap * 128 + 128]

    for p in range(half_rows):
        fine[2 * p, pl.ds(0, half_cols, stride=2), :] = part(p, 1, 1, 0)
        fine[2 * p, pl.ds(1, half_cols, stride=2), :] = part(p, 1, 2, 0) + part(p, 1, 0, 1)
        fine[2 * p + 1, pl.ds(0, half_cols, stride=2), :] = part(p, 2, 1, 0) + part(p + 1, 0, 1, 0)
        fine[2 * p + 1, pl.ds(1, half_cols, stride=2), :] = (
            part(p, 2, 2, 0) + part(p, 2, 0, 1) + part(p + 1, 0, 2, 0) + part(p + 1, 0, 0, 1)
        )
    for row in range(fine.shape[0]):
        target[row] = (base(row).astype(F32) + fine[row]).astype(BF16)


def raise_rows(field, even_taps, odd_taps, products, flat_up, flat_down, count, first, valid):
    spread_taps(field, even_taps, odd_taps, 2 * count + 1, first)
    pre_down = lower(even_taps, odd_taps, count, flat_down)
    reduced = pre_down * (0.5 + 0.5 * jnp.tanh(0.5 * pre_down))
    row, col = places(count, reduced.shape[1])
    reduced = jnp.where(valid(row, col), reduced, 0.0).astype(BF16)
    raised = lax.dot(reduced, flat_up[...], preferred_element_type=F32)
    products[...] = raised.reshape(count, PAD, 9 * 128)


def fine_row(products, mixed, target, picks):
    half_cols = target.shape[0] // 2
    col = []
    for b in range(3):
        terms = [
            products[q, :, (3 * a + b) * 128 : (3 * a + b) * 128 + 128]
            for a, q in enumerate(picks)
            if q is not None
        ]
        col.append(sum(terms[1:], terms[0]))
    mixed[0], mixed[1] = col[0], col[1] + col[2]
    mixed[2], mixed[3] = col[0] + col[1], col[2]
    target[pl.ds(0, half_cols, stride=2), :] = mixed[0, 0:half_cols] + mixed[1, 1 : half_cols + 1]
    target[pl.ds(1, half_cols, stride=2), :] = mixed[2, 1 : half_cols + 1] + mixed[3, 2 : half_cols + 2]


def right_edge(half_cols):
    has_right = lax.axis_index("ty") < lax.axis_size("ty") - 1
    return lambda row, col: (col <= half_cols) | has_right


def relay_choices(value, in_grad):
    position, segments = lax.axis_index("segment"), lax.axis_size("segment")
    near = jnp.where(position % 2 == 0, value, in_grad)
    return near, jnp.where(position < segments // 2, value, in_grad)


def forward_kernel(blocks, y0, y1, in_grad, flat_up, flat_down, near, far, *scratch):
    field, even_taps, odd_taps, products, mixed, fine = scratch
    rows, wide = blocks.shape[1], blocks.shape[2]
    breadth = wide - 16
    half_rows, half_cols = rows // 2, breadth // 2
    has_below = lax.axis_index("tx") < lax.axis_size("tx") - 1
    before, after = rims(y0, y1)
    field[:, wide:] = jnp.zeros((field.shape[0], field.shape[1] - wide, 128), F32)
    for k in range(3):
        field[k, 0:wide] = before(2 + k)
    for row in range(rows):
        field[row + 3, 0:wide] = blocks[2, row].astype(F32)
    for k in range(2):
        field[rows + 3 + k, 0:wide] = after(5 + k)
    edge = right_edge(half_cols)
    valid = lambda row, col: ((row <= half_rows) | has_below) & edge(row, col)
    raise_rows(field, even_taps, odd_taps, products, flat_up, flat_down, half_rows + 2, LEFT - 3, valid)
    for p in range(half_rows):
        fine_row(products, mixed, fine.at[2 * p], (p, p + 1, p + 1))
        fine_row(products, mixed, fine.at[2 * p + 1], (p + 1, p + 1, p + 2))
    for row in range(rows):
        value = (blocks[2, row, LEFT : LEFT + breadth].astype(F32) + fine[row]).astype(BF16)
        near[row], far[row] = relay_choices(value, in_grad[row])


def inner_kernel(blocks, flat_up, flat_down, value, *scratch):
    field, even_taps, odd_taps, products, mixed, fine = scratch
    rows, wide = blocks.shape[0], blocks.shape[1]
    breadth = wide - 16
    half_rows, half_cols = rows // 2, breadth // 2
    field[:, wide:] = jnp.zeros((field.shape[0], field.shape[1] - wide, 128), F32)
    field[0, 0:wide] = jnp.zeros((wide, 128), F32)
    for row in range(rows):
        field[row + 1, 0:wide] = blocks[row].astype(F32)
    edge = right_edge(half_cols)
    raise_rows(field, even_taps, odd_taps, products, flat_up, flat_down, half_rows, LEFT - 3, edge)
    for p in range(half_rows):
        fine_row(products, mixed, fine.at[2 * p], (p - 1 if p else None, p, p))
        below = p + 1 if p + 1 < half_rows else None
        fine_row(products, mixed, fine.at[2 * p + 1], (p, p, below))
    for row in range(rows):
        value[row] = (blocks[row, LEFT : LEFT + breadth].astype(F32) + fine[row]).astype(BF16)


def border_kernel(blocks, y0, value, in_grad, flat_up, flat_down, near, strip, *scratch):
    field, even_taps, odd_taps, products, mixed, fine = scratch
    rows, wide = blocks.shape[0], blocks.shape[1]
    breadth = wide - 16
    half_cols = breadth // 2
    upper = lax.axis_index("tx") == 0
    field[:, wide:] = jnp.zeros((field.shape[0], field.shape[1] - wide, 128), F32)

    def far_row(k):
        tiles = [y0[(breadth // 8 + 1) * k + part].astype(F32) for part in range(breadth // 8 + 1)]
        return jnp.concatenate([tiles[-1]] + tiles, axis=0)

    own = lambda row: blocks[row].astype(F32)
    for k in range(7):
        lower_tile = far_row(k) if k < 3 else own(k - 3)
        upper_tile = own(rows - 5 + k) if k < 5 else far_row(k - 5)
        field[k, 0:wide] = jnp.where(upper, upper_tile, lower_tile)
    edge = right_edge(half_cols)
    raise_rows(field, even_taps, odd_taps, products, flat_up, flat_down, 3, LEFT - 3, edge)
    fine_row(products, mixed, fine.at[0], (0, 1, 1))
    fine_row(products, mixed, fine.at[1], (1, 1, 2))
    fine_row(products, mixed, fine.at[2], (1, 2, 2))
    repaired = [None] * 3
    for k in range(3):
        base = jnp.where(upper, own(rows - 3 + k), own(k))[LEFT : LEFT + breadth]
        added = jnp.where(upper, fine[max(k - 1, 0)], fine[k])
        repaired[k] = (base + added).astype(BF16)
        if k == 0:
            repaired[k] = jnp.where(upper, value[rows - 3], repaired[k])
        strip[k] = relay_choices(repaired[k], jnp.where(upper, in_grad[rows - 3 + k], in_grad[k]))[1]
    for row in range(rows):
        result = value[row]
        if row < 3:
            result = jnp.where(upper, result, repaired[row])
        if row >= rows - 3:
            result = jnp.where(upper, repaired[row - (rows - 3)], result)
        near[row] = relay_choices(result, in_grad[row])[0]


def final_kernel(
    scaling, near, far, strip, own, first, second, third, act_out, grad_out, partner_out, up_sum, down_sum, d0, d1
):
    rows, border = near.shape[0], strip.shape[0]
    position, last = lax.axis_index("segment"), lax.axis_size("segment") - 1
    upper = lax.axis_index("tx") == 0
    odd = position % 2 == 1
    for row in range(rows):
        from_upper = far[row] if row < rows - border else strip[row - (rows - border)]
        from_lower = strip[row] if row < border else far[row - border]
        from_far = jnp.where(upper, from_upper, from_lower)
        blank = jnp.zeros_like(from_far)
        partner_out[0, row] = from_far
        act_out[0, row] = jnp.where(position == 0, blank, jnp.where(odd, near[row], from_far))
        grad_out[0, row] = jnp.where(position == last, blank, jnp.where(odd, from_far, near[row]))
    total = own[...] + first[...].astype(F32) + second[...].astype(F32) + third[...].astype(F32)
    piece = up_sum.shape[0]
    up_sum[...] = total[0:piece] * scaling
    tall = d0.shape[0]
    rests = total[piece + tall :] * scaling
    d0[...] = total[piece : piece + tall] * scaling
    d1[0 : tall // 2] = rests
    d1[tall // 2 :] = pltpu.roll(rests, 64, 1)
    flatten_rows(d0, d1, down_sum, 0)


def swaps(axis):
    size = lax.axis_size(axis)
    pairs = [(i, i + 1) for i in range(0, size - 1, 2)]
    other = [(i, i + 1) for i in range(1, size - 1, 2)]
    both = lambda pairs: pairs + [(j, i) for i, j in pairs]
    return both(pairs), both(other)


def crossed(axis, distance):
    return [(i, i ^ distance) for i in range(lax.axis_size(axis))]


def shape(dims, kind):
    return jax.ShapeDtypeStruct(tuple(dims), kind)


def local(
    act_in,
    partner_in,
    stashed,
    grad_in,
    down_weights,
    up_weights,
    coarse,
    nest_owner,
    nest_cell,
    land_weight,
):
    height, breadth, channels = act_in.shape[1:]
    depth = down_weights.shape[-1]
    half_rows = height // 2
    n_tx, n_ty = lax.axis_size("tx"), lax.axis_size("ty")
    position, segments = lax.axis_index("segment"), lax.axis_size("segment")
    scaling = 1.0 / math.sqrt(height * breadth * n_tx * n_ty)
    down_taps = jnp.swapaxes(down_weights, 3, 4).reshape(9, depth, channels)
    up_taps = up_weights.reshape(9, depth, channels)

    owners = nest_owner.reshape(-1)
    tile = shape((height, breadth, channels), BF16)
    pay = shape((height + 1 + coarse.shape[0] // 8, 8, channels), BF16)
    merged = n_ty == 4 and n_tx == 2
    if merged:
        st_far = lax.ppermute(stashed, "tx", crossed("tx", 1))
    side = pltpu.VMEM((height, 16, channels), BF16)
    full = pltpu.VMEM((height, breadth, channels), BF16)
    grad_own, z_pay0, z_pay1 = call(
        edge_kernel,
        (tile, pay, pay),
        [HBM] * 8,
        [side] * 4
        + [full] * 2
        + [pltpu.VMEM((height // 4, breadth, channels), F32), pltpu.VMEM(coarse.shape, BF16)]
        + [pltpu.SMEM(scalars.shape, jnp.int32) for scalars in (owners, nest_cell, land_weight)]
        + [pltpu.SemaphoreType.DMA((16,))],
        flops=1000,
        moved=1000,
    )(*in_hbm(owners, nest_cell, land_weight, act_in, partner_in, stashed, grad_in, coarse))
    pairs, others = swaps("ty")
    if merged:
        others = crossed("ty", 3)
        grad_far = lax.ppermute(grad_own, "tx", crossed("tx", 1))
    z0 = lax.ppermute(z_pay0, "ty", pairs)
    z1 = lax.ppermute(z_pay1, "ty", others)
    if merged:
        table_parts = (coarse, lax.ppermute(coarse, "ty", crossed("ty", 2)))
    else:
        table_parts = (lax.all_gather(coarse, "ty", tiled=True),)
    flat = shape((depth, 9 * channels), BF16)
    taps_room = pltpu.VMEM((9, depth, channels), BF16)
    base, stash, flat_up, flat_down = call(
        prepare_kernel,
        (shape((height, breadth, channels), F32), tile, flat, flat),
        [HBM] * 5,
        [full, full, taps_room, taps_room, pltpu.SemaphoreType.DMA((30,))],
        flops=1000,
        moved=1000,
    )(*in_hbm(act_in, partner_in, stashed, up_taps, down_taps))
    operands = (base, z0, z1, *table_parts)
    rooms = [
        pltpu.VMEM((n_ty * coarse.shape[0], channels), F32),
        pltpu.VMEM((height // 4, breadth, channels), F32),
    ]
    pairs, others = swaps("tx")
    if merged:
        rim = call(
            rim_kernel,
            shape((height, 8, channels), BF16),
            [VMEM] * 2 + [pl.BlockSpec(memory_space=pl.ANY)] * 2,
            flops=1000,
            moved=1000,
        )(z0, z1, flat_up, st_far)
        rim_far = lax.ppermute(rim, "tx", pairs)
        pay, blocks = call(
            functools.partial(condition_kernel, True),
            (shape((3 * (breadth // 8 + 1), 8, channels), BF16), shape((height, breadth + 16, channels), BF16)),
            [SMEM] * 2 + [VMEM] * len(operands),
            rooms,
            flops=2_000_000_000,
            moved=1000,
        )(owners, nest_cell, *operands)
        ys = [lax.ppermute(pay, "tx", pairs)]
    else:
        pay = shape((STRIP_ROWS, breadth + 16, channels), BF16)
        *pays, blocks = call(
            functools.partial(condition_kernel, False),
            (pay, pay, shape((3, height, breadth + 16, channels), BF16)),
            [SMEM] * 2 + [VMEM] * (len(operands) + 2),
            rooms,
        )(owners, nest_cell, *operands, stash, grad_own)
        ys = [lax.ppermute(pays[0], "tx", pairs), lax.ppermute(pays[1], "tx", others) if others else pays[1]]

    wide = 2 * PAD + 16
    rows_flat = 9 * depth

    def tap_rooms(count):
        room = pltpu.VMEM((count + 1, PAD, 3 * channels), BF16)
        return [pltpu.VMEM((2 * count + 2, wide, channels), F32), room, room]

    fine = pltpu.VMEM((height, breadth, channels), F32)
    products = lambda count: pltpu.VMEM((count, PAD, 9 * channels), F32)
    forward_rooms = lambda count: tap_rooms(count) + [
        products(count),
        pltpu.VMEM((4, PAD, channels), F32),
        fine,
    ]
    if merged:
        value = call(
            inner_kernel,
            tile,
            [VMEM] * 3,
            forward_rooms(half_rows),
            flops=1_000,
            moved=1000,
        )(blocks, flat_up, flat_down)
        piece = rows_flat // (n_tx * n_ty)
        part = shape((2 * piece, channels), BF16)
        far, in_grad, own_sum, *sends = call(
            paired_kernel,
            (shape((height - BORDER, breadth, channels), BF16), tile, shape((2 * piece, channels), F32), part, part, part),
            [VMEM] * 9,
            [
                pltpu.VMEM((2 * height + 4, wide, channels), F32),
                pltpu.VMEM((height + 1, breadth // 2, 6 * channels), BF16),
                pltpu.VMEM((height, breadth // 2, 9 * channels), BF16),
                pltpu.VMEM((9 * channels // 2, 128), F32),
                pltpu.VMEM((9 * channels // 2, 128), F32),
                pltpu.VMEM((5 * depth, channels), F32),
                pltpu.VMEM((height + 1, breadth // 2, depth), BF16),
                pltpu.VMEM((half_rows + 1, breadth // 2 + 8, 9 * channels), F32),
                fine,
                pltpu.VMEM((half_rows + 1, 8, 9 * channels), F32),
                pltpu.VMEM((half_rows + 1, 8, 9 * channels), F32),
                pltpu.VMEM((2 * height + 4, wide, channels), F32),
            ],
            flops=5_000_000_000,
            moved=4_000_000,
        )(stash, grad_own, st_far, grad_far, rim, rim_far, flat_up, flat_down, value)
    else:
        whole = shape((rows_flat, channels), F32)
        in_grad, up_flat, down_flat = call(
            grads_kernel,
            (tile, whole, whole),
            [VMEM] * 5,
            tap_rooms(half_rows + 1)
            + [
                pltpu.VMEM((half_rows + 1, PAD, 9 * channels), BF16),
                pltpu.VMEM((9 * channels, 128), F32),
                pltpu.VMEM((9 * channels, 128), F32),
                products(half_rows + 1),
                fine,
            ],
            flops=500_000_000,
            moved=4_000_000,
        )(blocks, *ys, flat_up, flat_down)
        pooled = lambda flat: lax.psum_scatter(
            flat.reshape(-1) * scaling, ("tx", "ty"), scatter_dimension=0, tiled=True
        )[None]
        down_sum, up_sum = pooled(down_flat), pooled(up_flat)

    mirror = [(i, segments - 1 - i) for i in range(segments)]
    if merged:
        ys = passed_on(ys, 2_000_000_000)
        near, strip = call(
            border_kernel,
            (tile, shape((BORDER, breadth, channels), BF16)),
            [VMEM] * 6,
            forward_rooms(3),
            flops=600_000_000,
            moved=4_000_000,
        )(blocks, ys[0], value, in_grad, flat_up, flat_down)
        from_far = lax.ppermute(far, "segment", mirror)
        from_strip = lax.ppermute(strip, "segment", mirror)
        from_near = lax.ppermute(near, "segment", crossed("segment", 1))
        arrived = [lax.ppermute(sends[d - 1], "ty", crossed("ty", d)) for d in (2, 1, 3)]
        arrived = passed_on(arrived[:1], 800_000_000) + arrived[1:]
        (from_far,) = passed_on([from_far], 100_000_000, arrived[:1])
        arrived = arrived[:1] + passed_on(arrived[1:], 3_000_000_000, [from_far])
        summed = shape((piece, channels), F32)
        act_out, grad_out, partner_out, up_sum, down_sum = call(
            functools.partial(final_kernel, scaling),
            (shape(act_in.shape, BF16),) * 3 + (summed, summed),
            [VMEM] * 7,
            [pltpu.VMEM((2 * piece // 3, 128), F32)] * 2,
            flops=1_000,
            moved=1000,
        )(from_near, from_far, from_strip, own_sum, *arrived)
        return act_out, grad_out, partner_out, down_sum.reshape(1, -1), up_sum.reshape(1, -1)
    near, far = call(
        forward_kernel,
        (tile, tile),
        [VMEM] * 6,
        forward_rooms(half_rows + 2),
        flops=600_000_000,
        moved=4_000_000,
    )(blocks, *ys, in_grad, flat_up, flat_down)
    from_far = lax.ppermute(far, "segment", mirror)
    from_near = lax.ppermute(near, "segment", crossed("segment", 1))
    blank = jnp.zeros_like(from_near)
    odd = position % 2 == 1
    act_out = jnp.where(position == 0, blank, jnp.where(odd, from_near, from_far))
    grad_out = jnp.where(position == segments - 1, blank, jnp.where(odd, from_far, from_near))
    return (act_out[None], grad_out[None], from_far[None], down_sum, up_sum)


def solution(mesh):
    tile = P("segment", "tx", "ty", None)
    weights = P("segment", None, None, None, None)
    grads = P("segment", ("tx", "ty"))
    rows = P(("tx", "ty"))
    return jax.shard_map(
        local,
        mesh=mesh,
        in_specs=(tile,) * 4 + (weights,) * 2 + (P(("tx", "ty"), None),) * 2 + (rows, P("tx", "ty")),
        out_specs=(tile,) * 3 + (grads,) * 2,
        check_vma=False,
    )
```

```python
import functools
import math

import jax
import jax.numpy as jnp
from jax import lax
from jax.experimental import pallas as pl
from jax.experimental.pallas import tpu as pltpu
from jax.sharding import PartitionSpec as P

F32 = jnp.float32
BF16 = jnp.bfloat16
VMEM = pl.BlockSpec(memory_space=pltpu.VMEM)
SMEM = pl.BlockSpec(memory_space=pltpu.SMEM)
HBM = pl.BlockSpec(memory_space=pltpu.HBM)
LEFT = 8
PAD = 48
BORDER = 3
STRIP_ROWS = 7


def call(body, out_shape, in_specs, scratch=(), flops=0, moved=0, limit=24, out_specs=None, aliases=()):
    out_specs = out_specs or jax.tree.map(lambda _: VMEM, out_shape)
    return pl.pallas_call(
        body,
        out_shape=out_shape,
        in_specs=in_specs,
        out_specs=out_specs,
        scratch_shapes=list(scratch),
        input_output_aliases=dict(aliases),
        compiler_params=pltpu.CompilerParams(vmem_limit_bytes=limit * 1024 * 1024),
        cost_estimate=pl.CostEstimate(flops=flops, bytes_accessed=moved, transcendentals=0),
    )


def passed_on(arrays, flops, after=()):
    here = [pl.BlockSpec(memory_space=pl.ANY)] * len(arrays)
    return list(call(
        lambda *refs: None,
        tuple(jax.ShapeDtypeStruct(x.shape, x.dtype) for x in arrays),
        here + [pl.BlockSpec(memory_space=pl.ANY)] * len(after),
        flops=flops,
        moved=1000,
        out_specs=tuple(here),
        aliases=[(k, k) for k in range(len(arrays))],
    )(*arrays, *after))


def copies_in_parts(pairs, arrived):
    copies = []
    for source, target, parts in pairs:
        length = source.shape[0] // parts
        for part in range(parts):
            rows = pl.ds(part * length, length)
            views = (source.at[rows], target.at[rows]) if parts > 1 else (source, target)
            copies.append(pltpu.make_async_copy(*views, arrived.at[len(copies)]))
    return copies


def in_hbm(*operands):
    return [pltpu.with_memory_space_constraint(x, pltpu.HBM) for x in operands]


def sublane(shape):
    return lax.broadcasted_iota(jnp.int32, shape, len(shape) - 2)


def flag(condition):
    return jnp.where(condition, 1.0, 0.0).astype(F32)


def traits():
    segments = lax.axis_size("segment")
    position = lax.axis_index("segment")
    decoder = flag(position >= segments // 2)
    return decoder, 1.0 - decoder, position == segments - 1


def edge_kernel(owner_in, cell_in, land_in, act, par, st, gr, coarse, grad_out, pay0, pay1, *scratch):
    act_l, act_r, st_l, st_r, par_v, gr_v, plane, held_v, owner, cell, land, arrived = scratch
    rows, breadth = gr.shape[1], gr.shape[2]
    first, final = pl.ds(0, 16), pl.ds(breadth - 16, 16)
    scalars = copies_in_parts(((owner_in, owner, 1), (cell_in, cell, 1), (land_in, land, 1)), arrived)
    copies = copies_in_parts(
        (
            (gr.at[0], gr_v, 1),
            (par.at[0], par_v, 1),
            (act.at[0, :, first], act_l, 1),
            (act.at[0, :, final], act_r, 1),
            (st.at[0, :, first], st_l, 1),
            (st.at[0, :, final], st_r, 1),
            (coarse, held_v, 1),
        ),
        arrived.at[pl.ds(3, 13)],
    )
    for copy in scalars + copies:
        copy.start()
    for copy in scalars:
        copy.wait()
    decoder, encoder, last = traits()
    groups = rows // 4
    per_row = breadth // 4
    low = sublane((8, 128)) < 4
    for group in range(groups):
        for part in range(breadth // 8):
            weigh = [jnp.where(last, land[group, 2 * part + k], 1).astype(F32) for k in range(2)]
            plane[group, 8 * part : 8 * part + 8] = jnp.where(low, weigh[0], weigh[1])

    def ids(column):
        tile = jnp.zeros((8, 128), F32)
        where = sublane((8, 128))
        for row in range(groups):
            spot = row * per_row + column
            tile = jnp.where(where == row, owner[spot].astype(F32), tile)
            tile = jnp.where(where == 4 + row, cell[spot].astype(F32), tile)
        return tile

    left_ids, right_ids = ids(0), ids(per_row - 1)
    for copy in copies:
        copy.wait()
    for row in range(rows):
        grad = gr_v[row].astype(F32) + encoder * par_v[row].astype(F32)
        grad_out[row] = (grad * plane[row // 4]).astype(BF16)

    where = sublane((rows, 8, 128))
    begin, end = slice(0, 16), slice(breadth - 16, breadth)
    grad = grad_out[:, begin].astype(F32)[:, 0:8]
    stash = st_l[...].astype(F32)[:, 0:8]
    block = act_l[...].astype(F32)[:, 0:8] + decoder * par_v[:, begin].astype(F32)[:, 0:8]
    after = jnp.where(
        where < 3, grad, jnp.where(where < 5, pltpu.roll(stash, 3, 1), pltpu.roll(block, 5, 1))
    )
    grad = grad_out[:, end].astype(F32)[:, 8:16]
    stash = st_r[...].astype(F32)[:, 8:16]
    block = act_r[...].astype(F32)[:, 8:16] + decoder * par_v[:, end].astype(F32)[:, 8:16]
    before = jnp.where(
        where == 7, grad, jnp.where(where == 6, pltpu.roll(stash, 7, 1), pltpu.roll(block, 6, 1))
    )
    even = lax.axis_index("ty") % 2 == 0
    strips = jnp.where(even, before, after).astype(BF16), jnp.where(even, after, before).astype(BF16)
    named = jnp.where(even, right_ids, left_ids), jnp.where(even, left_ids, right_ids)
    held = held_v[...].reshape(coarse.shape[0] // 8, 8, 128)
    for k, pay in enumerate((pay0, pay1)):
        pay[0:rows] = strips[k]
        pay[rows] = named[k].astype(BF16)
        pay[rows + 1 :] = held


def prepare_kernel(act, par, st, up, down, base, stash, flat_up, flat_down, *scratch):
    act_v, par_v, up_v, down_v, arrived = scratch
    tiles = (act.at[0], act_v, 1), (par.at[0], par_v, 1), (st.at[0], stash, 1)
    copies = copies_in_parts(tiles + ((up, up_v, 1), (down, down_v, 1)), arrived)
    for copy in copies:
        copy.start()
    decoder, _, _ = traits()
    for copy in copies:
        copy.wait()
    for row in range(act_v.shape[0]):
        base[row] = act_v[row].astype(F32) + decoder * par_v[row].astype(F32)
    lane_taps(up_v, flat_up)
    lane_taps(down_v, flat_down)


def side_rims(z0, z1, rows):
    ty = lax.axis_index("ty")
    even = ty % 2 == 0
    first, second = z0[0:rows].astype(F32), z1[0:rows].astype(F32)
    before = jnp.where(ty > 0, jnp.where(even, second, first), 0.0)
    after = jnp.where(ty < lax.axis_size("ty") - 1, jnp.where(even, first, second), 0.0)
    return before, after


def rim_kernel(z0, z1, _weights, _stash, rim, pack):
    before, after = side_rims(z0, z1, rim.shape[0])
    whole = jnp.where(sublane(rim.shape) < 5, after, before)
    rim[...] = whole.astype(BF16)
    rows, half = rim.shape[0], rim.shape[0] // 2
    turned = pltpu.roll(whole, 4, 1)
    spot = sublane((half, 8, 128))
    first = jnp.where(spot < 2, whole[:half], turned[:half])
    second = jnp.where(spot < 6, turned[half:], whole[half:])
    pack[0:half] = jnp.where(spot < 4, first, second).astype(BF16)
    upper = lax.axis_index("tx") == 0
    for k in range(BORDER):
        pack[half + k] = jnp.where(upper, whole[rows - BORDER + k], whole[k]).astype(BF16)


def unpacked_rims(pack):
    packed = pack[...].astype(F32)
    half = packed.shape[0] - BORDER
    rows = 2 * half
    turned = pltpu.roll(packed, 4, 1)
    low = sublane((half, 8, 128)) < 4
    first = jnp.where(low, packed[:half], turned[:half])
    second = jnp.where(low, turned[:half], packed[:half])
    tiles = [first[k] for k in range(half)] + [second[k] for k in range(half)]
    upper = lax.axis_index("tx") == 0
    for k in range(BORDER):
        tiles[k] = jnp.where(upper, packed[half + k], tiles[k])
        here = rows - BORDER + k
        tiles[here] = jnp.where(upper, tiles[here], packed[half + k])
    return jnp.concatenate([tile[None] for tile in tiles], axis=0)


def condition_kernel(merged, owner, cell, base, z0, z1, coarse, *rest):
    rows, breadth = base.shape[0], base.shape[1]
    groups = rows // 4
    per_row = breadth // 4
    cells = groups * per_row
    wide = LEFT + breadth
    ty = lax.axis_index("ty")
    low = sublane((8, 128)) < 4
    if merged:
        z2, pay, ext, table, plane, named_here = rest
        table[pl.ds(pl.multiple_of(ty * cells, 8), cells)] = coarse[...].astype(F32)
        others = (
            (ty ^ 1, z0[rows + 1 :].astype(F32).reshape(cells, 128)),
            (ty ^ 3, z1[rows + 1 :].astype(F32).reshape(cells, 128)),
            (ty ^ 2, z2[...].astype(F32)),
        )
        for other, value in others:
            table[pl.ds(pl.multiple_of(other * cells, 8), cells)] = value
    else:
        st, grad_own, pay, pay1, full, table, plane = rest
        ext = full.at[2]
        table[...] = coarse[...].astype(F32)
    before, after = side_rims(z0, z1, rows + 1)

    def rim_condition(tile, valid):
        wanted = tile[rows]
        spot = wanted * cells + pltpu.roll(wanted, 4, 0)
        lanes = lax.broadcasted_iota(jnp.int32, (8, table.shape[0]), 1).astype(F32)
        spread = jnp.broadcast_to(spot[:, 0:1], lanes.shape)
        hot = jnp.where(spread == lanes, 1.0, 0.0).astype(BF16)
        named = lax.dot(hot, table[...].astype(BF16), preferred_element_type=F32)
        picked = [jnp.broadcast_to(named[row : row + 1], (8, 128))[None] for row in range(groups)]
        spread_rows = jnp.concatenate([p for p in picked for _ in range(4)], axis=0)
        return jnp.where(valid, spread_rows, 0.0)

    rim = pltpu.roll(before[0:rows], 2, 1) + rim_condition(before, ty > 0)
    ext[:, 0:8] = rim.astype(BF16)
    rim = pltpu.roll(after[0:rows], 3, 1) + rim_condition(after, ty < lax.axis_size("ty") - 1)
    ext[:, wide : wide + 8] = rim.astype(BF16)
    if merged:
        named_here()
    for group in range(groups):
        for part in range(breadth // 8):
            spots = [group * per_row + 2 * part + k for k in range(2)]
            named = [
                jnp.broadcast_to(table[pl.ds(owner[s] * cells + cell[s], 1)], (8, 128)) for s in spots
            ]
            plane[group, 8 * part : 8 * part + 8] = jnp.where(low, named[0], named[1])
    for row in range(rows):
        ext[row, LEFT:wide] = (base[row] + plane[row // 4]).astype(BF16)

    upper = lax.axis_index("tx") % 2 == 0
    if merged:
        near = sublane((8, 128)) < 5
        for k in range(3):
            top, bottom = min(k, 1), rows - 3 + k
            for part in range(breadth // 8):
                cols = pl.ds(LEFT + 8 * part, 8)
                pay[9 * k + part] = jnp.where(upper, ext[bottom, cols], ext[top, cols])
            tiles = [
                jnp.where(near, ext[row, pl.ds(wide, 8)], ext[row, pl.ds(0, 8)]) for row in (top, bottom)
            ]
            pay[9 * k + breadth // 8] = jnp.where(upper, tiles[1], tiles[0])
        return
    full[0, :, 0:8] = before[0:rows].astype(BF16)
    full[1, :, 0:8] = pltpu.roll(before[0:rows], 1, 1).astype(BF16)
    full[0, :, wide : wide + 8] = after[0:rows].astype(BF16)
    full[1, :, wide : wide + 8] = pltpu.roll(after[0:rows], 5, 1).astype(BF16)
    full[0, :, LEFT:wide] = grad_own[...]
    full[1, :, LEFT:wide] = st[...]
    leading = [(0, 0), (0, 1), (0, 2), (1, 0), (1, 1), (2, 0), (2, 1)]
    closing = [(0, rows - 1), (1, rows - 1), (2, rows - 3), (2, rows - 2), (2, rows - 1)]
    closing = closing + closing[-1:] * 2
    for k in range(STRIP_ROWS):
        top, bottom = full[leading[k]], full[closing[k]]
        pay[k] = jnp.where(upper, bottom, top)
        pay1[k] = jnp.where(upper, top, bottom)


def rims(y0, y1):
    tx = lax.axis_index("tx")
    upper = tx % 2 == 0
    before_ok, after_ok = tx > 0, tx < lax.axis_size("tx") - 1

    def row(valid, from_first, k):
        value = jnp.where(from_first, y0[k].astype(F32), y1[k].astype(F32))
        return jnp.where(valid, value, 0.0)

    before = lambda k: row(before_ok, jnp.logical_not(upper), k)
    after = lambda k: row(after_ok, upper, k)
    return before, after


def spread_taps(field, taps, odd_taps, count, first):
    width = taps.shape[1]
    for row in range(count):
        target = taps if row % 2 == 0 else odd_taps
        for tap in range(3):
            value = field[row, pl.ds(first + tap, width, stride=2), :]
            target[row // 2, :, tap * 128 : tap * 128 + 128] = value.astype(BF16)


def three_rows(even_taps, odd_taps, count):
    wide = 3 * 128
    whole = lambda ref, a: ref[a : a + count].reshape(count * ref.shape[1], wide)
    return whole(even_taps, 0), whole(odd_taps, 0), whole(even_taps, 1)


def lower(even_taps, odd_taps, count, down):
    views = three_rows(even_taps, odd_taps, count)
    wide = 3 * 128
    total = None
    for a in range(3):
        term = lax.dot_general(
            views[a],
            down[:, a * wide : a * wide + wide],
            (((1,), (1,)), ((), ())),
            preferred_element_type=F32,
        )
        total = term if total is None else total + term
    return total


def lane_taps(taps, flat):
    for tap in range(9):
        flat[:, tap * 128 : tap * 128 + 128] = taps[tap]


def window_sums(plane_of, count, sums):
    previous = None
    for row in range(2 * count + 2):
        plane = [plane_of(row, k) for k in range(4)]
        current = [plane[2] + plane[3], plane[1] + plane[2], plane[0] + plane[1]]
        if row > 0:
            for a in range(3):
                double = row - 3 + a
                if double % 2 == 0 and 0 <= double // 2 < count:
                    for b in range(3):
                        lanes = slice((3 * a + b) * 128, (3 * a + b) * 128 + 128)
                        sums[double // 2, :, lanes] = (previous[b] + current[b]).astype(sums.dtype)
        previous = current


def sweep(wide, field, even_taps, odd_taps, sums, flat_up, down, count, fill_stash, fill_grad):
    field[:, wide:] = jnp.zeros((field.shape[0], field.shape[1] - wide, 128), F32)
    fill_stash()
    spread_taps(field, even_taps, odd_taps, 2 * count + 1, LEFT - 1)
    pre_back = lower(even_taps, odd_taps, count, down)
    logistic = 0.5 + 0.5 * jnp.tanh(0.5 * pre_back)
    reduced = pre_back * logistic
    slope = logistic * (1.0 + pre_back * (1.0 - logistic))
    fill_grad()
    window_sums(lambda row, k: field[row, pl.ds(LEFT - 1 + k, PAD, stride=2), :], count, sums)
    windows = sums[...].reshape(count * PAD, 9 * 128)
    raised = lax.dot_general(windows, flat_up[...], (((1,), (1,)), ((), ())), preferred_element_type=F32)
    return reduced.astype(BF16), raised * slope


def places(count, depth):
    shape = (count, PAD, depth)
    row = lax.broadcasted_iota(jnp.int32, shape, 0).reshape(count * PAD, depth)
    col = lax.broadcasted_iota(jnp.int32, shape, 1).reshape(count * PAD, depth)
    return row, col


def flatten_rows(d0, d1, flat, start):
    pairs = d0.shape[0] // 2
    left_even, left_odd = d0[pl.ds(0, pairs, stride=2)], d0[pl.ds(1, pairs, stride=2)]
    right_even, right_odd = d1[pl.ds(0, pairs, stride=2)], d1[pl.ds(1, pairs, stride=2)]
    near = lax.broadcasted_iota(jnp.int32, left_even.shape, 1) < 64
    turned = pltpu.roll(left_odd, 64, 1)
    flat[pl.ds(start, pairs, stride=3)] = left_even
    flat[pl.ds(start + 1, pairs, stride=3)] = jnp.where(near, right_even, turned)
    flat[pl.ds(start + 2, pairs, stride=3)] = jnp.where(near, turned, pltpu.roll(right_odd, 64, 1))


def across(left, right):
    return lax.dot_general(left, right, (((0,), (0,)), ((), ())), preferred_element_type=F32)


def grads_kernel(
    ext, y0, y1, flat_up, flat_down, in_grad, up_flat, down_flat, field, even_taps, odd_taps, sums, d0, d1, products, fine
):
    rows = ext.shape[1]
    wide = ext.shape[2]
    half_rows, half_cols = rows // 2, (wide - 16) // 2
    count = half_rows + 1
    before, after = rims(y0, y1)
    tx, ty = lax.axis_index("tx"), lax.axis_index("ty")
    has_below, has_right = tx < lax.axis_size("tx") - 1, ty < lax.axis_size("ty") - 1

    def fill(kind, top, bottom):
        field[0, 0:wide] = before(top)
        for row in range(rows):
            field[row + 1, 0:wide] = ext[kind, row].astype(F32)
        for k, spot in enumerate(bottom):
            field[rows + 1 + k, 0:wide] = after(spot)

    reduced, pre_grad = sweep(
        wide,
        field,
        even_taps,
        odd_taps,
        sums,
        flat_up,
        flat_down,
        count,
        lambda: fill(1, 1, (3, 4)),
        lambda: fill(0, 0, (0, 1, 2)),
    )
    depth = reduced.shape[1]
    row, col = places(count, depth)
    inside = ((row < half_rows) | has_below) & ((col < half_cols) | (has_right & (col == half_cols)))
    pre_grad = jnp.where(inside, pre_grad, 0.0).astype(BF16).reshape(count, PAD, depth)
    base = lambda row_id: ext[0, row_id, LEFT : wide - 8]
    moved = lax.dot(pre_grad.reshape(count * PAD, depth), flat_down[...], preferred_element_type=F32)
    products[...] = moved.reshape(count, PAD, 9 * 128)
    combine_fine(products, base, fine, in_grad)
    cells = half_rows * half_cols
    own = lambda value: value[:half_rows, :half_cols].reshape(cells, value.shape[-1])
    reduced, own_grad = own(reduced.reshape(count, PAD, depth)), own(pre_grad)
    terms = across(reduced, own(sums))
    for tap in range(9):
        up_flat[tap * depth : tap * depth + depth] = terms[:, tap * 128 : tap * 128 + 128]
    span = 3 * 128
    for a, view in enumerate((even_taps, odd_taps, even_taps)):
        taps = view[a // 2 : a // 2 + half_rows, 0:half_cols].reshape(cells, span)
        term = across(taps, own_grad)
        d0[a * span : a * span + span] = term[:, 0:128]
        d1[a * span : a * span + span, 0:64] = term[:, 128:192]
    flatten_rows(d0, d1, down_flat, 0)


def paired_kernel(
    st, grad, st_far, grad_far, rim, rim_far, flat_up, flat_down, value, far, in_grad, *rest
):
    own_sum, send1, send2, send3, field, taps, sums, d0, d1, up_flat = rest[:10]
    grads, products, fine, edge_taps, edge_sums, grad_field = rest[10:]
    rows, breadth = grad.shape[0], grad.shape[1]
    wide = breadth + 16
    count, half_rows, half_cols = rows, rows // 2, breadth // 2
    cells = count * half_cols
    edge_count = half_rows + 1
    tx, ty = lax.axis_index("tx"), lax.axis_index("ty")
    has_below = tx < lax.axis_size("tx") - 1
    has_right = ty < lax.axis_size("ty") - 1
    first_row = rows * tx

    rim_here, rim_there = rim[...].astype(F32), unpacked_rims(rim_far)

    def fill(field, here_rows, there_rows, turn_before, turn_after):
        blank = jnp.zeros((wide, 128), F32)
        field[0, 0:wide] = blank
        field[2 * rows + 1, 0:wide] = blank
        here, there = 1 + rows * tx, 1 + rows * (1 - tx)
        for start, source, sides in ((here, here_rows, rim_here), (there, there_rows, rim_there)):
            for row in range(rows):
                field[start + row, LEFT : LEFT + breadth] = source(row).astype(F32)
            turned = lambda turn: pltpu.roll(sides, turn, 1) if turn else sides
            field[pl.ds(start, rows), 0:8] = turned(turn_before)
            field[pl.ds(start, rows), LEFT + breadth : wide] = turned(turn_after)

    def slopes(pre_back):
        logistic = 0.5 + 0.5 * jnp.tanh(0.5 * pre_back)
        return logistic, logistic * (1.0 + pre_back * (1.0 - logistic))

    def full_taps(values, weights):
        return lax.dot_general(values, weights[...], (((1,), (1,)), ((), ())), preferred_element_type=F32)

    edge = lambda field, row, k: field[first_row + row, pl.ds(LEFT - 1 + k + breadth, 8, stride=2), :]
    flat_edge = lambda ref: ref[...].reshape(edge_count * 8, 9 * 128).astype(BF16)

    for each in (field, grad_field):
        each[:, wide:] = jnp.zeros((each.shape[0], each.shape[1] - wide, 128), F32)
    fill(field, lambda row: st[row], lambda row: st_far[0, row], 1, 5)
    spread_taps(field, taps.at[:, :, 0:384], taps.at[:, :, 384:768], 2 * count + 1, LEFT - 1)
    for p in range(edge_count):
        for tap in range(9):
            edge_taps[p, :, tap * 128 : tap * 128 + 128] = edge(field, 2 * p + tap // 3, tap % 3)
    pre_back = full_taps(taps[0:count].reshape(cells, 768), flat_down.at[:, 0:768])
    pre_back += full_taps(taps[1 : count + 1, :, 0:384].reshape(cells, 384), flat_down.at[:, 768:1152])
    logistic, slope = slopes(pre_back)
    reduced = (pre_back * logistic).astype(BF16)
    edge_slope = slopes(full_taps(flat_edge(edge_taps), flat_down))[1]

    fill(grad_field, lambda row: grad[row], lambda row: grad_far[row], 0, 0)
    window_sums(lambda row, k: grad_field[row, pl.ds(LEFT - 1 + k, half_cols, stride=2), :], count, sums)
    window_sums(lambda row, k: edge(grad_field, row, k), edge_count, edge_sums)
    depth = reduced.shape[1]
    coupled = (full_taps(sums[...].reshape(cells, 9 * 128), flat_up) * slope).astype(BF16)
    edge_shape = (edge_count, 8, depth)
    row = lax.broadcasted_iota(jnp.int32, edge_shape, 0).reshape(edge_count * 8, depth)
    inside = has_right & ((row < half_rows) | has_below)
    edge_grad = jnp.where(inside, full_taps(flat_edge(edge_sums), flat_up) * edge_slope, 0.0).astype(BF16)
    half = up_flat.shape[0] - depth // 2
    lanes = pl.ds(pl.multiple_of(tx * 512, 128), 640)
    terms = across(reduced, sums[:, :, lanes].reshape(cells, 640))
    for tap in range(5):
        up_flat[tap * depth : tap * depth + depth] = terms[:, tap * 128 : tap * 128 + 128]
    span = 3 * 128
    outer = across(taps[pl.ds(tx, count), :, 0:span].reshape(cells, span), coupled)
    middle = across(taps[0:count, :, span : 2 * span].reshape(cells, span), coupled)
    outer_at = pl.multiple_of(tx * (span // 2), 8)
    middle_at = pl.multiple_of((1 - tx) * span, 8)
    middle_half = jnp.where(tx == 0, middle[0 : span // 2], middle[span // 2 : span])
    d0[pl.ds(outer_at, span)] = outer[:, 0:128]
    d1[pl.ds(outer_at, span), 0:64] = outer[:, 128:192]
    d0[pl.ds(middle_at, span // 2)] = middle_half[:, 0:128]
    d1[pl.ds(middle_at, span // 2), 0:64] = middle_half[:, 128:192]
    piece, tall = half // 4, d0.shape[0] // 4
    up_start = tx * (depth // 2)
    near = lax.broadcasted_iota(jnp.int32, (tall // 2, 128), 1) < 64
    for distance, target in enumerate((own_sum, send1, send2, send3)):
        peer = ty ^ distance
        start = pl.multiple_of(peer * tall, 8)
        later = pl.multiple_of(peer * tall + tall // 2, 8)
        rests = jnp.where(near, d1[pl.ds(start, tall // 2)], pltpu.roll(d1[pl.ds(later, tall // 2)], 64, 1))
        parts = [up_flat[pl.ds(pl.multiple_of(up_start + peer * piece, 8), piece)], d0[pl.ds(start, tall)], rests]
        target[...] = jnp.concatenate(parts, axis=0).astype(target.dtype)
    grads[0:count] = coupled.reshape(count, half_cols, depth)
    grads[count] = jnp.zeros((half_cols, depth), BF16)
    own_rows = grads[pl.ds(half_rows * tx, edge_count)].reshape(edge_count * half_cols, depth)
    moved = lax.dot(own_rows, flat_down[...], preferred_element_type=F32)
    products[:, 0:half_cols] = moved.reshape(edge_count, half_cols, 9 * 128)
    moved = lax.dot(edge_grad, flat_down[...], preferred_element_type=F32)
    products[:, half_cols:] = moved.reshape(edge_count, 8, 9 * 128)
    combine_fine(products, lambda row: grad[row], fine, in_grad)
    for row in range(far.shape[0]):
        here = row + (rows - far.shape[0]) * tx
        far[row] = relay_choices(value[here], in_grad[here])[1]


def combine_fine(products, base, fine, target):
    half_rows, half_cols = fine.shape[0] // 2, fine.shape[1] // 2

    def part(p, a, b, offset):
        tap = 3 * a + b
        return products[p, offset : offset + half_cols, tap * 128 : tap * 128 + 128]

    for p in range(half_rows):
        fine[2 * p, pl.ds(0, half_cols, stride=2), :] = part(p, 1, 1, 0)
        fine[2 * p, pl.ds(1, half_cols, stride=2), :] = part(p, 1, 2, 0) + part(p, 1, 0, 1)
        fine[2 * p + 1, pl.ds(0, half_cols, stride=2), :] = part(p, 2, 1, 0) + part(p + 1, 0, 1, 0)
        fine[2 * p + 1, pl.ds(1, half_cols, stride=2), :] = (
            part(p, 2, 2, 0) + part(p, 2, 0, 1) + part(p + 1, 0, 2, 0) + part(p + 1, 0, 0, 1)
        )
    for row in range(fine.shape[0]):
        target[row] = (base(row).astype(F32) + fine[row]).astype(BF16)


def raise_rows(field, even_taps, odd_taps, products, flat_up, flat_down, count, first, valid):
    spread_taps(field, even_taps, odd_taps, 2 * count + 1, first)
    pre_down = lower(even_taps, odd_taps, count, flat_down)
    reduced = pre_down * (0.5 + 0.5 * jnp.tanh(0.5 * pre_down))
    row, col = places(count, reduced.shape[1])
    reduced = jnp.where(valid(row, col), reduced, 0.0).astype(BF16)
    raised = lax.dot(reduced, flat_up[...], preferred_element_type=F32)
    products[...] = raised.reshape(count, PAD, 9 * 128)


def fine_row(products, mixed, target, picks):
    half_cols = target.shape[0] // 2
    col = []
    for b in range(3):
        terms = [
            products[q, :, (3 * a + b) * 128 : (3 * a + b) * 128 + 128]
            for a, q in enumerate(picks)
            if q is not None
        ]
        col.append(sum(terms[1:], terms[0]))
    mixed[0], mixed[1] = col[0], col[1] + col[2]
    mixed[2], mixed[3] = col[0] + col[1], col[2]
    target[pl.ds(0, half_cols, stride=2), :] = mixed[0, 0:half_cols] + mixed[1, 1 : half_cols + 1]
    target[pl.ds(1, half_cols, stride=2), :] = mixed[2, 1 : half_cols + 1] + mixed[3, 2 : half_cols + 2]


def right_edge(half_cols):
    has_right = lax.axis_index("ty") < lax.axis_size("ty") - 1
    return lambda row, col: (col <= half_cols) | has_right


def relay_choices(value, in_grad):
    position, segments = lax.axis_index("segment"), lax.axis_size("segment")
    near = jnp.where(position % 2 == 0, value, in_grad)
    return near, jnp.where(position < segments // 2, value, in_grad)


def forward_kernel(blocks, y0, y1, in_grad, flat_up, flat_down, near, far, *scratch):
    field, even_taps, odd_taps, products, mixed, fine = scratch
    rows, wide = blocks.shape[1], blocks.shape[2]
    breadth = wide - 16
    half_rows, half_cols = rows // 2, breadth // 2
    has_below = lax.axis_index("tx") < lax.axis_size("tx") - 1
    before, after = rims(y0, y1)
    field[:, wide:] = jnp.zeros((field.shape[0], field.shape[1] - wide, 128), F32)
    for k in range(3):
        field[k, 0:wide] = before(2 + k)
    for row in range(rows):
        field[row + 3, 0:wide] = blocks[2, row].astype(F32)
    for k in range(2):
        field[rows + 3 + k, 0:wide] = after(5 + k)
    edge = right_edge(half_cols)
    valid = lambda row, col: ((row <= half_rows) | has_below) & edge(row, col)
    raise_rows(field, even_taps, odd_taps, products, flat_up, flat_down, half_rows + 2, LEFT - 3, valid)
    for p in range(half_rows):
        fine_row(products, mixed, fine.at[2 * p], (p, p + 1, p + 1))
        fine_row(products, mixed, fine.at[2 * p + 1], (p + 1, p + 1, p + 2))
    for row in range(rows):
        value = (blocks[2, row, LEFT : LEFT + breadth].astype(F32) + fine[row]).astype(BF16)
        near[row], far[row] = relay_choices(value, in_grad[row])


def inner_kernel(blocks, flat_up, flat_down, value, *scratch):
    field, even_taps, odd_taps, products, mixed, fine = scratch
    rows, wide = blocks.shape[0], blocks.shape[1]
    breadth = wide - 16
    half_rows, half_cols = rows // 2, breadth // 2
    field[:, wide:] = jnp.zeros((field.shape[0], field.shape[1] - wide, 128), F32)
    field[0, 0:wide] = jnp.zeros((wide, 128), F32)
    for row in range(rows):
        field[row + 1, 0:wide] = blocks[row].astype(F32)
    edge = right_edge(half_cols)
    raise_rows(field, even_taps, odd_taps, products, flat_up, flat_down, half_rows, LEFT - 3, edge)
    for p in range(half_rows):
        fine_row(products, mixed, fine.at[2 * p], (p - 1 if p else None, p, p))
        below = p + 1 if p + 1 < half_rows else None
        fine_row(products, mixed, fine.at[2 * p + 1], (p, p, below))
    for row in range(rows):
        value[row] = (blocks[row, LEFT : LEFT + breadth].astype(F32) + fine[row]).astype(BF16)


def condition_inner_kernel(
    owner_in, cell_in, base, z0, z1, coarse, z2, flat_up, flat_down, pay, ext, value, *scratch
):
    table, plane, owner, cell, arrived = scratch[:5]
    copies = copies_in_parts(((owner_in, owner, 1), (cell_in, cell, 1)), arrived)
    for copy in copies:
        copy.start()

    def named():
        for copy in copies:
            copy.wait()

    condition_kernel(True, owner, cell, base, z0, z1, coarse, z2, pay, ext, table, plane, named)
    inner_kernel(ext, flat_up, flat_down, value, *scratch[5:])


def border_kernel(blocks, y0, value, in_grad, flat_up, flat_down, near, strip, *scratch):
    field, even_taps, odd_taps, products, mixed, fine = scratch
    rows, wide = blocks.shape[0], blocks.shape[1]
    breadth = wide - 16
    half_cols = breadth // 2
    upper = lax.axis_index("tx") == 0
    field[:, wide:] = jnp.zeros((field.shape[0], field.shape[1] - wide, 128), F32)

    def far_row(k):
        tiles = [y0[(breadth // 8 + 1) * k + part].astype(F32) for part in range(breadth // 8 + 1)]
        return jnp.concatenate([tiles[-1]] + tiles, axis=0)

    own = lambda row: blocks[row].astype(F32)
    for k in range(7):
        lower_tile = far_row(k) if k < 3 else own(k - 3)
        upper_tile = own(rows - 5 + k) if k < 5 else far_row(k - 5)
        field[k, 0:wide] = jnp.where(upper, upper_tile, lower_tile)
    edge = right_edge(half_cols)
    raise_rows(field, even_taps, odd_taps, products, flat_up, flat_down, 3, LEFT - 3, edge)
    fine_row(products, mixed, fine.at[0], (0, 1, 1))
    fine_row(products, mixed, fine.at[1], (1, 1, 2))
    fine_row(products, mixed, fine.at[2], (1, 2, 2))
    repaired = [None] * 3
    for k in range(3):
        base = jnp.where(upper, own(rows - 3 + k), own(k))[LEFT : LEFT + breadth]
        added = jnp.where(upper, fine[max(k - 1, 0)], fine[k])
        repaired[k] = (base + added).astype(BF16)
        if k == 0:
            repaired[k] = jnp.where(upper, value[rows - 3], repaired[k])
        strip[k] = relay_choices(repaired[k], jnp.where(upper, in_grad[rows - 3 + k], in_grad[k]))[1]
    for row in range(rows):
        result = value[row]
        if row < 3:
            result = jnp.where(upper, result, repaired[row])
        if row >= rows - 3:
            result = jnp.where(upper, repaired[row - (rows - 3)], result)
        near[row] = relay_choices(result, in_grad[row])[0]


def final_kernel(
    scaling, near, far, strip, own, first, second, third, act_out, grad_out, partner_out, up_sum, down_sum, d0, d1
):
    rows, border = near.shape[0], strip.shape[0]
    position, last = lax.axis_index("segment"), lax.axis_size("segment") - 1
    upper = lax.axis_index("tx") == 0
    odd = position % 2 == 1
    for row in range(rows):
        from_upper = far[row] if row < rows - border else strip[row - (rows - border)]
        from_lower = strip[row] if row < border else far[row - border]
        from_far = jnp.where(upper, from_upper, from_lower)
        blank = jnp.zeros_like(from_far)
        partner_out[0, row] = from_far
        act_out[0, row] = jnp.where(position == 0, blank, jnp.where(odd, near[row], from_far))
        grad_out[0, row] = jnp.where(position == last, blank, jnp.where(odd, from_far, near[row]))
    total = own[...] + first[...].astype(F32) + second[...].astype(F32) + third[...].astype(F32)
    piece = up_sum.shape[0]
    up_sum[...] = total[0:piece] * scaling
    tall = d0.shape[0]
    rests = total[piece + tall :] * scaling
    d0[...] = total[piece : piece + tall] * scaling
    d1[0 : tall // 2] = rests
    d1[tall // 2 :] = pltpu.roll(rests, 64, 1)
    flatten_rows(d0, d1, down_sum, 0)


def swaps(axis):
    size = lax.axis_size(axis)
    pairs = [(i, i + 1) for i in range(0, size - 1, 2)]
    other = [(i, i + 1) for i in range(1, size - 1, 2)]
    both = lambda pairs: pairs + [(j, i) for i, j in pairs]
    return both(pairs), both(other)


def crossed(axis, distance):
    return [(i, i ^ distance) for i in range(lax.axis_size(axis))]


def shape(dims, kind):
    return jax.ShapeDtypeStruct(tuple(dims), kind)


def local(
    act_in,
    partner_in,
    stashed,
    grad_in,
    down_weights,
    up_weights,
    coarse,
    nest_owner,
    nest_cell,
    land_weight,
):
    height, breadth, channels = act_in.shape[1:]
    depth = down_weights.shape[-1]
    half_rows = height // 2
    n_tx, n_ty = lax.axis_size("tx"), lax.axis_size("ty")
    position, segments = lax.axis_index("segment"), lax.axis_size("segment")
    scaling = 1.0 / math.sqrt(height * breadth * n_tx * n_ty)
    down_taps = jnp.swapaxes(down_weights, 3, 4).reshape(9, depth, channels)
    up_taps = up_weights.reshape(9, depth, channels)

    owners = nest_owner.reshape(-1)
    tile = shape((height, breadth, channels), BF16)
    pay = shape((height + 1 + coarse.shape[0] // 8, 8, channels), BF16)
    merged = n_ty == 4 and n_tx == 2
    if merged:
        st_far = lax.ppermute(stashed, "tx", crossed("tx", 1))
    side = pltpu.VMEM((height, 16, channels), BF16)
    full = pltpu.VMEM((height, breadth, channels), BF16)
    grad_own, z_pay0, z_pay1 = call(
        edge_kernel,
        (tile, pay, pay),
        [HBM] * 8,
        [side] * 4
        + [full] * 2
        + [pltpu.VMEM((height // 4, breadth, channels), F32), pltpu.VMEM(coarse.shape, BF16)]
        + [pltpu.SMEM(scalars.shape, jnp.int32) for scalars in (owners, nest_cell, land_weight)]
        + [pltpu.SemaphoreType.DMA((16,))],
        flops=1000,
        moved=1000,
    )(*in_hbm(owners, nest_cell, land_weight, act_in, partner_in, stashed, grad_in, coarse))
    pairs, others = swaps("ty")
    if merged:
        others = crossed("ty", 3)
        grad_far = lax.ppermute(grad_own, "tx", crossed("tx", 1))
    z0 = lax.ppermute(z_pay0, "ty", pairs)
    z1 = lax.ppermute(z_pay1, "ty", others)
    if merged:
        table_parts = (coarse, lax.ppermute(coarse, "ty", crossed("ty", 2)))
    else:
        table_parts = (lax.all_gather(coarse, "ty", tiled=True),)
    flat = shape((depth, 9 * channels), BF16)
    taps_room = pltpu.VMEM((9, depth, channels), BF16)
    base, stash, flat_up, flat_down = call(
        prepare_kernel,
        (shape((height, breadth, channels), F32), tile, flat, flat),
        [HBM] * 5,
        [full, full, taps_room, taps_room, pltpu.SemaphoreType.DMA((30,))],
        flops=1000,
        moved=1000,
    )(*in_hbm(act_in, partner_in, stashed, up_taps, down_taps))
    wide = 2 * PAD + 16
    rows_flat = 9 * depth

    def tap_rooms(count):
        room = pltpu.VMEM((count + 1, PAD, 3 * channels), BF16)
        return [pltpu.VMEM((2 * count + 2, wide, channels), F32), room, room]

    fine = pltpu.VMEM((height, breadth, channels), F32)
    products = lambda count: pltpu.VMEM((count, PAD, 9 * channels), F32)
    forward_rooms = lambda count: tap_rooms(count) + [
        products(count),
        pltpu.VMEM((4, PAD, channels), F32),
        fine,
    ]
    operands = (base, z0, z1, *table_parts)
    rooms = [
        pltpu.VMEM((n_ty * coarse.shape[0], channels), F32),
        pltpu.VMEM((height // 4, breadth, channels), F32),
    ]
    pairs, others = swaps("tx")
    if merged:
        rim, pack = call(
            rim_kernel,
            (shape((height, 8, channels), BF16), shape((height // 2 + BORDER, 8, channels), BF16)),
            [VMEM] * 2 + [pl.BlockSpec(memory_space=pl.ANY)] * 2,
            flops=1000,
            moved=1000,
        )(z0, z1, flat_up, st_far)
        rim_far = lax.ppermute(pack, "tx", pairs)
        pay, blocks, value = call(
            condition_inner_kernel,
            (
                shape((3 * (breadth // 8 + 1), 8, channels), BF16),
                shape((height, breadth + 16, channels), BF16),
                tile,
            ),
            [HBM] * 2 + [VMEM] * (len(operands) + 2),
            rooms
            + [pltpu.SMEM(owners.shape, jnp.int32), pltpu.SMEM(nest_cell.shape, jnp.int32)]
            + [pltpu.SemaphoreType.DMA((2,))]
            + forward_rooms(half_rows),
            flops=2_000_000_000,
            moved=1000,
        )(*in_hbm(owners, nest_cell), *operands, flat_up, flat_down)
        ys = [lax.ppermute(pay, "tx", pairs)]
    else:
        pay = shape((STRIP_ROWS, breadth + 16, channels), BF16)
        *pays, blocks = call(
            functools.partial(condition_kernel, False),
            (pay, pay, shape((3, height, breadth + 16, channels), BF16)),
            [SMEM] * 2 + [VMEM] * (len(operands) + 2),
            rooms,
        )(owners, nest_cell, *operands, stash, grad_own)
        ys = [lax.ppermute(pays[0], "tx", pairs), lax.ppermute(pays[1], "tx", others) if others else pays[1]]

    if merged:
        piece = rows_flat // (n_tx * n_ty)
        part = shape((2 * piece, channels), BF16)
        far, in_grad, own_sum, *sends = call(
            paired_kernel,
            (shape((height - BORDER, breadth, channels), BF16), tile, shape((2 * piece, channels), F32), part, part, part),
            [VMEM] * 9,
            [
                pltpu.VMEM((2 * height + 4, wide, channels), F32),
                pltpu.VMEM((height + 1, breadth // 2, 6 * channels), BF16),
                pltpu.VMEM((height, breadth // 2, 9 * channels), BF16),
                pltpu.VMEM((9 * channels // 2, 128), F32),
                pltpu.VMEM((9 * channels // 2, 128), F32),
                pltpu.VMEM((5 * depth, channels), F32),
                pltpu.VMEM((height + 1, breadth // 2, depth), BF16),
                pltpu.VMEM((half_rows + 1, breadth // 2 + 8, 9 * channels), F32),
                fine,
                pltpu.VMEM((half_rows + 1, 8, 9 * channels), F32),
                pltpu.VMEM((half_rows + 1, 8, 9 * channels), F32),
                pltpu.VMEM((2 * height + 4, wide, channels), F32),
            ],
            flops=5_000_000_000,
            moved=4_000_000,
        )(stash, grad_own, st_far, grad_far, rim, rim_far, flat_up, flat_down, value)
    else:
        whole = shape((rows_flat, channels), F32)
        in_grad, up_flat, down_flat = call(
            grads_kernel,
            (tile, whole, whole),
            [VMEM] * 5,
            tap_rooms(half_rows + 1)
            + [
                pltpu.VMEM((half_rows + 1, PAD, 9 * channels), BF16),
                pltpu.VMEM((9 * channels, 128), F32),
                pltpu.VMEM((9 * channels, 128), F32),
                products(half_rows + 1),
                fine,
            ],
            flops=500_000_000,
            moved=4_000_000,
        )(blocks, *ys, flat_up, flat_down)
        pooled = lambda flat: lax.psum_scatter(
            flat.reshape(-1) * scaling, ("tx", "ty"), scatter_dimension=0, tiled=True
        )[None]
        down_sum, up_sum = pooled(down_flat), pooled(up_flat)

    mirror = [(i, segments - 1 - i) for i in range(segments)]
    if merged:
        ys = passed_on(ys, 2_000_000_000)
        near, strip = call(
            border_kernel,
            (tile, shape((BORDER, breadth, channels), BF16)),
            [VMEM] * 6,
            forward_rooms(3),
            flops=600_000_000,
            moved=4_000_000,
        )(blocks, ys[0], value, in_grad, flat_up, flat_down)
        from_far = lax.ppermute(far, "segment", mirror)
        from_strip = lax.ppermute(strip, "segment", mirror)
        from_near = lax.ppermute(near, "segment", crossed("segment", 1))
        arrived = [lax.ppermute(sends[d - 1], "ty", crossed("ty", d)) for d in (2, 1, 3)]
        arrived = passed_on(arrived[:1], 800_000_000) + arrived[1:]
        (from_far,) = passed_on([from_far], 100_000_000, arrived[:1])
        arrived = arrived[:1] + passed_on(arrived[1:], 3_000_000_000, [from_far])
        summed = shape((piece, channels), F32)
        act_out, grad_out, partner_out, up_sum, down_sum = call(
            functools.partial(final_kernel, scaling),
            (shape(act_in.shape, BF16),) * 3 + (summed, summed),
            [VMEM] * 7,
            [pltpu.VMEM((2 * piece // 3, 128), F32)] * 2,
            flops=1_000,
            moved=1000,
        )(from_near, from_far, from_strip, own_sum, *arrived)
        return act_out, grad_out, partner_out, down_sum.reshape(1, -1), up_sum.reshape(1, -1)
    near, far = call(
        forward_kernel,
        (tile, tile),
        [VMEM] * 6,
        forward_rooms(half_rows + 2),
        flops=600_000_000,
        moved=4_000_000,
    )(blocks, *ys, in_grad, flat_up, flat_down)
    from_far = lax.ppermute(far, "segment", mirror)
    from_near = lax.ppermute(near, "segment", crossed("segment", 1))
    blank = jnp.zeros_like(from_near)
    odd = position % 2 == 1
    act_out = jnp.where(position == 0, blank, jnp.where(odd, from_near, from_far))
    grad_out = jnp.where(position == segments - 1, blank, jnp.where(odd, from_far, from_near))
    return (act_out[None], grad_out[None], from_far[None], down_sum, up_sum)


def solution(mesh):
    tile = P("segment", "tx", "ty", None)
    weights = P("segment", None, None, None, None)
    grads = P("segment", ("tx", "ty"))
    rows = P(("tx", "ty"))
    return jax.shard_map(
        local,
        mesh=mesh,
        in_specs=(tile,) * 4 + (weights,) * 2 + (P(("tx", "ty"), None),) * 2 + (rows, P("tx", "ty")),
        out_specs=(tile,) * 3 + (grads,) * 2,
        check_vma=False,
    )
```

```python
import functools
import math

import jax
import jax.numpy as jnp
from jax import lax
from jax.experimental import pallas as pl
from jax.experimental.pallas import tpu as pltpu
from jax.sharding import PartitionSpec as P

F32 = jnp.float32
BF16 = jnp.bfloat16
VMEM = pl.BlockSpec(memory_space=pltpu.VMEM)
SMEM = pl.BlockSpec(memory_space=pltpu.SMEM)
HBM = pl.BlockSpec(memory_space=pltpu.HBM)
LEFT = 8
PAD = 48
BORDER = 3
STRIP_ROWS = 7


def call(body, out_shape, in_specs, scratch=(), flops=0, moved=0, limit=24, out_specs=None, aliases=()):
    out_specs = out_specs or jax.tree.map(lambda _: VMEM, out_shape)
    return pl.pallas_call(
        body,
        out_shape=out_shape,
        in_specs=in_specs,
        out_specs=out_specs,
        scratch_shapes=list(scratch),
        input_output_aliases=dict(aliases),
        compiler_params=pltpu.CompilerParams(vmem_limit_bytes=limit * 1024 * 1024),
        cost_estimate=pl.CostEstimate(flops=flops, bytes_accessed=moved, transcendentals=0),
    )


def passed_on(arrays, flops, after=()):
    here = [pl.BlockSpec(memory_space=pl.ANY)] * len(arrays)
    return list(call(
        lambda *refs: None,
        tuple(jax.ShapeDtypeStruct(x.shape, x.dtype) for x in arrays),
        here + [pl.BlockSpec(memory_space=pl.ANY)] * len(after),
        flops=flops,
        moved=1000,
        out_specs=tuple(here),
        aliases=[(k, k) for k in range(len(arrays))],
    )(*arrays, *after))


def copies_in_parts(pairs, arrived):
    copies = []
    for source, target, parts in pairs:
        length = source.shape[0] // parts
        for part in range(parts):
            rows = pl.ds(part * length, length)
            views = (source.at[rows], target.at[rows]) if parts > 1 else (source, target)
            copies.append(pltpu.make_async_copy(*views, arrived.at[len(copies)]))
    return copies


def in_hbm(*operands):
    return [pltpu.with_memory_space_constraint(x, pltpu.HBM) for x in operands]


def sublane(shape):
    return lax.broadcasted_iota(jnp.int32, shape, len(shape) - 2)


def flag(condition):
    return jnp.where(condition, 1.0, 0.0).astype(F32)


def traits():
    segments = lax.axis_size("segment")
    position = lax.axis_index("segment")
    decoder = flag(position >= segments // 2)
    return decoder, 1.0 - decoder, position == segments - 1


def edge_kernel(owner_in, cell_in, land_in, act, par, st, gr, coarse, grad_out, pay0, pay1, *scratch):
    act_l, act_r, st_l, st_r, par_v, gr_v, plane, held_v, owner, cell, land, arrived = scratch
    rows, breadth = gr.shape[1], gr.shape[2]
    first, final = pl.ds(0, 16), pl.ds(breadth - 16, 16)
    scalars = copies_in_parts(((owner_in, owner, 1), (cell_in, cell, 1), (land_in, land, 1)), arrived)
    copies = copies_in_parts(
        (
            (gr.at[0], gr_v, 1),
            (par.at[0], par_v, 1),
            (act.at[0, :, first], act_l, 1),
            (act.at[0, :, final], act_r, 1),
            (st.at[0, :, first], st_l, 1),
            (st.at[0, :, final], st_r, 1),
            (coarse, held_v, 1),
        ),
        arrived.at[pl.ds(3, 13)],
    )
    for copy in scalars + copies:
        copy.start()
    for copy in scalars:
        copy.wait()
    decoder, encoder, last = traits()
    groups = rows // 4
    per_row = breadth // 4
    low = sublane((8, 128)) < 4
    for group in range(groups):
        for part in range(breadth // 8):
            weigh = [jnp.where(last, land[group, 2 * part + k], 1).astype(F32) for k in range(2)]
            plane[group, 8 * part : 8 * part + 8] = jnp.where(low, weigh[0], weigh[1])

    def ids(column):
        tile = jnp.zeros((8, 128), F32)
        where = sublane((8, 128))
        for row in range(groups):
            spot = row * per_row + column
            tile = jnp.where(where == row, owner[spot].astype(F32), tile)
            tile = jnp.where(where == 4 + row, cell[spot].astype(F32), tile)
        return tile

    left_ids, right_ids = ids(0), ids(per_row - 1)
    for copy in copies:
        copy.wait()
    for row in range(rows):
        grad = gr_v[row].astype(F32) + encoder * par_v[row].astype(F32)
        grad_out[row] = (grad * plane[row // 4]).astype(BF16)

    where = sublane((rows, 8, 128))
    begin, end = slice(0, 16), slice(breadth - 16, breadth)
    grad = grad_out[:, begin].astype(F32)[:, 0:8]
    stash = st_l[...].astype(F32)[:, 0:8]
    block = act_l[...].astype(F32)[:, 0:8] + decoder * par_v[:, begin].astype(F32)[:, 0:8]
    after = jnp.where(
        where < 3, grad, jnp.where(where < 5, pltpu.roll(stash, 3, 1), pltpu.roll(block, 5, 1))
    )
    grad = grad_out[:, end].astype(F32)[:, 8:16]
    stash = st_r[...].astype(F32)[:, 8:16]
    block = act_r[...].astype(F32)[:, 8:16] + decoder * par_v[:, end].astype(F32)[:, 8:16]
    before = jnp.where(
        where == 7, grad, jnp.where(where == 6, pltpu.roll(stash, 7, 1), pltpu.roll(block, 6, 1))
    )
    even = lax.axis_index("ty") % 2 == 0
    strips = jnp.where(even, before, after).astype(BF16), jnp.where(even, after, before).astype(BF16)
    named = jnp.where(even, right_ids, left_ids), jnp.where(even, left_ids, right_ids)
    held = held_v[...].reshape(coarse.shape[0] // 8, 8, 128)
    for k, pay in enumerate((pay0, pay1)):
        pay[0:rows] = strips[k]
        pay[rows] = named[k].astype(BF16)
        pay[rows + 1 :] = held


def prepare_kernel(act, par, st, up, down, base, stash, flat_up, flat_down, *scratch):
    act_v, par_v, up_v, down_v, arrived = scratch
    tiles = (act.at[0], act_v, 1), (par.at[0], par_v, 1), (st.at[0], stash, 1)
    copies = copies_in_parts(tiles + ((up, up_v, 1), (down, down_v, 1)), arrived)
    for copy in copies:
        copy.start()
    decoder, _, _ = traits()
    for copy in copies:
        copy.wait()
    for row in range(act_v.shape[0]):
        base[row] = act_v[row].astype(F32) + decoder * par_v[row].astype(F32)
    lane_taps(up_v, flat_up)
    lane_taps(down_v, flat_down)


def side_rims(z0, z1, rows):
    ty = lax.axis_index("ty")
    even = ty % 2 == 0
    first, second = z0[0:rows].astype(F32), z1[0:rows].astype(F32)
    before = jnp.where(ty > 0, jnp.where(even, second, first), 0.0)
    after = jnp.where(ty < lax.axis_size("ty") - 1, jnp.where(even, first, second), 0.0)
    return before, after


def rim_kernel(z0, z1, _weights, _stash, rim, pack):
    before, after = side_rims(z0, z1, rim.shape[0])
    whole = jnp.where(sublane(rim.shape) < 5, after, before)
    rim[...] = whole.astype(BF16)
    rows, half = rim.shape[0], rim.shape[0] // 2
    turned = pltpu.roll(whole, 4, 1)
    spot = sublane((half, 8, 128))
    first = jnp.where(spot < 2, whole[:half], turned[:half])
    second = jnp.where(spot < 6, turned[half:], whole[half:])
    pack[0:half] = jnp.where(spot < 4, first, second).astype(BF16)
    upper = lax.axis_index("tx") == 0
    for k in range(BORDER):
        pack[half + k] = jnp.where(upper, whole[rows - BORDER + k], whole[k]).astype(BF16)


def unpacked_rims(pack):
    packed = pack[...].astype(F32)
    half = packed.shape[0] - BORDER
    rows = 2 * half
    turned = pltpu.roll(packed, 4, 1)
    low = sublane((half, 8, 128)) < 4
    first = jnp.where(low, packed[:half], turned[:half])
    second = jnp.where(low, turned[:half], packed[:half])
    tiles = [first[k] for k in range(half)] + [second[k] for k in range(half)]
    upper = lax.axis_index("tx") == 0
    for k in range(BORDER):
        tiles[k] = jnp.where(upper, packed[half + k], tiles[k])
        here = rows - BORDER + k
        tiles[here] = jnp.where(upper, tiles[here], packed[half + k])
    return jnp.concatenate([tile[None] for tile in tiles], axis=0)


def condition_kernel(merged, owner, cell, base, z0, z1, coarse, *rest):
    rows, breadth = base.shape[0], base.shape[1]
    groups = rows // 4
    per_row = breadth // 4
    cells = groups * per_row
    wide = LEFT + breadth
    ty = lax.axis_index("ty")
    low = sublane((8, 128)) < 4
    if merged:
        z2, pay, ext, table, plane, named_here = rest
        table[pl.ds(pl.multiple_of(ty * cells, 8), cells)] = coarse[...].astype(F32)
        others = (
            (ty ^ 1, z0[rows + 1 :].astype(F32).reshape(cells, 128)),
            (ty ^ 3, z1[rows + 1 :].astype(F32).reshape(cells, 128)),
            (ty ^ 2, z2[...].astype(F32)),
        )
        for other, value in others:
            table[pl.ds(pl.multiple_of(other * cells, 8), cells)] = value
    else:
        st, grad_own, pay, pay1, full, table, plane = rest
        ext = full.at[2]
        table[...] = coarse[...].astype(F32)
    before, after = side_rims(z0, z1, rows + 1)

    def rim_condition(tile, valid):
        wanted = tile[rows]
        spot = wanted * cells + pltpu.roll(wanted, 4, 0)
        lanes = lax.broadcasted_iota(jnp.int32, (8, table.shape[0]), 1).astype(F32)
        spread = jnp.broadcast_to(spot[:, 0:1], lanes.shape)
        hot = jnp.where(spread == lanes, 1.0, 0.0).astype(BF16)
        named = lax.dot(hot, table[...].astype(BF16), preferred_element_type=F32)
        picked = [jnp.broadcast_to(named[row : row + 1], (8, 128))[None] for row in range(groups)]
        spread_rows = jnp.concatenate([p for p in picked for _ in range(4)], axis=0)
        return jnp.where(valid, spread_rows, 0.0)

    rim = pltpu.roll(before[0:rows], 2, 1) + rim_condition(before, ty > 0)
    ext[:, 0:8] = rim.astype(BF16)
    rim = pltpu.roll(after[0:rows], 3, 1) + rim_condition(after, ty < lax.axis_size("ty") - 1)
    ext[:, wide : wide + 8] = rim.astype(BF16)
    if merged:
        named_here()
    for group in range(groups):
        for part in range(breadth // 8):
            spots = [group * per_row + 2 * part + k for k in range(2)]
            named = [
                jnp.broadcast_to(table[pl.ds(owner[s] * cells + cell[s], 1)], (8, 128)) for s in spots
            ]
            plane[group, 8 * part : 8 * part + 8] = jnp.where(low, named[0], named[1])
    for row in range(rows):
        ext[row, LEFT:wide] = (base[row] + plane[row // 4]).astype(BF16)

    upper = lax.axis_index("tx") % 2 == 0
    if merged:
        near = sublane((8, 128)) < 5
        for k in range(3):
            top, bottom = min(k, 1), rows - 3 + k
            for part in range(breadth // 8):
                cols = pl.ds(LEFT + 8 * part, 8)
                pay[9 * k + part] = jnp.where(upper, ext[bottom, cols], ext[top, cols])
            tiles = [
                jnp.where(near, ext[row, pl.ds(wide, 8)], ext[row, pl.ds(0, 8)]) for row in (top, bottom)
            ]
            pay[9 * k + breadth // 8] = jnp.where(upper, tiles[1], tiles[0])
        return
    full[0, :, 0:8] = before[0:rows].astype(BF16)
    full[1, :, 0:8] = pltpu.roll(before[0:rows], 1, 1).astype(BF16)
    full[0, :, wide : wide + 8] = after[0:rows].astype(BF16)
    full[1, :, wide : wide + 8] = pltpu.roll(after[0:rows], 5, 1).astype(BF16)
    full[0, :, LEFT:wide] = grad_own[...]
    full[1, :, LEFT:wide] = st[...]
    leading = [(0, 0), (0, 1), (0, 2), (1, 0), (1, 1), (2, 0), (2, 1)]
    closing = [(0, rows - 1), (1, rows - 1), (2, rows - 3), (2, rows - 2), (2, rows - 1)]
    closing = closing + closing[-1:] * 2
    for k in range(STRIP_ROWS):
        top, bottom = full[leading[k]], full[closing[k]]
        pay[k] = jnp.where(upper, bottom, top)
        pay1[k] = jnp.where(upper, top, bottom)


def rims(y0, y1):
    tx = lax.axis_index("tx")
    upper = tx % 2 == 0
    before_ok, after_ok = tx > 0, tx < lax.axis_size("tx") - 1

    def row(valid, from_first, k):
        value = jnp.where(from_first, y0[k].astype(F32), y1[k].astype(F32))
        return jnp.where(valid, value, 0.0)

    before = lambda k: row(before_ok, jnp.logical_not(upper), k)
    after = lambda k: row(after_ok, upper, k)
    return before, after


def spread_taps(field, taps, odd_taps, count, first):
    width = taps.shape[1]
    for row in range(count):
        target = taps if row % 2 == 0 else odd_taps
        for tap in range(3):
            value = field[row, pl.ds(first + tap, width, stride=2), :]
            target[row // 2, :, tap * 128 : tap * 128 + 128] = value.astype(BF16)


def three_rows(even_taps, odd_taps, count):
    wide = 3 * 128
    whole = lambda ref, a: ref[a : a + count].reshape(count * ref.shape[1], wide)
    return whole(even_taps, 0), whole(odd_taps, 0), whole(even_taps, 1)


def lower(even_taps, odd_taps, count, down):
    views = three_rows(even_taps, odd_taps, count)
    wide = 3 * 128
    total = None
    for a in range(3):
        term = lax.dot_general(
            views[a],
            down[:, a * wide : a * wide + wide],
            (((1,), (1,)), ((), ())),
            preferred_element_type=F32,
        )
        total = term if total is None else total + term
    return total


def lane_taps(taps, flat):
    for tap in range(9):
        flat[:, tap * 128 : tap * 128 + 128] = taps[tap]


def window_sums(plane_of, count, sums):
    previous = None
    for row in range(2 * count + 2):
        plane = [plane_of(row, k) for k in range(4)]
        current = [plane[2] + plane[3], plane[1] + plane[2], plane[0] + plane[1]]
        if row > 0:
            for a in range(3):
                double = row - 3 + a
                if double % 2 == 0 and 0 <= double // 2 < count:
                    for b in range(3):
                        lanes = slice((3 * a + b) * 128, (3 * a + b) * 128 + 128)
                        sums[double // 2, :, lanes] = (previous[b] + current[b]).astype(sums.dtype)
        previous = current


def sweep(wide, field, even_taps, odd_taps, sums, flat_up, down, count, fill_stash, fill_grad):
    field[:, wide:] = jnp.zeros((field.shape[0], field.shape[1] - wide, 128), F32)
    fill_stash()
    spread_taps(field, even_taps, odd_taps, 2 * count + 1, LEFT - 1)
    pre_back = lower(even_taps, odd_taps, count, down)
    logistic = 0.5 + 0.5 * jnp.tanh(0.5 * pre_back)
    reduced = pre_back * logistic
    slope = logistic * (1.0 + pre_back * (1.0 - logistic))
    fill_grad()
    window_sums(lambda row, k: field[row, pl.ds(LEFT - 1 + k, PAD, stride=2), :], count, sums)
    windows = sums[...].reshape(count * PAD, 9 * 128)
    raised = lax.dot_general(windows, flat_up[...], (((1,), (1,)), ((), ())), preferred_element_type=F32)
    return reduced.astype(BF16), raised * slope


def places(count, depth):
    shape = (count, PAD, depth)
    row = lax.broadcasted_iota(jnp.int32, shape, 0).reshape(count * PAD, depth)
    col = lax.broadcasted_iota(jnp.int32, shape, 1).reshape(count * PAD, depth)
    return row, col


def flatten_rows(d0, d1, flat, start):
    pairs = d0.shape[0] // 2
    left_even, left_odd = d0[pl.ds(0, pairs, stride=2)], d0[pl.ds(1, pairs, stride=2)]
    right_even, right_odd = d1[pl.ds(0, pairs, stride=2)], d1[pl.ds(1, pairs, stride=2)]
    near = lax.broadcasted_iota(jnp.int32, left_even.shape, 1) < 64
    turned = pltpu.roll(left_odd, 64, 1)
    flat[pl.ds(start, pairs, stride=3)] = left_even
    flat[pl.ds(start + 1, pairs, stride=3)] = jnp.where(near, right_even, turned)
    flat[pl.ds(start + 2, pairs, stride=3)] = jnp.where(near, turned, pltpu.roll(right_odd, 64, 1))


def across(left, right):
    return lax.dot_general(left, right, (((0,), (0,)), ((), ())), preferred_element_type=F32)


def grads_kernel(
    ext, y0, y1, flat_up, flat_down, in_grad, up_flat, down_flat, field, even_taps, odd_taps, sums, d0, d1, products, fine
):
    rows = ext.shape[1]
    wide = ext.shape[2]
    half_rows, half_cols = rows // 2, (wide - 16) // 2
    count = half_rows + 1
    before, after = rims(y0, y1)
    tx, ty = lax.axis_index("tx"), lax.axis_index("ty")
    has_below, has_right = tx < lax.axis_size("tx") - 1, ty < lax.axis_size("ty") - 1

    def fill(kind, top, bottom):
        field[0, 0:wide] = before(top)
        for row in range(rows):
            field[row + 1, 0:wide] = ext[kind, row].astype(F32)
        for k, spot in enumerate(bottom):
            field[rows + 1 + k, 0:wide] = after(spot)

    reduced, pre_grad = sweep(
        wide,
        field,
        even_taps,
        odd_taps,
        sums,
        flat_up,
        flat_down,
        count,
        lambda: fill(1, 1, (3, 4)),
        lambda: fill(0, 0, (0, 1, 2)),
    )
    depth = reduced.shape[1]
    row, col = places(count, depth)
    inside = ((row < half_rows) | has_below) & ((col < half_cols) | (has_right & (col == half_cols)))
    pre_grad = jnp.where(inside, pre_grad, 0.0).astype(BF16).reshape(count, PAD, depth)
    base = lambda row_id: ext[0, row_id, LEFT : wide - 8]
    moved = lax.dot(pre_grad.reshape(count * PAD, depth), flat_down[...], preferred_element_type=F32)
    products[...] = moved.reshape(count, PAD, 9 * 128)
    combine_fine(products, base, fine, in_grad)
    cells = half_rows * half_cols
    own = lambda value: value[:half_rows, :half_cols].reshape(cells, value.shape[-1])
    reduced, own_grad = own(reduced.reshape(count, PAD, depth)), own(pre_grad)
    terms = across(reduced, own(sums))
    for tap in range(9):
        up_flat[tap * depth : tap * depth + depth] = terms[:, tap * 128 : tap * 128 + 128]
    span = 3 * 128
    for a, view in enumerate((even_taps, odd_taps, even_taps)):
        taps = view[a // 2 : a // 2 + half_rows, 0:half_cols].reshape(cells, span)
        term = across(taps, own_grad)
        d0[a * span : a * span + span] = term[:, 0:128]
        d1[a * span : a * span + span, 0:64] = term[:, 128:192]
    flatten_rows(d0, d1, down_flat, 0)


def paired_kernel(
    st, grad, st_far, grad_far, rim, rim_far, flat_up, flat_down, value, far, in_grad, *rest
):
    own_sum, send1, send2, send3, field, taps, sums, d0, d1, up_flat = rest[:10]
    grads, products, fine, edge_taps, edge_sums, grad_field = rest[10:]
    rows, breadth = grad.shape[0], grad.shape[1]
    wide = breadth + 16
    count, half_rows, half_cols = rows, rows // 2, breadth // 2
    cells = count * half_cols
    edge_count = half_rows + 1
    tx, ty = lax.axis_index("tx"), lax.axis_index("ty")
    has_below = tx < lax.axis_size("tx") - 1
    has_right = ty < lax.axis_size("ty") - 1
    first_row = rows * tx

    rim_here, rim_there = rim[...].astype(F32), unpacked_rims(rim_far)

    def fill(field, here_rows, there_rows, turn_before, turn_after):
        blank = jnp.zeros((wide, 128), F32)
        field[0, 0:wide] = blank
        field[2 * rows + 1, 0:wide] = blank
        here, there = 1 + rows * tx, 1 + rows * (1 - tx)
        for start, source, sides in ((here, here_rows, rim_here), (there, there_rows, rim_there)):
            for row in range(rows):
                field[start + row, LEFT : LEFT + breadth] = source(row).astype(F32)
            turned = lambda turn: pltpu.roll(sides, turn, 1) if turn else sides
            field[pl.ds(start, rows), 0:8] = turned(turn_before)
            field[pl.ds(start, rows), LEFT + breadth : wide] = turned(turn_after)

    def slopes(pre_back):
        logistic = 0.5 + 0.5 * jnp.tanh(0.5 * pre_back)
        return logistic, logistic * (1.0 + pre_back * (1.0 - logistic))

    def full_taps(values, weights):
        return lax.dot_general(values, weights[...], (((1,), (1,)), ((), ())), preferred_element_type=F32)

    edge = lambda field, row, k: field[first_row + row, pl.ds(LEFT - 1 + k + breadth, 8, stride=2), :]
    flat_edge = lambda ref: ref[...].reshape(edge_count * 8, 9 * 128).astype(BF16)

    fill(field, lambda row: st[row], lambda row: st_far[0, row], 1, 5)
    spread_taps(field, taps.at[:, :, 0:384], taps.at[:, :, 384:768], 2 * count + 1, LEFT - 1)
    for p in range(edge_count):
        for tap in range(9):
            edge_taps[p, :, tap * 128 : tap * 128 + 128] = edge(field, 2 * p + tap // 3, tap % 3)
    pre_back = full_taps(taps[0:count].reshape(cells, 768), flat_down.at[:, 0:768])
    pre_back += full_taps(taps[1 : count + 1, :, 0:384].reshape(cells, 384), flat_down.at[:, 768:1152])
    logistic, slope = slopes(pre_back)
    reduced = (pre_back * logistic).astype(BF16)
    edge_slope = slopes(full_taps(flat_edge(edge_taps), flat_down))[1]

    fill(grad_field, lambda row: grad[row], lambda row: grad_far[row], 0, 0)
    window_sums(lambda row, k: grad_field[row, pl.ds(LEFT - 1 + k, half_cols, stride=2), :], count, sums)
    window_sums(lambda row, k: edge(grad_field, row, k), edge_count, edge_sums)
    depth = reduced.shape[1]
    coupled = (full_taps(sums[...].reshape(cells, 9 * 128), flat_up) * slope).astype(BF16)
    edge_shape = (edge_count, 8, depth)
    row = lax.broadcasted_iota(jnp.int32, edge_shape, 0).reshape(edge_count * 8, depth)
    inside = has_right & ((row < half_rows) | has_below)
    edge_grad = jnp.where(inside, full_taps(flat_edge(edge_sums), flat_up) * edge_slope, 0.0).astype(BF16)
    half = up_flat.shape[0] - depth // 2
    lanes = pl.ds(pl.multiple_of(tx * 512, 128), 640)
    terms = across(reduced, sums[:, :, lanes].reshape(cells, 640))
    for tap in range(5):
        up_flat[tap * depth : tap * depth + depth] = terms[:, tap * 128 : tap * 128 + 128]
    span = 3 * 128
    outer = across(taps[pl.ds(tx, count), :, 0:span].reshape(cells, span), coupled)
    middle = across(taps[0:count, :, span : 2 * span].reshape(cells, span), coupled)
    outer_at = pl.multiple_of(tx * (span // 2), 8)
    middle_at = pl.multiple_of((1 - tx) * span, 8)
    middle_half = jnp.where(tx == 0, middle[0 : span // 2], middle[span // 2 : span])
    d0[pl.ds(outer_at, span)] = outer[:, 0:128]
    d1[pl.ds(outer_at, span), 0:64] = outer[:, 128:192]
    d0[pl.ds(middle_at, span // 2)] = middle_half[:, 0:128]
    d1[pl.ds(middle_at, span // 2), 0:64] = middle_half[:, 128:192]
    piece, tall = half // 4, d0.shape[0] // 4
    up_start = tx * (depth // 2)
    near = lax.broadcasted_iota(jnp.int32, (tall // 2, 128), 1) < 64
    for distance, target in enumerate((own_sum, send1, send2, send3)):
        peer = ty ^ distance
        start = pl.multiple_of(peer * tall, 8)
        later = pl.multiple_of(peer * tall + tall // 2, 8)
        rests = jnp.where(near, d1[pl.ds(start, tall // 2)], pltpu.roll(d1[pl.ds(later, tall // 2)], 64, 1))
        parts = [up_flat[pl.ds(pl.multiple_of(up_start + peer * piece, 8), piece)], d0[pl.ds(start, tall)], rests]
        target[...] = jnp.concatenate(parts, axis=0).astype(target.dtype)
    grads[0:count] = coupled.reshape(count, half_cols, depth)
    grads[count] = jnp.zeros((half_cols, depth), BF16)
    own_rows = grads[pl.ds(half_rows * tx, edge_count)].reshape(edge_count * half_cols, depth)
    moved = lax.dot(own_rows, flat_down[...], preferred_element_type=F32)
    products[:, 0:half_cols] = moved.reshape(edge_count, half_cols, 9 * 128)
    moved = lax.dot(edge_grad, flat_down[...], preferred_element_type=F32)
    products[:, half_cols:] = moved.reshape(edge_count, 8, 9 * 128)
    combine_fine(products, lambda row: grad[row], fine, in_grad)
    for row in range(far.shape[0]):
        here = row + (rows - far.shape[0]) * tx
        far[row] = relay_choices(value[here], in_grad[here])[1]


def combine_fine(products, base, fine, target):
    half_rows, half_cols = fine.shape[0] // 2, fine.shape[1] // 2

    def part(p, a, b, offset):
        tap = 3 * a + b
        return products[p, offset : offset + half_cols, tap * 128 : tap * 128 + 128]

    for p in range(half_rows):
        fine[2 * p, pl.ds(0, half_cols, stride=2), :] = part(p, 1, 1, 0)
        fine[2 * p, pl.ds(1, half_cols, stride=2), :] = part(p, 1, 2, 0) + part(p, 1, 0, 1)
        fine[2 * p + 1, pl.ds(0, half_cols, stride=2), :] = part(p, 2, 1, 0) + part(p + 1, 0, 1, 0)
        fine[2 * p + 1, pl.ds(1, half_cols, stride=2), :] = (
            part(p, 2, 2, 0) + part(p, 2, 0, 1) + part(p + 1, 0, 2, 0) + part(p + 1, 0, 0, 1)
        )
    for row in range(fine.shape[0]):
        target[row] = (base(row).astype(F32) + fine[row]).astype(BF16)


def raise_rows(field, even_taps, odd_taps, products, flat_up, flat_down, count, first, valid):
    spread_taps(field, even_taps, odd_taps, 2 * count + 1, first)
    pre_down = lower(even_taps, odd_taps, count, flat_down)
    reduced = pre_down * (0.5 + 0.5 * jnp.tanh(0.5 * pre_down))
    row, col = places(count, reduced.shape[1])
    reduced = jnp.where(valid(row, col), reduced, 0.0).astype(BF16)
    raised = lax.dot(reduced, flat_up[...], preferred_element_type=F32)
    products[...] = raised.reshape(count, PAD, 9 * 128)


def fine_row(products, mixed, target, picks):
    half_cols = target.shape[0] // 2
    col = []
    for b in range(3):
        terms = [
            products[q, :, (3 * a + b) * 128 : (3 * a + b) * 128 + 128]
            for a, q in enumerate(picks)
            if q is not None
        ]
        col.append(sum(terms[1:], terms[0]))
    mixed[0], mixed[1] = col[0], col[1] + col[2]
    mixed[2], mixed[3] = col[0] + col[1], col[2]
    target[pl.ds(0, half_cols, stride=2), :] = mixed[0, 0:half_cols] + mixed[1, 1 : half_cols + 1]
    target[pl.ds(1, half_cols, stride=2), :] = mixed[2, 1 : half_cols + 1] + mixed[3, 2 : half_cols + 2]


def right_edge(half_cols):
    has_right = lax.axis_index("ty") < lax.axis_size("ty") - 1
    return lambda row, col: (col <= half_cols) | has_right


def relay_choices(value, in_grad):
    position, segments = lax.axis_index("segment"), lax.axis_size("segment")
    near = jnp.where(position % 2 == 0, value, in_grad)
    return near, jnp.where(position < segments // 2, value, in_grad)


def forward_kernel(blocks, y0, y1, in_grad, flat_up, flat_down, near, far, *scratch):
    field, even_taps, odd_taps, products, mixed, fine = scratch
    rows, wide = blocks.shape[1], blocks.shape[2]
    breadth = wide - 16
    half_rows, half_cols = rows // 2, breadth // 2
    has_below = lax.axis_index("tx") < lax.axis_size("tx") - 1
    before, after = rims(y0, y1)
    field[:, wide:] = jnp.zeros((field.shape[0], field.shape[1] - wide, 128), F32)
    for k in range(3):
        field[k, 0:wide] = before(2 + k)
    for row in range(rows):
        field[row + 3, 0:wide] = blocks[2, row].astype(F32)
    for k in range(2):
        field[rows + 3 + k, 0:wide] = after(5 + k)
    edge = right_edge(half_cols)
    valid = lambda row, col: ((row <= half_rows) | has_below) & edge(row, col)
    raise_rows(field, even_taps, odd_taps, products, flat_up, flat_down, half_rows + 2, LEFT - 3, valid)
    for p in range(half_rows):
        fine_row(products, mixed, fine.at[2 * p], (p, p + 1, p + 1))
        fine_row(products, mixed, fine.at[2 * p + 1], (p + 1, p + 1, p + 2))
    for row in range(rows):
        value = (blocks[2, row, LEFT : LEFT + breadth].astype(F32) + fine[row]).astype(BF16)
        near[row], far[row] = relay_choices(value, in_grad[row])


def inner_kernel(blocks, flat_up, flat_down, value, *scratch):
    field, even_taps, odd_taps, products, mixed, fine = scratch
    rows, wide = blocks.shape[0], blocks.shape[1]
    breadth = wide - 16
    half_rows, half_cols = rows // 2, breadth // 2
    field[:, wide:] = jnp.zeros((field.shape[0], field.shape[1] - wide, 128), F32)
    field[0, 0:wide] = jnp.zeros((wide, 128), F32)
    for row in range(rows):
        field[row + 1, 0:wide] = blocks[row].astype(F32)
    edge = right_edge(half_cols)
    raise_rows(field, even_taps, odd_taps, products, flat_up, flat_down, half_rows, LEFT - 3, edge)
    for p in range(half_rows):
        fine_row(products, mixed, fine.at[2 * p], (p - 1 if p else None, p, p))
        below = p + 1 if p + 1 < half_rows else None
        fine_row(products, mixed, fine.at[2 * p + 1], (p, p, below))
    for row in range(rows):
        value[row] = (blocks[row, LEFT : LEFT + breadth].astype(F32) + fine[row]).astype(BF16)


def condition_inner_kernel(
    owner_in, cell_in, base, z0, z1, coarse, z2, flat_up, flat_down, pay, ext, value, *scratch
):
    table, plane, owner, cell, arrived = scratch[:5]
    copies = copies_in_parts(((owner_in, owner, 1), (cell_in, cell, 1)), arrived)
    for copy in copies:
        copy.start()

    def named():
        for copy in copies:
            copy.wait()

    condition_kernel(True, owner, cell, base, z0, z1, coarse, z2, pay, ext, table, plane, named)
    inner_kernel(ext, flat_up, flat_down, value, *scratch[5:])


def border_kernel(blocks, y0, value, in_grad, flat_up, flat_down, near, strip, *scratch):
    field, even_taps, odd_taps, products, mixed, fine = scratch
    rows, wide = blocks.shape[0], blocks.shape[1]
    breadth = wide - 16
    half_cols = breadth // 2
    upper = lax.axis_index("tx") == 0
    field[:, wide:] = jnp.zeros((field.shape[0], field.shape[1] - wide, 128), F32)

    def far_row(k):
        tiles = [y0[(breadth // 8 + 1) * k + part].astype(F32) for part in range(breadth // 8 + 1)]
        return jnp.concatenate([tiles[-1]] + tiles, axis=0)

    own = lambda row: blocks[row].astype(F32)
    for k in range(7):
        lower_tile = far_row(k) if k < 3 else own(k - 3)
        upper_tile = own(rows - 5 + k) if k < 5 else far_row(k - 5)
        field[k, 0:wide] = jnp.where(upper, upper_tile, lower_tile)
    edge = right_edge(half_cols)
    raise_rows(field, even_taps, odd_taps, products, flat_up, flat_down, 3, LEFT - 3, edge)
    fine_row(products, mixed, fine.at[0], (0, 1, 1))
    fine_row(products, mixed, fine.at[1], (1, 1, 2))
    fine_row(products, mixed, fine.at[2], (1, 2, 2))
    repaired = [None] * 3
    for k in range(3):
        base = jnp.where(upper, own(rows - 3 + k), own(k))[LEFT : LEFT + breadth]
        added = jnp.where(upper, fine[max(k - 1, 0)], fine[k])
        repaired[k] = (base + added).astype(BF16)
        if k == 0:
            repaired[k] = jnp.where(upper, value[rows - 3], repaired[k])
        strip[k] = relay_choices(repaired[k], jnp.where(upper, in_grad[rows - 3 + k], in_grad[k]))[1]
    for row in range(rows):
        result = value[row]
        if row < 3:
            result = jnp.where(upper, result, repaired[row])
        if row >= rows - 3:
            result = jnp.where(upper, repaired[row - (rows - 3)], result)
        near[row] = relay_choices(result, in_grad[row])[0]


def final_kernel(
    scaling, near, far, strip, own, first, second, third, act_out, grad_out, partner_out, up_sum, down_sum, d0, d1
):
    rows, border = near.shape[0], strip.shape[0]
    position, last = lax.axis_index("segment"), lax.axis_size("segment") - 1
    upper = lax.axis_index("tx") == 0
    odd = position % 2 == 1
    for row in range(rows):
        from_upper = far[row] if row < rows - border else strip[row - (rows - border)]
        from_lower = strip[row] if row < border else far[row - border]
        from_far = jnp.where(upper, from_upper, from_lower)
        blank = jnp.zeros_like(from_far)
        partner_out[0, row] = from_far
        act_out[0, row] = jnp.where(position == 0, blank, jnp.where(odd, near[row], from_far))
        grad_out[0, row] = jnp.where(position == last, blank, jnp.where(odd, from_far, near[row]))
    total = own[...] + first[...].astype(F32) + second[...].astype(F32) + third[...].astype(F32)
    piece = up_sum.shape[0]
    up_sum[...] = total[0:piece] * scaling
    tall = d0.shape[0]
    rests = total[piece + tall :] * scaling
    d0[...] = total[piece : piece + tall] * scaling
    d1[0 : tall // 2] = rests
    d1[tall // 2 :] = pltpu.roll(rests, 64, 1)
    flatten_rows(d0, d1, down_sum, 0)


def swaps(axis):
    size = lax.axis_size(axis)
    pairs = [(i, i + 1) for i in range(0, size - 1, 2)]
    other = [(i, i + 1) for i in range(1, size - 1, 2)]
    both = lambda pairs: pairs + [(j, i) for i, j in pairs]
    return both(pairs), both(other)


def crossed(axis, distance):
    return [(i, i ^ distance) for i in range(lax.axis_size(axis))]


def shape(dims, kind):
    return jax.ShapeDtypeStruct(tuple(dims), kind)


def local(
    act_in,
    partner_in,
    stashed,
    grad_in,
    down_weights,
    up_weights,
    coarse,
    nest_owner,
    nest_cell,
    land_weight,
):
    height, breadth, channels = act_in.shape[1:]
    depth = down_weights.shape[-1]
    half_rows = height // 2
    n_tx, n_ty = lax.axis_size("tx"), lax.axis_size("ty")
    position, segments = lax.axis_index("segment"), lax.axis_size("segment")
    scaling = 1.0 / math.sqrt(height * breadth * n_tx * n_ty)
    down_taps = jnp.swapaxes(down_weights, 3, 4).reshape(9, depth, channels)
    up_taps = up_weights.reshape(9, depth, channels)

    owners = nest_owner.reshape(-1)
    tile = shape((height, breadth, channels), BF16)
    pay = shape((height + 1 + coarse.shape[0] // 8, 8, channels), BF16)
    merged = n_ty == 4 and n_tx == 2
    if merged:
        st_far = lax.ppermute(stashed, "tx", crossed("tx", 1))
    side = pltpu.VMEM((height, 16, channels), BF16)
    full = pltpu.VMEM((height, breadth, channels), BF16)
    grad_own, z_pay0, z_pay1 = call(
        edge_kernel,
        (tile, pay, pay),
        [HBM] * 8,
        [side] * 4
        + [full] * 2
        + [pltpu.VMEM((height // 4, breadth, channels), F32), pltpu.VMEM(coarse.shape, BF16)]
        + [pltpu.SMEM(scalars.shape, jnp.int32) for scalars in (owners, nest_cell, land_weight)]
        + [pltpu.SemaphoreType.DMA((16,))],
        flops=1000,
        moved=1000,
    )(*in_hbm(owners, nest_cell, land_weight, act_in, partner_in, stashed, grad_in, coarse))
    pairs, others = swaps("ty")
    if merged:
        others = crossed("ty", 3)
        grad_far = lax.ppermute(grad_own, "tx", crossed("tx", 1))
    z0 = lax.ppermute(z_pay0, "ty", pairs)
    z1 = lax.ppermute(z_pay1, "ty", others)
    if merged:
        table_parts = (coarse, lax.ppermute(coarse, "ty", crossed("ty", 2)))
    else:
        table_parts = (lax.all_gather(coarse, "ty", tiled=True),)
    flat = shape((depth, 9 * channels), BF16)
    taps_room = pltpu.VMEM((9, depth, channels), BF16)
    base, stash, flat_up, flat_down = call(
        prepare_kernel,
        (shape((height, breadth, channels), F32), tile, flat, flat),
        [HBM] * 5,
        [full, full, taps_room, taps_room, pltpu.SemaphoreType.DMA((30,))],
        flops=1000,
        moved=1000,
    )(*in_hbm(act_in, partner_in, stashed, up_taps, down_taps))
    wide = 2 * PAD + 16
    rows_flat = 9 * depth

    def tap_rooms(count):
        room = pltpu.VMEM((count + 1, PAD, 3 * channels), BF16)
        return [pltpu.VMEM((2 * count + 2, wide, channels), F32), room, room]

    fine = pltpu.VMEM((height, breadth, channels), F32)
    products = lambda count: pltpu.VMEM((count, PAD, 9 * channels), F32)
    forward_rooms = lambda count: tap_rooms(count) + [
        products(count),
        pltpu.VMEM((4, PAD, channels), F32),
        fine,
    ]
    operands = (base, z0, z1, *table_parts)
    rooms = [
        pltpu.VMEM((n_ty * coarse.shape[0], channels), F32),
        pltpu.VMEM((height // 4, breadth, channels), F32),
    ]
    pairs, others = swaps("tx")
    if merged:
        rim, pack = call(
            rim_kernel,
            (shape((height, 8, channels), BF16), shape((height // 2 + BORDER, 8, channels), BF16)),
            [VMEM] * 2 + [pl.BlockSpec(memory_space=pl.ANY)] * 2,
            flops=1000,
            moved=1000,
        )(z0, z1, flat_up, st_far)
        rim_far = lax.ppermute(pack, "tx", pairs)
        pay, blocks, value = call(
            condition_inner_kernel,
            (
                shape((3 * (breadth // 8 + 1), 8, channels), BF16),
                shape((height, breadth + 16, channels), BF16),
                tile,
            ),
            [HBM] * 2 + [VMEM] * (len(operands) + 2),
            rooms
            + [pltpu.SMEM(owners.shape, jnp.int32), pltpu.SMEM(nest_cell.shape, jnp.int32)]
            + [pltpu.SemaphoreType.DMA((2,))]
            + forward_rooms(half_rows),
            flops=2_000_000_000,
            moved=1000,
        )(*in_hbm(owners, nest_cell), *operands, flat_up, flat_down)
        ys = [lax.ppermute(pay, "tx", pairs)]
    else:
        pay = shape((STRIP_ROWS, breadth + 16, channels), BF16)
        *pays, blocks = call(
            functools.partial(condition_kernel, False),
            (pay, pay, shape((3, height, breadth + 16, channels), BF16)),
            [SMEM] * 2 + [VMEM] * (len(operands) + 2),
            rooms,
        )(owners, nest_cell, *operands, stash, grad_own)
        ys = [lax.ppermute(pays[0], "tx", pairs), lax.ppermute(pays[1], "tx", others) if others else pays[1]]

    if merged:
        piece = rows_flat // (n_tx * n_ty)
        part = shape((2 * piece, channels), BF16)
        far, in_grad, own_sum, *sends = call(
            paired_kernel,
            (shape((height - BORDER, breadth, channels), BF16), tile, shape((2 * piece, channels), F32), part, part, part),
            [VMEM] * 9,
            [
                pltpu.VMEM((2 * height + 4, wide, channels), F32),
                pltpu.VMEM((height + 1, breadth // 2, 6 * channels), BF16),
                pltpu.VMEM((height, breadth // 2, 9 * channels), BF16),
                pltpu.VMEM((9 * channels // 2, 128), F32),
                pltpu.VMEM((9 * channels // 2, 128), F32),
                pltpu.VMEM((5 * depth, channels), F32),
                pltpu.VMEM((height + 1, breadth // 2, depth), BF16),
                pltpu.VMEM((half_rows + 1, breadth // 2 + 8, 9 * channels), F32),
                fine,
                pltpu.VMEM((half_rows + 1, 8, 9 * channels), F32),
                pltpu.VMEM((half_rows + 1, 8, 9 * channels), F32),
                pltpu.VMEM((2 * height + 4, wide, channels), F32),
            ],
            flops=5_000_000_000,
            moved=4_000_000,
        )(stash, grad_own, st_far, grad_far, rim, rim_far, flat_up, flat_down, value)
    else:
        whole = shape((rows_flat, channels), F32)
        in_grad, up_flat, down_flat = call(
            grads_kernel,
            (tile, whole, whole),
            [VMEM] * 5,
            tap_rooms(half_rows + 1)
            + [
                pltpu.VMEM((half_rows + 1, PAD, 9 * channels), BF16),
                pltpu.VMEM((9 * channels, 128), F32),
                pltpu.VMEM((9 * channels, 128), F32),
                products(half_rows + 1),
                fine,
            ],
            flops=500_000_000,
            moved=4_000_000,
        )(blocks, *ys, flat_up, flat_down)
        pooled = lambda flat: lax.psum_scatter(
            flat.reshape(-1) * scaling, ("tx", "ty"), scatter_dimension=0, tiled=True
        )[None]
        down_sum, up_sum = pooled(down_flat), pooled(up_flat)

    mirror = [(i, segments - 1 - i) for i in range(segments)]
    if merged:
        ys = passed_on(ys, 2_000_000_000)
        near, strip = call(
            border_kernel,
            (tile, shape((BORDER, breadth, channels), BF16)),
            [VMEM] * 6,
            forward_rooms(3),
            flops=600_000_000,
            moved=4_000_000,
        )(blocks, ys[0], value, in_grad, flat_up, flat_down)
        from_far = lax.ppermute(far, "segment", mirror)
        from_strip = lax.ppermute(strip, "segment", mirror)
        from_near = lax.ppermute(near, "segment", crossed("segment", 1))
        arrived = [lax.ppermute(sends[d - 1], "ty", crossed("ty", d)) for d in (2, 1, 3)]
        arrived = passed_on(arrived[:1], 800_000_000) + arrived[1:]
        (from_far,) = passed_on([from_far], 100_000_000, arrived[:1])
        arrived = arrived[:1] + passed_on(arrived[1:], 3_000_000_000, [from_far])
        summed = shape((piece, channels), F32)
        act_out, grad_out, partner_out, up_sum, down_sum = call(
            functools.partial(final_kernel, scaling),
            (shape(act_in.shape, BF16),) * 3 + (summed, summed),
            [VMEM] * 7,
            [pltpu.VMEM((2 * piece // 3, 128), F32)] * 2,
            flops=1_000,
            moved=1000,
        )(from_near, from_far, from_strip, own_sum, *arrived)
        return act_out, grad_out, partner_out, down_sum.reshape(1, -1), up_sum.reshape(1, -1)
    near, far = call(
        forward_kernel,
        (tile, tile),
        [VMEM] * 6,
        forward_rooms(half_rows + 2),
        flops=600_000_000,
        moved=4_000_000,
    )(blocks, *ys, in_grad, flat_up, flat_down)
    from_far = lax.ppermute(far, "segment", mirror)
    from_near = lax.ppermute(near, "segment", crossed("segment", 1))
    blank = jnp.zeros_like(from_near)
    odd = position % 2 == 1
    act_out = jnp.where(position == 0, blank, jnp.where(odd, from_near, from_far))
    grad_out = jnp.where(position == segments - 1, blank, jnp.where(odd, from_far, from_near))
    return (act_out[None], grad_out[None], from_far[None], down_sum, up_sum)


def solution(mesh):
    tile = P("segment", "tx", "ty", None)
    weights = P("segment", None, None, None, None)
    grads = P("segment", ("tx", "ty"))
    rows = P(("tx", "ty"))
    return jax.shard_map(
        local,
        mesh=mesh,
        in_specs=(tile,) * 4 + (weights,) * 2 + (P(("tx", "ty"), None),) * 2 + (rows, P("tx", "ty")),
        out_specs=(tile,) * 3 + (grads,) * 2,
        check_vma=False,
    )
```
